32 devices in a mesh: tower: 2 (over core), dp: 16 (over z, y, x).
Axes of the slice: x: 2, y: 2, z: 4, core: 2. Of those that a mesh axis runs over, the one named last changes fastest.
Arguments:
- text_tokens: bfloat16 [1024, 16, 768], P(('tower', 'dp')), may hold values from -6 to 6
- image_tokens: bfloat16 [1024, 50, 768], P(('tower', 'dp')), may hold values from -6 to 6
- counts: int32 [32], replicated, may hold values from 16 to 32, as said below
- caption_group: int32 [1024], replicated, may hold values from 0 to 7
- image_gains: bfloat16 [2, 768], replicated, may hold values from 0.5 to 1.5
- image_shifts: bfloat16 [2, 768], replicated, may hold values from -1.25 to 1.25
- image_attend: bfloat16 [768, 2304], replicated, may hold values from -0.21875 to 0.21875
- image_attend_bias: bfloat16 [1536], replicated, may hold values from -1.25 to 1.25
- image_output: bfloat16 [768, 768], replicated, may hold values from -1.5 to 1.5
- image_output_bias: bfloat16 [768], replicated, may hold values from -1.25 to 1.25
- image_expand: bfloat16 [768, 3072], replicated, may hold values from -0.21875 to 0.21875
- image_expand_bias: bfloat16 [3072], replicated, may hold values from -1.25 to 1.25
- image_contract: bfloat16 [3072, 768], replicated, may hold values from -0.109375 to 0.109375
- image_contract_bias: bfloat16 [768], replicated, may hold values from -1.25 to 1.25
- text_gains: bfloat16 [2, 768], replicated, may hold values from 0.5 to 1.5
- text_shifts: bfloat16 [2, 768], replicated, may hold values from -1.25 to 1.25
- text_attend: bfloat16 [768, 2304], replicated, may hold values from -0.21875 to 0.21875
- text_attend_bias: bfloat16 [1536], replicated, may hold values from -1.25 to 1.25
- text_output: bfloat16 [768, 768], replicated, may hold values from -0.875 to 0.875
- text_output_bias: bfloat16 [768], replicated, may hold values from -1.25 to 1.25
- text_expand: bfloat16 [768, 3072], replicated, may hold values from -0.21875 to 0.21875
- text_expand_bias: bfloat16 [3072], replicated, may hold values from -1.25 to 1.25
- text_contract: bfloat16 [3072, 768], replicated, may hold values from -0.109375 to 0.109375
- text_contract_bias: bfloat16 [768], replicated, may hold values from -1.25 to 1.25
Outputs:
- loss_value: float32 [], replicated
- text_grad: float32 [1024, 16, 768], P(('tower', 'dp'))
- grad_gains: float32 [2, 768], P(None, 'dp')
- grad_shifts: float32 [2, 768], P(None, 'dp')
- grad_attend: float32 [768, 2304], P('dp')
- grad_attend_bias: float32 [1536], P('dp')
- grad_output: float32 [768, 768], P('dp')
- grad_output_bias: float32 [768], P('dp')
- grad_expand: float32 [768, 3072], P(None, 'dp')
- grad_expand_bias: float32 [3072], P('dp')
- grad_contract: float32 [3072, 768], P('dp')
- grad_contract_bias: float32 [768], P('dp')
The draws below stay inside these ranges and needn't reach their ends.
Inputs may be any that keep to these rules, and one draw needn't show every extreme that they name: Device d, counted along tower then dp, holds pairs d * 32 to (d + 1) * 32 - 1, of which the first counts[d] are live.
All inputs are finite; a program needn't handle non-finite values.
Results may differ from the reference program's by a relative error of at most 0.019.
The reference program's roundings to bfloat16 on the way count: a program that leaves them out, or rounds other values in their place, can miss the bound.
Values may be sent and summed in bfloat16 or wider, within the bound.
A program may use at most 192 MiB of HBM per device.

```python
import jax
import jax.numpy as jnp
from jax import lax

D = 768
HEADS = 12
HEAD_DIM = 64
FF = 3072
IMG_ROWS = 50
TXT_ROWS = 16
CLASSES = 8
EX_DEV = 32
EXAMPLES = 1024
N_TOWER = 2
N_DP = 16


def draw_counts(key, part):
    key = jax.random.fold_in(key, 7)
    first_key, second_key = jax.random.split(key)
    devices_all = N_TOWER * N_DP
    drawn = jax.random.randint(first_key, (devices_all,), EX_DEV // 2, EX_DEV + 1)
    order = jax.random.permutation(second_key, devices_all)
    drawn = drawn.at[order[0]].set(EX_DEV)
    drawn = drawn.at[order[1]].set(EX_DEV // 2)
    return drawn.astype(jnp.int32)


def with_ends(values, key, smallest, high):
    shape = values.shape
    place = [jax.random.randint(jax.random.fold_in(key, axis), (), 0, shape[axis]) for axis in range(len(shape))]
    values = values.at[tuple(place)].set(smallest)
    longest = shape.index(max(shape))
    place[longest] = (place[longest] + 1) % shape[longest]
    return values.at[tuple(place)].set(high)


def shard_levels(stream_key, dims, pieces, low, high):
    level, own = 1.0, jax.random.fold_in(stream_key, 6)
    for axis_at, blocks in pieces:
        heights = jnp.exp(jax.random.uniform(jax.random.fold_in(own, axis_at), (blocks,), jnp.float32, low / len(pieces), high / len(pieces)))
        level = level * jnp.repeat(heights, dims[axis_at] // blocks).reshape([-1 if axis == axis_at else 1 for axis in range(len(dims))])
    return level


def gaussian(stream_key, shape, scale, reach, cuts=(), held_as=jnp.bfloat16):
    array = jax.random.normal(stream_key, shape, jnp.float32) * scale
    if len(cuts) > 0:
        array = shard_levels(stream_key, shape, cuts, -0.22, 0.18) * array
    return jnp.clip(array, min=-reach, max=reach).astype(held_as)


def setup_inputs(seed: int = 0) -> dict:
    arg_keys = jax.random.split(jax.random.key(seed), 25)
    return {
        "text_tokens": gaussian(arg_keys[0], (EXAMPLES, TXT_ROWS, D), 1.0, 6.0, ((0, 32),)),
        "image_tokens": gaussian(arg_keys[1], (EXAMPLES, IMG_ROWS, D), 1.0, 6.0, ((0, 32),)),
        "counts": draw_counts(jax.random.fold_in(arg_keys[24], 71), 0),
        "caption_group": with_ends(jax.random.randint(arg_keys[3], (EXAMPLES,), 0, CLASSES), jax.random.fold_in(arg_keys[3], 1), 0, CLASSES - 1).astype(jnp.int32),
        "image_gains": jnp.clip(1.0 + 0.1 * jax.random.normal(arg_keys[4], (2, D), jnp.float32), 0.5, 1.5).astype(jnp.bfloat16),
        "image_shifts": gaussian(arg_keys[5], (2, D), 0.2, 1.25),
        "image_attend": gaussian(arg_keys[6], (D, 3 * D), D ** -0.5, 0.21875),
        "image_attend_bias": gaussian(arg_keys[7], (2 * D,), 0.2, 1.25),
        "image_output": gaussian(arg_keys[8], (D, D), (D // IMG_ROWS) ** -0.5, 1.5),
        "image_output_bias": gaussian(arg_keys[9], (D,), 0.2, 1.25),
        "image_expand": gaussian(arg_keys[10], (D, FF), D ** -0.5, 0.21875),
        "image_expand_bias": gaussian(arg_keys[11], (FF,), 0.2, 1.25),
        "image_contract": gaussian(arg_keys[12], (FF, D), FF ** -0.5, 0.109375),
        "image_contract_bias": gaussian(arg_keys[13], (D,), 0.2, 1.25),
        "text_gains": jnp.clip(1.0 + 0.1 * jax.random.normal(arg_keys[14], (2, D), jnp.float32), 0.5, 1.5).astype(jnp.bfloat16),
        "text_shifts": gaussian(arg_keys[15], (2, D), 0.2, 1.25),
        "text_attend": gaussian(arg_keys[16], (D, 3 * D), D ** -0.5, 0.21875),
        "text_attend_bias": gaussian(arg_keys[17], (2 * D,), 0.2, 1.25),
        "text_output": gaussian(arg_keys[18], (D, D), (D // TXT_ROWS) ** -0.5, 0.875),
        "text_output_bias": gaussian(arg_keys[19], (D,), 0.2, 1.25),
        "text_expand": gaussian(arg_keys[20], (D, FF), D ** -0.5, 0.21875),
        "text_expand_bias": gaussian(arg_keys[21], (FF,), 0.2, 1.25),
        "text_contract": gaussian(arg_keys[22], (FF, D), FF ** -0.5, 0.109375),
        "text_contract_bias": gaussian(arg_keys[23], (D,), 0.2, 1.25),
    }


@jax.custom_vjp
def low(v):
    return lax.optimization_barrier(v.astype(jnp.bfloat16)).astype(jnp.float32)

@jax.custom_vjp
def low_back(v):
    return v

def low_keep(v):
    return (low(v), None)

def low_pass(kept, grad):
    return (grad,)

def back_keep(v):
    return (v, None)

def back_low(kept, grad):
    return (low(grad),)
low.defvjp(low_keep, low_pass)
low_back.defvjp(back_keep, back_low)
HIGHEST = lax.Precision.HIGHEST
LOGIT_SCALE = 64.0
NORM_EPS = 1e-05
EMBED_EPS = 1e-06

def product(left, right):
    return jnp.dot(left, right, precision=HIGHEST, preferred_element_type=jnp.float32)

def layer_norm(rows_in, gain, shift):
    centre = rows_in - lax.optimization_barrier(jnp.mean(rows_in, -1, keepdims=True))
    variance = lax.optimization_barrier(jnp.mean(centre * centre, -1, keepdims=True))
    return centre * lax.rsqrt(variance + NORM_EPS) * gain + shift

def block(tokens, params):
    gains, shifts, attend, attend_bias, output, output_bias, expand, expand_bias, contract, contract_bias = params
    examples, row_count, features = tokens.shape
    inputs = tokens.reshape(examples * row_count, features)
    normed_one = low(layer_norm(inputs, gains[0], shifts[0]))
    full_bias = jnp.concatenate([attend_bias[:features], jnp.zeros_like(output_bias), attend_bias[features:]])
    projected = low(low_back(product(normed_one, attend) + full_bias))
    projected = projected.reshape(examples, row_count, 3, HEADS, HEAD_DIM)
    queries = projected[:, :, 0]
    keys = projected[:, :, 1]
    values = projected[:, :, 2]
    scores = low_back(jnp.einsum('erhd,eshd->ehrs', queries, keys, precision=HIGHEST) * HEAD_DIM ** (-0.5))
    attention = low(jax.nn.softmax(scores, axis=-1))
    context = low(low_back(jnp.einsum('ehrs,eshd->erhd', attention, values, precision=HIGHEST)))
    context = context.reshape(examples * row_count, features)
    middle = inputs + low_back(product(context, output) + output_bias)
    normed_two = low(layer_norm(middle, gains[1], shifts[1]))
    pre_gelu = low_back(product(normed_two, expand) + expand_bias)
    activated = low(jax.nn.gelu(pre_gelu))
    block_out = middle + low_back(product(activated, contract) + contract_bias)
    pooled = lax.optimization_barrier(jnp.mean(block_out.reshape(examples, row_count, features), axis=1))
    return pooled * lax.rsqrt(lax.optimization_barrier(jnp.sum(pooled * pooled, -1, keepdims=True)) + EMBED_EPS)

def embed(tokens, params):
    group_size = EX_DEV * 8
    grouped = tokens.reshape(-1, group_size, tokens.shape[1], tokens.shape[2])
    step_block = jax.checkpoint(lambda batch_group: block(batch_group, params))
    return lax.map(step_block, grouped).reshape(-1, tokens.shape[2])

def masked_lse(logits, allowed, live_rows):
    filled = jnp.where(allowed, logits, -1e+30)
    largest = lax.optimization_barrier(jnp.max(filled, -1, keepdims=True))
    weights = jnp.exp(filled - largest) * allowed.astype(jnp.float32)
    return largest[:, 0] + jnp.log(lax.optimization_barrier(jnp.sum(weights, -1)) + (1.0 - live_rows))

def contrast(text_embedding, image_low, counts, caption_group):
    text_low = low(text_embedding)
    forward_logits = low_back(product(text_low, image_low.T) * LOGIT_SCALE)
    backward_logits = low_back(product(image_low, text_low.T) * LOGIT_SCALE)
    positions = jnp.arange(EXAMPLES, dtype=jnp.int32)
    live = positions % EX_DEV < jnp.repeat(counts, EX_DEV, total_repeat_length=EXAMPLES)
    distinct = (caption_group[:, None] != caption_group[None, :]) | (positions[:, None] == positions[None, :])
    allowed = live[:, None] & live[None, :] & distinct
    live_rows = live.astype(jnp.float32)
    text_terms = masked_lse(forward_logits, allowed, live_rows) - jnp.diagonal(forward_logits)
    image_terms = masked_lse(backward_logits, allowed, live_rows) - jnp.diagonal(backward_logits)
    return 0.5 * (jnp.sum(live_rows * text_terms) + jnp.sum(live_rows * image_terms))

def reference(text_tokens, image_tokens, counts, caption_group, image_gains, image_shifts, image_attend, image_attend_bias, image_output, image_output_bias, image_expand, image_expand_bias, image_contract, image_contract_bias, text_gains, text_shifts, text_attend, text_attend_bias, text_output, text_output_bias, text_expand, text_expand_bias, text_contract, text_contract_bias):
    image_params = tuple((weight.astype(jnp.float32) for weight in (image_gains, image_shifts, image_attend, image_attend_bias, image_output, image_output_bias, image_expand, image_expand_bias, image_contract, image_contract_bias)))
    text_params = tuple((weight.astype(jnp.float32) for weight in (text_gains, text_shifts, text_attend, text_attend_bias, text_output, text_output_bias, text_expand, text_expand_bias, text_contract, text_contract_bias)))
    image_low = low(embed(image_tokens.astype(jnp.float32), image_params))

    def objective(tokens, params):
        return contrast(embed(tokens, params), image_low, counts, caption_group)
    loss_sum, pullback = jax.vjp(objective, text_tokens.astype(jnp.float32), text_params)
    text_grad, grads = pullback(jnp.ones_like(loss_sum))
    loss_value = loss_sum / jnp.sum(counts).astype(jnp.float32)
    return (loss_value, text_grad, grads[0], grads[1], grads[2], grads[3], grads[4], grads[5], grads[6], grads[7], grads[8], grads[9])
```

```python
import functools
import jax
import jax.numpy as jnp
import numpy as np
from jax import lax
from jax.experimental import pallas as pl
from jax.experimental.pallas import tpu as pltpu
from jax.sharding import PartitionSpec as P

F32, BF16 = jnp.float32, jnp.bfloat16
D, HD, FF = 768, 64, 3072
PAIRS = D // (2 * HD)
KW = 128
NORM_EPS, EMBED_EPS, LOGIT_SCALE = 1e-5, 1e-6, 64.0
NEG = -1e30
ANY = pl.BlockSpec(memory_space=pl.ANY)
VM = pl.BlockSpec(memory_space=pltpu.VMEM)
GELU_C, GELU_A = float(np.sqrt(2 / np.pi)), 0.044715


def dot(a, b):
    return jnp.dot(a, b, preferred_element_type=F32)


def dot_t(a, b):
    return lax.dot_general(a, b, (((1,), (1,)), ((), ())), preferred_element_type=F32)


def t_dot(a, b):
    return lax.dot_general(a, b, (((0,), (0,)), ((), ())), preferred_element_type=F32)


def unit_rows(v):
    centre = v - jnp.mean(v, -1, keepdims=True)
    inv = lax.rsqrt(jnp.mean(centre * centre, -1, keepdims=True) + NORM_EPS)
    return centre * inv, inv


def head_masks():
    lane = lax.broadcasted_iota(jnp.int32, (1, 2 * HD), 1)
    even = (lane < HD).astype(F32)
    return even.astype(BF16), (1.0 - even).astype(BF16)


def pair_mask(rows, per, real):
    r = lax.broadcasted_iota(jnp.int32, (rows, 2 * KW), 0)
    c = lax.broadcasted_iota(jnp.int32, (rows, 2 * KW), 1) % KW
    ok = (r // per == c // per) & (c % per < real) & (c < rows)
    return jnp.where(ok, 0.0, NEG).astype(F32)


def split_heads(a, even, odd):
    return jnp.concatenate([a * even, a * odd], axis=0)


def softmax_half(s):
    m = jnp.max(s, -1, keepdims=True)
    p = jnp.exp(s - m)
    return p / jnp.sum(p, -1, keepdims=True)


def exp_half(s):
    return jnp.exp(s - jnp.max(s, -1, keepdims=True)).astype(BF16)


def block_forward(x, rows, groups, small, W, wait, proj, ctx, mask, att_out, keep):
    attend, output, expand, contract = W
    unit, _ = unit_rows(x)
    n1 = (unit * small[0:1, :] + small[2:3, :]).astype(BF16)
    keep("n1", n1)
    wait("attend")
    M = rows * groups
    step = 256
    for c in range(3 * D // step):
        y = dot(n1, attend[:, c * step:(c + 1) * step])
        if c * step < D:
            y = y + small[4:5, c * step:(c + 1) * step]
        elif c * step >= 2 * D:
            y = y + small[5:6, c * step - 2 * D:(c + 1) * step - 2 * D]
        proj[0:M, c * step:(c + 1) * step] = y.astype(BF16)
    even, odd = head_masks()
    ones = split_heads(jnp.ones((KW, 2 * HD), BF16), even, odd)

    def group(g, _):
        r0 = pl.multiple_of(g * rows, 16)
        for j in range(PAIRS):
            lanes = slice(j * 2 * HD, (j + 1) * 2 * HD)
            q = proj[pl.ds(r0, rows), j * 128:(j + 1) * 128]
            kk = split_heads(proj[pl.ds(r0, KW), D + j * 128:D + (j + 1) * 128], even, odd)
            vv = split_heads(proj[pl.ds(r0, KW), 2 * D + j * 128:2 * D + (j + 1) * 128], even, odd)
            s = dot_t(q, kk) * HD ** -0.5 + mask[...]
            if att_out is None:
                p = jnp.concatenate([exp_half(s[:, :KW]), exp_half(s[:, KW:])], axis=1)
                both = dot(p, jnp.concatenate([vv, ones], axis=1))
                ctx[pl.ds(r0, rows), lanes] = (both[:, :128] / both[:, 128:]).astype(BF16)
            else:
                a = jnp.concatenate([softmax_half(s[:, :KW]), softmax_half(s[:, KW:])], axis=1)
                att_out[g * PAIRS + j] = a
                ctx[pl.ds(r0, rows), lanes] = dot(a.astype(BF16), vv).astype(BF16)
        return 0

    lax.fori_loop(0, groups, group, 0)
    wait("output")
    middle = x + (dot(ctx[...], output[...]) + small[6:7, :])
    keep("middle", middle)
    unit, _ = unit_rows(middle)
    n2 = (unit * small[1:2, :] + small[3:4, :]).astype(BF16)
    keep("n2", n2)
    wait("expand")
    acc = middle + small[11:12, :]
    step = 768
    for c in range(FF // step):
        pre = dot(n2, expand[:, c * step:(c + 1) * step]) + small[7 + c:8 + c, :]
        sq = pre * pre
        th = jnp.tanh(pre * (GELU_C + GELU_C * GELU_A * sq))
        cdf = 0.5 + 0.5 * th
        act = (pre * cdf).astype(BF16)
        keep("act", act, c, pre, sq, th, cdf)
        if c == 0:
            wait("contract")
        acc = acc + dot(act, contract[c * step:(c + 1) * step, :])
    return acc


def embed_rows(pooled):
    inv = lax.rsqrt(jnp.sum(pooled * pooled, -1, keepdims=True) + EMBED_EPS)
    return pooled * inv, inv


def image_kernel(per, real, pairs_step, x_ref, small, attend_h, output_h, expand_h, contract_h, low_ref,
                 attend, output, expand, contract, sems, xs, proj, ctx, mask):
    rows = 2 * per
    ex = 2 * pairs_step
    copies = {}
    for k, (n, h, v) in enumerate((("attend", attend_h, attend), ("output", output_h, output), ("expand", expand_h, expand), ("contract", contract_h, contract))):
        copies[n] = pltpu.make_async_copy(h, v, sems.at[k])
        copies[n].start()
    M = rows * pairs_step
    xs[...] = jnp.zeros_like(xs)
    proj[M:, :] = jnp.zeros((proj.shape[0] - M, 3 * D), BF16)
    mask[...] = pair_mask(rows, per, real)

    def chunk(i, _):
        def wait(n):
            @pl.when(i == 0)
            def _():
                copies[n].wait()
        for e in range(ex):
            xs[e * per:e * per + real, :] = x_ref[i * ex + e].astype(F32)
        out = block_forward(xs[...], rows, pairs_step, small, (attend, output, expand, contract), wait, proj, ctx, mask, None, lambda *a: None)
        out = out.reshape(ex, per, D)
        ok = lax.broadcasted_iota(jnp.int32, (ex, per, D), 1) < real
        pooled = jnp.sum(jnp.where(ok, out, 0.0), 1) * (1.0 / real)
        emb, _ = embed_rows(pooled)
        low_ref[i] = emb.astype(BF16)
        return 0

    lax.fori_loop(0, x_ref.shape[0] // ex, chunk, 0)


def image_forward(tokens, small, attend, output, expand, contract, pairs_step=8):
    n, real, _ = tokens.shape
    per = -(-real // 8) * 8
    rows = 2 * per
    ex = 2 * pairs_step
    M = rows * pairs_step
    low = pl.pallas_call(
        functools.partial(image_kernel, per, real, pairs_step),
        out_shape=jax.ShapeDtypeStruct((n // ex, ex, D), BF16),
        in_specs=[VM, VM, ANY, ANY, ANY, ANY], out_specs=VM,
        scratch_shapes=[pltpu.VMEM((D, 3 * D), BF16), pltpu.VMEM((D, D), BF16), pltpu.VMEM((D, FF), BF16), pltpu.VMEM((FF, D), BF16),
                        pltpu.SemaphoreType.DMA((4,)), pltpu.VMEM((M, D), F32), pltpu.VMEM((M + 16, 3 * D), BF16), pltpu.VMEM((M, D), BF16), pltpu.VMEM((rows, 2 * KW), F32)],
        compiler_params=pltpu.CompilerParams(vmem_limit_bytes=56 << 20),
        name="image_forward",
    )(tokens, small, attend, output, expand, contract)
    return low.reshape(n, D)


def text_kernel(per, n_dp, x_ref, small, attend_h, output_h, expand_h, contract_h,
                low_ref, emb_ref, inv_ref, asum_ref, n1_ref, proj_ref, att_ref, ctx_ref, mid_ref, n2_ref, gp_ref,
                attend, output, expand, contract, sems, mask):
    copies = {}
    for k, (n, h, v) in enumerate((("attend", attend_h, attend), ("output", output_h, output), ("expand", expand_h, expand), ("contract", contract_h, contract))):
        copies[n] = pltpu.make_async_copy(h, v, sems.at[k])
        copies[n].start()
    rows = KW
    M = x_ref.shape[0]
    ex = M // per
    mask[...] = pair_mask(rows, per, per)
    shard = FF // n_dp
    wide = asum_ref.shape[1] // n_dp
    for k in range(n_dp):
        asum_ref[:, k * wide + shard:(k + 1) * wide] = jnp.full((ex, wide - shard), per, BF16)

    def keep(name, value, *extra):
        if name == "n1":
            n1_ref[...] = value
        elif name == "middle":
            mid_ref[...] = value
        elif name == "n2":
            n2_ref[...] = value
        else:
            c, pre, sq, th, cdf = extra
            w = value.shape[1]
            total = jnp.sum(value.astype(F32).reshape(ex, per, w), 1).astype(BF16)
            for k in range(c * w // shard, (c + 1) * w // shard):
                asum_ref[:, k * wide:k * wide + shard] = total[:, k * shard - c * w:(k + 1) * shard - c * w]
            gp_ref[:, c * w:(c + 1) * w] = (cdf + (0.5 * GELU_C) * pre * (1.0 - th * th) * (1.0 + (3 * GELU_A) * sq)).astype(BF16)

    out = block_forward(x_ref[...].astype(F32), rows, M // rows, small, (attend, output, expand, contract), lambda n: copies[n].wait(), proj_ref, ctx_ref, mask, att_ref, keep)
    pooled = jnp.sum(out.reshape(ex, per, D), 1) * (1.0 / per)
    emb, inv = embed_rows(pooled)
    low_ref[...] = emb.astype(BF16)
    emb_ref[...] = emb
    inv_ref[...] = jnp.broadcast_to(inv, inv_ref.shape)


def wide_of(n_dp):
    return -(-(FF // n_dp + 1) // 128) * 128


def text_forward(tokens, small, attend, output, expand, contract, n_dp):
    n, per, _ = tokens.shape
    M = n * per
    S = jax.ShapeDtypeStruct
    outs = [S((n, D), BF16), S((n, D), F32), S((n, 128), F32), S((n, n_dp * wide_of(n_dp)), BF16), S((M, D), BF16), S((M, 3 * D), BF16),
            S((M // KW * PAIRS, KW, 2 * KW), F32), S((M, D), BF16), S((M, D), F32), S((M, D), BF16), S((M, FF), BF16)]
    return pl.pallas_call(
        functools.partial(text_kernel, per, n_dp), out_shape=outs,
        in_specs=[VM, VM, ANY, ANY, ANY, ANY], out_specs=[VM] * len(outs),
        scratch_shapes=[pltpu.VMEM((D, 3 * D), BF16), pltpu.VMEM((D, D), BF16), pltpu.VMEM((D, FF), BF16), pltpu.VMEM((FF, D), BF16),
                        pltpu.SemaphoreType.DMA((4,)), pltpu.VMEM((KW, 2 * KW), F32)],
        compiler_params=pltpu.CompilerParams(vmem_limit_bytes=60 << 20),
        name="text_forward",
    )(tokens.reshape(M, D), small, attend, output, expand, contract)


def pack_small(gains, shifts, attend_bias, output_bias, expand_bias, contract_bias):
    parts = [gains, shifts, attend_bias.reshape(2, D), output_bias.reshape(1, D), expand_bias.reshape(FF // D, D), contract_bias.reshape(1, D)]
    return jnp.concatenate([p.astype(F32) for p in parts], 0)


MESH_ID = pl.DeviceIdType.MESH


def place():
    return lax.axis_index("tower"), lax.axis_index("dp")


def enter(n):
    t, d = place()
    barrier = pltpu.get_barrier_semaphore()

    def greet(k, _):
        who = (lax.rem(t + k // n, 2), lax.rem(d + lax.rem(k, n), n))
        pl.semaphore_signal(barrier, inc=1, device_id=who, device_id_type=MESH_ID)
        return 0

    lax.fori_loop(1, 2 * n, greet, 0)
    pl.semaphore_wait(barrier, 2 * n - 1)


def spread(n, src, dst, send, recv):
    t, d = place()

    def one(k, _):
        pltpu.make_async_remote_copy(src_ref=src, dst_ref=dst.at[d], send_sem=send, recv_sem=recv,
                                     device_id=(t, lax.rem(d + k, n)), device_id_type=MESH_ID).start()
        return 0

    lax.fori_loop(1, n, one, 0)


def settle(n, dst, send, recv):
    part = dst.at[pl.ds(0, n - 1)]
    pltpu.make_async_copy(part, part, send).wait()
    pltpu.make_async_copy(part, part, recv).wait()


def contrast_rows(fl, allowed, live_rows):
    filled = jnp.where(allowed, fl, NEG)
    largest = jnp.max(filled, -1, keepdims=True)
    weights = jnp.where(allowed, jnp.exp(filled - largest), 0.0)
    total = jnp.sum(weights, -1, keepdims=True) + (1.0 - live_rows)
    return weights / total, largest + jnp.log(total)


def loss_kernel(n, low_ref, asum_ref, meta_ref, emb_ref, inv_ref,
                g_ref, grow_ref, loss_ref, ag_ref, lows, own_rows, sems):
    t, d = place()
    ex = low_ref.shape[1]
    wide = ag_ref.shape[2]
    enter(n)
    spread(n, low_ref, lows.at[t], sems.at[0], sems.at[1])

    def one(k, _):
        to = lax.rem(d + k, n)
        pltpu.make_async_remote_copy(src_ref=asum_ref.at[to], dst_ref=ag_ref.at[d], send_sem=sems.at[2], recv_sem=sems.at[3],
                                     device_id=(t, to), device_id_type=MESH_ID).start()
        return 0

    lax.fori_loop(1, n, one, 0)
    lows[t, d] = low_ref[...]
    ag_ref[d] = asum_ref[d]
    settle(n, lows.at[t], sems.at[0], sems.at[1])
    over = pltpu.make_async_remote_copy(src_ref=lows.at[t], dst_ref=lows.at[t], send_sem=sems.at[4], recv_sem=sems.at[5],
                                        device_id=(1 - t, d), device_id_type=MESH_ID)
    over.start()
    over.wait()
    settle(n, ag_ref, sems.at[2], sems.at[3])

    every = 2 * n * ex
    both = lows[...].reshape(2 * n, 2, ex, D)
    texts, images = both[:, 0].reshape(every, D), both[:, 1].reshape(every, D)
    rank = t * n + d
    row_group, row_live = meta_ref[0:1, :], meta_ref[1:2, :]
    position = lax.broadcasted_iota(jnp.int32, (ex, every), 1)
    diagonal = (position == lax.broadcasted_iota(jnp.int32, (ex, every), 0) + rank * ex).astype(F32)
    columns = jnp.transpose(jnp.broadcast_to(meta_ref[0:1, :], (128, every)))[:, 0:1], jnp.transpose(jnp.broadcast_to(meta_ref[1:2, :], (128, every)))[:, 0:1]
    logits = dot_t(texts, images) * LOGIT_SCALE
    same = lax.broadcasted_iota(jnp.int32, (every, every), 0) == lax.broadcasted_iota(jnp.int32, (every, every), 1)
    allowed = (columns[1] * row_live > 0.0) & ((columns[0] != row_group) | same)
    filled = jnp.where(allowed, logits, NEG)
    largest = jnp.max(filled, 0, keepdims=True)
    total = jnp.sum(jnp.where(allowed, jnp.exp(filled - largest), 0.0), 0, keepdims=True) + (1.0 - row_live)
    image_lse = largest + jnp.log(total)
    own_rows[...] = dot_t(low_ref[0], images) * LOGIT_SCALE
    fl = own_rows[...]
    live_own = jnp.sum(diagonal * row_live, -1, keepdims=True)
    group_own = jnp.sum(diagonal * row_group, -1, keepdims=True)
    allowed = (live_own * row_live > 0.0) & ((group_own != row_group) | (diagonal > 0.0))
    probs, text_lse = contrast_rows(fl, allowed, live_own)
    own_diag = fl * diagonal
    terms = live_own * (text_lse - jnp.sum(own_diag, -1, keepdims=True))
    terms2 = jnp.sum(diagonal * (live_own * image_lse) - live_own * own_diag, -1, keepdims=True)
    loss_ref[...] = jnp.broadcast_to(0.5 * jnp.sum(terms + terms2, 0, keepdims=True), loss_ref.shape)
    forward_coef = (0.5 * live_own * (probs - diagonal)).astype(BF16)
    shifted = jnp.where(allowed, jnp.exp(jnp.where(allowed, fl - image_lse, NEG)), 0.0)
    column_coef = (0.5 * row_live * (shifted - diagonal)).astype(BF16)
    grad = LOGIT_SCALE * dot(forward_coef, images) + LOGIT_SCALE * dot(column_coef, images)
    emb = emb_ref[...]
    pooled = inv_ref[:, 0:1] * (grad - emb * jnp.sum(grad * emb, -1, keepdims=True))
    rows = pooled * meta_ref[2:3, 0:1]
    grow_ref[...] = rows
    g_ref[...] = rows.astype(BF16)


def exchange_and_loss(n, lows, asum, meta, emb, inv):
    _, ex, _ = lows.shape
    wide = asum.shape[1] // n
    S = jax.ShapeDtypeStruct
    return pl.pallas_call(
        functools.partial(loss_kernel, n),
        out_shape=[S((ex, D), BF16), S((ex, D), F32), S((8, 128), F32), S((n, ex, wide), BF16)],
        in_specs=[VM] * 5, out_specs=[VM] * 4,
        scratch_shapes=[pltpu.VMEM((2, n, 2, ex, D), BF16), pltpu.VMEM((ex, 2 * n * ex), F32), pltpu.SemaphoreType.DMA((6,))],
        compiler_params=pltpu.CompilerParams(collective_id=0, has_side_effects=True, vmem_limit_bytes=56 << 20),
        name="gather_and_loss",
    )(lows, asum.reshape(ex, n, wide).transpose(1, 0, 2), meta, emb, inv)


def order_position(s, order):
    p = 0
    for b in order:
        p = 2 * p + ((s >> b) & 1)
    return p


def orders(n):
    bits = list(range(n.bit_length() - 1))
    return bits, bits[1::-1] + bits[2:]


def norm_back(grad, unit, inv, gain):
    gu = grad * gain
    out = inv * (gu - jnp.mean(gu, -1, keepdims=True) - unit * jnp.mean(gu * unit, -1, keepdims=True))
    return out, jnp.sum(grad * unit, 0, keepdims=True), jnp.sum(grad, 0, keepdims=True)


def back_kernel(per, n, x_ref, small, g_ref, grow_ref, n1_ref, proj_ref, att_ref, ctx_ref, mid_ref, n2_ref, gp_ref,
                contract_h, expand_h, output_h, attend_h,
                tg_ref, ex_ref, ey_ref, px_ref, py_ref,
                contract, expand, output, attend, sems, gpre, gctx, gproj, rowsums):
    copies = {}
    for k, (name, h, v) in enumerate((("contract", contract_h, contract), ("expand", expand_h, expand), ("output", output_h, output), ("attend", attend_h, attend))):
        copies[name] = pltpu.make_async_copy(h, v, sems.at[k])
        copies[name].start()
    M = x_ref.shape[0]
    ex = M // per
    order_x, order_y = orders(n)
    rows_e, rows_a = FF // n, D // n
    half_e = rows_e // 2
    H = D // 2
    g_low = g_ref[...]
    step = D
    per_step = step // rows_e
    gn2 = None
    for c in range(FF // step):
        if c == 0:
            copies["contract"].wait()
        cols = slice(c * step, (c + 1) * step)
        ga = dot_t(g_low, contract[cols, :])
        pre = (ga[:, None, :] * gp_ref[:, cols].astype(F32).reshape(ex, per, step)).reshape(M, step).astype(BF16)
        gpre[:, cols] = pre
        rowsums[8 + c:9 + c, :] = jnp.sum(pre.astype(F32), 0, keepdims=True)
        ge = t_dot(pre, n2_ref[...]).astype(BF16)
        for k in range(per_step):
            s = c * per_step + k
            for h in range(2):
                for o, ref, a in ((order_x, ex_ref, 0), (order_y, ey_ref, half_e)):
                    p = order_position(s, o) * half_e
                    ref[h, p:p + half_e, :] = ge[k * rows_e + a:k * rows_e + a + half_e, h * H:(h + 1) * H]
        if c == 0:
            copies["expand"].wait()
        part = dot_t(pre, expand[:, cols])
        gn2 = part if gn2 is None else gn2 + part
    unit, inv = unit_rows(mid_ref[...])
    gm, gain_two, shift_two = norm_back(gn2, unit, inv, small[1:2, :])
    rowsums[1:2, :] = gain_two
    rowsums[3:4, :] = shift_two
    gm = (gm.reshape(ex, per, D) + grow_ref[...][:, None, :]).reshape(M, D)
    tg_ref[...] = gm
    gb = gm.astype(BF16)
    rowsums[12:13, :] = jnp.sum(gb.astype(F32), 0, keepdims=True)

    def put(ref, o, value, lane):
        for s in range(n):
            p = order_position(s, o) * rows_a
            for h in range(2):
                ref[h, p:p + rows_a, lane:lane + H] = value[s * rows_a:(s + 1) * rows_a, h * H:(h + 1) * H]

    put(py_ref, order_y, t_dot(ctx_ref[...], gb).astype(BF16), 0)
    copies["output"].wait()
    gctx[...] = dot_t(gb, output[...]).astype(BF16)
    even, odd = head_masks()
    lane = lax.broadcasted_iota(jnp.int32, (KW, 2 * HD), 1)

    def group(i, _):
        r0 = pl.multiple_of(i * KW, KW)
        for j in range(PAIRS):
            L = slice(j * 128, (j + 1) * 128)
            gc = gctx[pl.ds(r0, KW), L]
            q = proj_ref[pl.ds(r0, KW), j * 128:(j + 1) * 128]
            kk = split_heads(proj_ref[pl.ds(r0, KW), D + j * 128:D + (j + 1) * 128], even, odd)
            vv = split_heads(proj_ref[pl.ds(r0, KW), 2 * D + j * 128:2 * D + (j + 1) * 128], even, odd)
            a = att_ref[i * PAIRS + j]
            gatt = dot_t(gc, vv)
            prod = gatt * a
            gs = jnp.concatenate([a[:, h * KW:(h + 1) * KW] * (gatt[:, h * KW:(h + 1) * KW] - jnp.sum(prod[:, h * KW:(h + 1) * KW], -1, keepdims=True)) for h in range(2)], axis=1).astype(BF16)
            gv = t_dot(a.astype(BF16), gc)
            gk = t_dot(gs, q) * HD ** -0.5
            gproj[pl.ds(r0, KW), j * 128:(j + 1) * 128] = (dot(gs, kk) * HD ** -0.5).astype(BF16)
            gproj[pl.ds(r0, KW), D + j * 128:D + (j + 1) * 128] = jnp.where(lane < HD, gk[:KW], gk[KW:]).astype(BF16)
            gproj[pl.ds(r0, KW), 2 * D + j * 128:2 * D + (j + 1) * 128] = jnp.where(lane < HD, gv[:KW], gv[KW:]).astype(BF16)
        return 0

    lax.fori_loop(0, M // KW, group, 0)
    for part, (ref, o, at) in enumerate(((px_ref, order_x, 0), (px_ref, order_x, H), (py_ref, order_y, H))):
        put(ref, o, t_dot(n1_ref[...], gproj[:, part * D:(part + 1) * D]).astype(BF16), at)
    rowsums[4:5, :] = jnp.sum(gproj[:, 0:D].astype(F32), 0, keepdims=True)
    rowsums[5:6, :] = rowsums[4:5, :]
    rowsums[6:7, :] = jnp.sum(gproj[:, 2 * D:3 * D].astype(F32), 0, keepdims=True)
    rowsums[7:8, :] = rowsums[6:7, :]
    copies["attend"].wait()
    gn1 = dot_t(gproj[...], attend[...])
    unit, inv = unit_rows(x_ref[...].astype(F32))
    gx, gain_one, shift_one = norm_back(gn1, unit, inv, small[0:1, :])
    tg_ref[...] += gx
    rowsums[0:1, :] = gain_one
    rowsums[2:3, :] = shift_one
    sums = rowsums[...]
    parts = [sums[0:8, :]] + [jnp.broadcast_to(sums[8 + r:9 + r, :], (4, D)) for r in range(4)] + [sums[12:13, :], jnp.zeros((128 - 25, D), F32)]
    cols = jnp.transpose(jnp.concatenate(parts, 0))
    at = lax.broadcasted_iota(jnp.int32, (rows_a, 128), 1)
    for s in range(n):
        piece = jnp.where((at < 4) | (at == 24), cols[s * rows_a:(s + 1) * rows_a, :], 0.0)
        r0, first = 2 * s * rows_a % D, 2 * s * rows_a // D * 2
        for c in range(2):
            piece = jnp.where(at == 4 + first + c, cols[r0 + c * rows_a:r0 + (c + 1) * rows_a, :], piece)
        r0, first = 4 * s * rows_a % D, 4 * s * rows_a // D * 4
        for c in range(4):
            piece = jnp.where(at == 8 + first + c, cols[r0 + c * rows_a:r0 + (c + 1) * rows_a, :], piece)
        p = order_position(s, order_x) * rows_a
        px_ref[0, p:p + rows_a, D:] = piece.astype(BF16)
        px_ref[1, p:p + rows_a, D:] = jnp.zeros((rows_a, 128), BF16)


def text_backward(per, n, x, small, g, grow, saved, attend, output, expand, contract):
    n1, proj, att, ctx, mid, n2, gp = saved
    M = x.shape[0]
    S = jax.ShapeDtypeStruct
    outs = [S((M, D), F32), S((2, FF // 2, D // 2), BF16), S((2, FF // 2, D // 2), BF16), S((2, D, D + 128), BF16), S((2, D, D), BF16)]
    return pl.pallas_call(
        functools.partial(back_kernel, per, n), out_shape=outs,
        in_specs=[VM] * 11 + [ANY] * 4, out_specs=[VM] * 5,
        scratch_shapes=[pltpu.VMEM((FF, D), BF16), pltpu.VMEM((D, FF), BF16), pltpu.VMEM((D, D), BF16), pltpu.VMEM((D, 3 * D), BF16), pltpu.SemaphoreType.DMA((4,)),
                        pltpu.VMEM((M, FF), BF16), pltpu.VMEM((M, D), BF16), pltpu.VMEM((M, 3 * D), BF16), pltpu.VMEM((16, D), F32)],
        compiler_params=pltpu.CompilerParams(vmem_limit_bytes=62 << 20),
        name="text_backward",
    )(x, small, g, grow, n1, proj, att, ctx, mid, n2, gp, contract, expand, output, attend)


def reduce_kernel(n, g_ref, ag_ref, loss_ref, ex_ref, ey_ref, px_ref, py_ref,
                  oe_ref, oa_ref, oo_ref, os_ref, oc_ref, ol_ref,
                  gall, pc, pc_in, lossall, fin_e, fin_px, fin_py, *scr):
    t, d = place()
    ex = g_ref.shape[0]
    units = (ex_ref, ey_ref, px_ref, py_ref)
    recvs, (core_send, core_recv, send, recv, gsem, lsem, fsend, frecv) = scr[:-8], scr[-8:]
    order_x, order_y = orders(n)
    nb = len(order_x)
    stage_orders = (order_x, order_y, order_x, order_y)
    enter(n)
    other = (1 - t, d)
    first = []
    for u, ref in enumerate(units):
        c = pltpu.make_async_remote_copy(src_ref=ref.at[1 - t], dst_ref=recvs[u].at[pl.ds(0, ref.shape[1])], send_sem=core_send.at[u], recv_sem=core_recv.at[u], device_id=other, device_id_type=MESH_ID)
        c.start()
        first.append(c)
    accs = [scr_acc for scr_acc in recvs[4:8]]
    for u, ref in enumerate(units):
        first[u].wait()
        accs[u][...] = (ref[t].astype(F32) + recvs[u][0:ref.shape[1], :].astype(F32)).astype(BF16)
    spread(n, g_ref, gall, gsem.at[0], gsem.at[1])
    gall[d] = g_ref[...]

    def tell(k, _):
        who = (lax.rem(t + k // n, 2), lax.rem(d + lax.rem(k, n), n))
        pltpu.make_async_remote_copy(src_ref=loss_ref, dst_ref=lossall.at[t * n + d], send_sem=lsem.at[0], recv_sem=lsem.at[1], device_id=who, device_id_type=MESH_ID).start()
        return 0

    lax.fori_loop(1, 2 * n, tell, 0)
    lossall[t * n + d] = loss_ref[...]
    offs = [0] * 4
    sizes = [r.shape[1] for r in units]
    bases = [r.shape[1] for r in units]
    fins = (fin_e.at[0], fin_e.at[1], fin_px, fin_py)
    for st in range(nb):
        going = []
        for u in range(4):
            b = stage_orders[u][st]
            half = sizes[u] // 2
            mine = lax.rem(d // (1 << b), 2)
            step = 1 << b
            to = d + step * (1 - 2 * mine)
            keep = pl.multiple_of(offs[u] + mine * half, 16)
            away = pl.multiple_of(offs[u] + (1 - mine) * half, 16)
            c = pltpu.make_async_remote_copy(src_ref=accs[u].at[pl.ds(away, half)], dst_ref=recvs[u].at[pl.ds(bases[u], half)],
                                             send_sem=send.at[u, st], recv_sem=recv.at[u, st], device_id=(t, to), device_id_type=MESH_ID)
            c.start()
            going.append((c, keep, half, bases[u]))
            offs[u], sizes[u], bases[u] = keep, half, bases[u] + half
        for u, (c, keep, half, base) in enumerate(going):
            c.wait()
            total = accs[u][pl.ds(keep, half), :].astype(F32) + recvs[u][base:base + half, :].astype(F32)
            if st < nb - 1:
                accs[u][pl.ds(keep, half), :] = total.astype(BF16)
            else:
                fins[u][t] = total.astype(BF16)
    settle(n, gall, gsem.at[0], gsem.at[1])
    part = lossall.at[pl.ds(0, 2 * n - 1)]
    pltpu.make_async_copy(part, part, lsem.at[0]).wait()
    pltpu.make_async_copy(part, part, lsem.at[1]).wait()
    wide = ag_ref.shape[2]
    pc[...] = t_dot(ag_ref[...].reshape(n * ex, wide), gall[...].reshape(n * ex, D)).astype(BF16)
    last = []
    for k, (src, dst) in enumerate([(f.at[t], f.at[t]) for f in fins] + [(pc, pc_in)]):
        c = pltpu.make_async_remote_copy(src_ref=src, dst_ref=dst, send_sem=fsend.at[k], recv_sem=frecv.at[k], device_id=other, device_id_type=MESH_ID)
        c.start()
        last.append(c)
    ol_ref[...] = jnp.sum(lossall[...], 0)
    for c in last:
        c.wait()
    H = D // 2
    rows_e = oe_ref.shape[0] // 2
    for h in range(2):
        oe_ref[0:rows_e, h * H:(h + 1) * H] = fin_e[0, h].astype(F32)
        oe_ref[rows_e:, h * H:(h + 1) * H] = fin_e[1, h].astype(F32)
        for part in range(2):
            oa_ref[:, part * D + h * H:part * D + (h + 1) * H] = fin_px[h, :, part * H:(part + 1) * H].astype(F32)
        oa_ref[:, 2 * D + h * H:2 * D + (h + 1) * H] = fin_py[h, :, H:].astype(F32)
        oo_ref[:, h * H:(h + 1) * H] = fin_py[h, :, :H].astype(F32)
    os_ref[...] = fin_px[0, :, D:].astype(F32)
    oc_ref[...] = pc[...].astype(F32) + pc_in[...].astype(F32)


def reduce_all(n, g, ag, loss, ge_x, ge_y, gp_x, gp_y):
    S = jax.ShapeDtypeStruct
    ex, wide = g.shape[0], ag.shape[2]
    rows_e, rows_a = FF // n, D // n
    units = (ge_x, ge_y, gp_x, gp_y)
    outs = [S((rows_e, D), F32), S((rows_a, 3 * D), F32), S((rows_a, D), F32), S((rows_a, 128), F32), S((wide, D), F32), S((8, 128), F32)]
    nb = n.bit_length() - 1
    scratch = [pltpu.VMEM((n, ex, D), BF16), pltpu.VMEM((wide, D), BF16), pltpu.VMEM((wide, D), BF16), pltpu.VMEM((2 * n, 8, 128), F32),
               pltpu.VMEM((2, 2, rows_e // 2, D // 2), BF16), pltpu.VMEM((2, rows_a, D + 128), BF16), pltpu.VMEM((2, rows_a, D), BF16)]
    scratch += [pltpu.VMEM((2 * u.shape[1], u.shape[2]), BF16) for u in units]
    scratch += [pltpu.VMEM((u.shape[1], u.shape[2]), BF16) for u in units]
    dma = pltpu.SemaphoreType.DMA
    scratch += [dma((4,)), dma((4,)), dma((4, nb)), dma((4, nb)), dma((2,)), dma((2,)), dma((5,)), dma((5,))]
    return pl.pallas_call(
        functools.partial(reduce_kernel, n), out_shape=outs, in_specs=[VM] * 7, out_specs=[VM] * 6, scratch_shapes=scratch,
        compiler_params=pltpu.CompilerParams(collective_id=1, has_side_effects=True, vmem_limit_bytes=56 << 20),
        name="reduce_gradients",
    )(g, ag, loss, *units)


def on_device(n, text_tokens, image_tokens, counts, caption_group, *weights):
    (image_gains, image_shifts, image_attend, image_attend_bias, image_output, image_output_bias, image_expand, image_expand_bias, image_contract, image_contract_bias,
     text_gains, text_shifts, text_attend, text_attend_bias, text_output, text_output_bias, text_expand, text_expand_bias, text_contract, text_contract_bias) = weights
    ex, per, _ = text_tokens.shape
    image_small = pack_small(image_gains, image_shifts, image_attend_bias, image_output_bias, image_expand_bias, image_contract_bias)
    text_small = pack_small(text_gains, text_shifts, text_attend_bias, text_output_bias, text_expand_bias, text_contract_bias)
    every = caption_group.shape[0]
    live = (jnp.arange(ex, dtype=jnp.int32)[None, :] < counts[:, None]).reshape(1, every).astype(F32)
    meta = jnp.concatenate([caption_group.astype(F32)[None, :], live, jnp.full((6, every), 1.0 / per, F32)], 0)
    low, emb, inv, asum, *saved = text_forward(text_tokens, text_small, text_attend, text_output, text_expand, text_contract, n)
    image_low = image_forward(image_tokens, image_small, image_attend, image_output, image_expand, image_contract)
    g, grow, loss, ag = exchange_and_loss(n, jnp.stack([low, image_low]), asum, meta, emb, inv)
    text_grad, *units = text_backward(per, n, text_tokens.reshape(ex * per, D), text_small, g, grow, saved, text_attend, text_output, text_expand, text_contract)
    oe, oa, oo, os, oc, ol = reduce_all(n, g, ag, loss, *units)
    d = lax.axis_index("dp")
    rows_e, rows_a = FF // n, D // n
    loss_value = ol[0, 0] / jnp.sum(counts).astype(F32)
    low_bias, high_bias = os[:, 4:6] + os[:, 6:8], os[:, 8:12] + os[:, 12:16] + os[:, 16:20] + os[:, 20:24]
    return (loss_value, text_grad.reshape(ex, per, D), os[:, 0:2].T, os[:, 2:4].T, oa, low_bias.T.reshape(2 * rows_a), oo, os[:, 24],
            oe.T, high_bias.T.reshape(4 * rows_a), oc[:rows_e], lax.dynamic_slice(oc[rows_e], (d * rows_a,), (rows_a,)))


HEADS = 12
HEAD_DIM = 64


def multiply(left, right):
    return jnp.dot(left, right, preferred_element_type=jnp.float32)


def left_inner(left, right):
    return lax.dot_general(
        left, right, (((0,), (0,)), ((), ())), preferred_element_type=jnp.float32
    )


def right_inner(left, right):
    return lax.dot_general(
        left, right, (((1,), (1,)), ((), ())), preferred_element_type=jnp.float32
    )


def normalize(rows_in, gain, shift):
    centre = rows_in - jnp.mean(rows_in, -1, keepdims=True)
    inverse_std = lax.rsqrt(jnp.mean(centre * centre, -1, keepdims=True) + NORM_EPS)
    unit_rows = centre * inverse_std
    return (unit_rows * gain + shift, unit_rows, inverse_std)


def normalize_back(grad_rows, unit_rows, inverse_std, gain):
    grad_unit = grad_rows * gain
    grad_in = inverse_std * (
        grad_unit
        - jnp.mean(grad_unit, -1, keepdims=True)
        - unit_rows * jnp.mean(grad_unit * unit_rows, -1, keepdims=True)
    )
    return (grad_in, jnp.sum(grad_rows * unit_rows, 0), jnp.sum(grad_rows, 0))


def plain_forward(tokens, params):
    (
        gains,
        shifts,
        attend,
        attend_bias,
        output,
        output_bias,
        expand,
        expand_bias,
        contract,
        contract_bias,
    ) = params
    examples, row_count, features = tokens.shape
    inputs = tokens.astype(jnp.float32).reshape(examples * row_count, features)
    normed, unit_one, inverse_one = normalize(
        inputs, gains[0].astype(jnp.float32), shifts[0].astype(jnp.float32)
    )
    normed_one = normed.astype(jnp.bfloat16)
    full_bias = jnp.concatenate(
        [attend_bias[:features], jnp.zeros_like(output_bias), attend_bias[features:]]
    ).astype(jnp.float32)
    projected = (multiply(normed_one, attend) + full_bias).astype(jnp.bfloat16)
    projected = projected.reshape(examples, row_count, 3, HEADS, HEAD_DIM)
    queries = projected[:, :, 0]
    keys = projected[:, :, 1]
    values = projected[:, :, 2]
    scores = jnp.einsum(
        "erhd,eshd->ehrs", queries, keys, preferred_element_type=jnp.float32
    ) * HEAD_DIM ** (-0.5)
    attention = jax.nn.softmax(scores, axis=-1)
    attention_low = attention.astype(jnp.bfloat16)
    context = jnp.einsum(
        "ehrs,eshd->erhd", attention_low, values, preferred_element_type=jnp.float32
    )
    context = context.astype(jnp.bfloat16).reshape(examples * row_count, features)
    middle = inputs + (multiply(context, output) + output_bias.astype(jnp.float32))
    normed, unit_two, inverse_two = normalize(
        middle, gains[1].astype(jnp.float32), shifts[1].astype(jnp.float32)
    )
    normed_two = normed.astype(jnp.bfloat16)
    pre_gelu = multiply(normed_two, expand) + expand_bias.astype(jnp.float32)
    activated = jax.nn.gelu(pre_gelu).astype(jnp.bfloat16)
    block_out = middle + (multiply(activated, contract) + contract_bias.astype(jnp.float32))
    pooled = jnp.mean(block_out.reshape(examples, row_count, features), axis=1)
    inverse_norm = lax.rsqrt(jnp.sum(pooled * pooled, -1, keepdims=True) + EMBED_EPS)
    embedding = pooled * inverse_norm
    saved = (
        normed_one,
        unit_one,
        inverse_one,
        queries,
        keys,
        values,
        attention,
        attention_low,
        context,
        unit_two,
        inverse_two,
        normed_two,
        pre_gelu,
        activated,
        embedding,
        inverse_norm,
    )
    return (embedding, saved)


def backward(params, saved, grad_embedding, row_count):
    (
        gains,
        shifts,
        attend,
        attend_bias,
        output,
        output_bias,
        expand,
        expand_bias,
        contract,
        contract_bias,
    ) = params
    (
        normed_one,
        unit_one,
        inverse_one,
        queries,
        keys,
        values,
        attention,
        attention_low,
        context,
        unit_two,
        inverse_two,
        normed_two,
        pre_gelu,
        activated,
        embedding,
        inverse_norm,
    ) = saved
    examples, features = embedding.shape
    grad_pooled = inverse_norm * (
        grad_embedding - embedding * jnp.sum(grad_embedding * embedding, -1, keepdims=True)
    )
    grad_rows = jnp.broadcast_to(
        (grad_pooled / row_count)[:, None, :], (examples, row_count, features)
    ).reshape(examples * row_count, features)
    grad_mlp = grad_rows.astype(jnp.bfloat16)
    grad_contract = left_inner(activated, grad_mlp)
    grad_contract_bias = jnp.sum(grad_mlp.astype(jnp.float32), 0)
    grad_activated = right_inner(grad_mlp, contract)
    gelu_back = jax.vjp(jax.nn.gelu, pre_gelu)[1]
    grad_pre = gelu_back(grad_activated)[0].astype(jnp.bfloat16)
    grad_expand = left_inner(normed_two, grad_pre)
    grad_expand_bias = jnp.sum(grad_pre.astype(jnp.float32), 0)
    grad_normed_two = right_inner(grad_pre, expand)
    grad_middle, gain_two, shift_two = normalize_back(
        grad_normed_two, unit_two, inverse_two, gains[1].astype(jnp.float32)
    )
    grad_middle = grad_middle + grad_rows
    grad_branch = grad_middle.astype(jnp.bfloat16)
    grad_output = left_inner(context, grad_branch)
    grad_output_bias = jnp.sum(grad_branch.astype(jnp.float32), 0)
    grad_context = (
        right_inner(grad_branch, output)
        .astype(jnp.bfloat16)
        .reshape(examples, row_count, HEADS, HEAD_DIM)
    )
    grad_attention = jnp.einsum(
        "erhd,eshd->ehrs", grad_context, values, preferred_element_type=jnp.float32
    )
    grad_values = jnp.einsum(
        "ehrs,erhd->eshd", attention_low, grad_context, preferred_element_type=jnp.float32
    )
    grad_scores = (
        attention * (grad_attention - jnp.sum(grad_attention * attention, -1, keepdims=True))
    ).astype(jnp.bfloat16)
    grad_queries = jnp.einsum(
        "ehrs,eshd->erhd", grad_scores, keys, preferred_element_type=jnp.float32
    ) * HEAD_DIM ** (-0.5)
    grad_keys = jnp.einsum(
        "ehrs,erhd->eshd", grad_scores, queries, preferred_element_type=jnp.float32
    ) * HEAD_DIM ** (-0.5)
    grad_projected = (
        jnp.stack([grad_queries, grad_keys, grad_values], 2)
        .astype(jnp.bfloat16)
        .reshape(examples * row_count, 3 * features)
    )
    grad_attend = left_inner(normed_one, grad_projected)
    column_sums = jnp.sum(grad_projected.astype(jnp.float32), 0)
    grad_attend_bias = jnp.concatenate([column_sums[:features], column_sums[2 * features :]])
    grad_normed_one = right_inner(grad_projected, attend)
    grad_inputs, gain_one, shift_one = normalize_back(
        grad_normed_one, unit_one, inverse_one, gains[0].astype(jnp.float32)
    )
    grad_inputs = grad_inputs + grad_middle
    grads = (
        jnp.stack([gain_one, gain_two]),
        jnp.stack([shift_one, shift_two]),
        grad_attend,
        grad_attend_bias,
        grad_output,
        grad_output_bias,
        grad_expand,
        grad_expand_bias,
        grad_contract,
        grad_contract_bias,
    )
    return (grad_inputs.reshape(examples, row_count, features), grads)


def masked_softmax(logits, allowed, live_rows):
    filled = jnp.where(allowed, logits, -1e30)
    largest = jnp.max(filled, -1, keepdims=True)
    weights = jnp.exp(filled - largest) * allowed.astype(jnp.float32)
    safe_total = jnp.sum(weights, -1, keepdims=True) + (1.0 - live_rows)[:, None]
    return (weights / safe_total, largest[:, 0] + jnp.log(safe_total[:, 0]))


def plain_on_device(
    text_tokens,
    image_tokens,
    counts,
    caption_group,
    image_gains,
    image_shifts,
    image_attend,
    image_attend_bias,
    image_output,
    image_output_bias,
    image_expand,
    image_expand_bias,
    image_contract,
    image_contract_bias,
    text_gains,
    text_shifts,
    text_attend,
    text_attend_bias,
    text_output,
    text_output_bias,
    text_expand,
    text_expand_bias,
    text_contract,
    text_contract_bias,
):
    image_params = (
        image_gains,
        image_shifts,
        image_attend,
        image_attend_bias,
        image_output,
        image_output_bias,
        image_expand,
        image_expand_bias,
        image_contract,
        image_contract_bias,
    )
    text_params = (
        text_gains,
        text_shifts,
        text_attend,
        text_attend_bias,
        text_output,
        text_output_bias,
        text_expand,
        text_expand_bias,
        text_contract,
        text_contract_bias,
    )
    image_embedding, image_saved = plain_forward(image_tokens, image_params)
    text_embedding, text_saved = plain_forward(text_tokens, text_params)
    image_low = image_embedding.astype(jnp.bfloat16)
    text_low = text_embedding.astype(jnp.bfloat16)
    all_images, all_texts = (
        lax.all_gather(image_low, ("tower", "dp"), axis=0, tiled=True),
        lax.all_gather(text_low, ("tower", "dp"), axis=0, tiled=True),
    )
    per_device = image_low.shape[0]
    everyone = all_images.shape[0]
    device_rank = lax.axis_index(("tower", "dp"))
    positions = jnp.arange(everyone, dtype=jnp.int32)
    owned = device_rank * per_device + jnp.arange(per_device, dtype=jnp.int32)
    live_all = positions % per_device < jnp.repeat(counts, per_device, total_repeat_length=everyone)
    live_own = lax.dynamic_slice_in_dim(live_all, device_rank * per_device, per_device)
    group_own = lax.dynamic_slice_in_dim(caption_group, device_rank * per_device, per_device)
    diagonal = owned[:, None] == positions[None, :]
    allowed = (
        live_own[:, None]
        & live_all[None, :]
        & ((group_own[:, None] != caption_group[None, :]) | diagonal)
    )
    live_rows = live_own.astype(jnp.float32)
    diagonal_float = diagonal.astype(jnp.float32)
    forward_logits = right_inner(text_low, all_images) * LOGIT_SCALE
    backward_logits = right_inner(image_low, all_texts) * LOGIT_SCALE
    forward_probs, forward_lse = masked_softmax(forward_logits, allowed, live_rows)
    backward_probs, backward_lse = masked_softmax(backward_logits, allowed, live_rows)
    forward_terms = forward_lse - jnp.sum(forward_logits * diagonal_float, -1)
    backward_terms = backward_lse - jnp.sum(backward_logits * diagonal_float, -1)
    local_sum = 0.5 * (jnp.sum(live_rows * forward_terms) + jnp.sum(live_rows * backward_terms))
    loss_sum = lax.psum(local_sum, ("tower", "dp"))
    loss_value = loss_sum / jnp.sum(counts).astype(jnp.float32)
    forward_coef = (0.5 * live_rows[:, None] * (forward_probs - diagonal_float)).astype(
        jnp.bfloat16
    )
    grad_embedding = LOGIT_SCALE * multiply(forward_coef, all_images)
    lse_everyone = lax.all_gather(backward_lse, ("tower", "dp"), axis=0, tiled=True)
    shifted = jnp.where(allowed, forward_logits - lse_everyone[None, :], -1e30)
    live_columns = live_all.astype(jnp.float32)
    column_coef = (0.5 * live_columns[None, :] * (jnp.exp(shifted) - diagonal_float)).astype(
        jnp.bfloat16
    )
    grad_embedding = grad_embedding + LOGIT_SCALE * multiply(column_coef, all_images)
    text_grad, grads = backward(text_params, text_saved, grad_embedding, text_tokens.shape[1])
    shards = (
        lax.psum_scatter(grads[0], "dp", scatter_dimension=1, tiled=True),
        lax.psum_scatter(grads[1], "dp", scatter_dimension=1, tiled=True),
        lax.psum_scatter(grads[2], "dp", scatter_dimension=0, tiled=True),
        lax.psum_scatter(grads[3], "dp", scatter_dimension=0, tiled=True),
        lax.psum_scatter(grads[4], "dp", scatter_dimension=0, tiled=True),
        lax.psum_scatter(grads[5], "dp", scatter_dimension=0, tiled=True),
        lax.psum_scatter(grads[6], "dp", scatter_dimension=1, tiled=True),
        lax.psum_scatter(grads[7], "dp", scatter_dimension=0, tiled=True),
        lax.psum_scatter(grads[8], "dp", scatter_dimension=0, tiled=True),
        lax.psum_scatter(grads[9], "dp", scatter_dimension=0, tiled=True),
    )
    totals = (
        lax.psum(shards[0].astype(jnp.bfloat16), "tower").astype(jnp.float32),
        lax.psum(shards[1].astype(jnp.bfloat16), "tower").astype(jnp.float32),
        lax.psum(shards[2].astype(jnp.bfloat16), "tower").astype(jnp.float32),
        lax.psum(shards[3].astype(jnp.bfloat16), "tower").astype(jnp.float32),
        lax.psum(shards[4].astype(jnp.bfloat16), "tower").astype(jnp.float32),
        lax.psum(shards[5].astype(jnp.bfloat16), "tower").astype(jnp.float32),
        lax.psum(shards[6].astype(jnp.bfloat16), "tower").astype(jnp.float32),
        lax.psum(shards[7].astype(jnp.bfloat16), "tower").astype(jnp.float32),
        lax.psum(shards[8].astype(jnp.bfloat16), "tower").astype(jnp.float32),
        lax.psum(shards[9].astype(jnp.bfloat16), "tower").astype(jnp.float32),
    )
    return (
        loss_value,
        text_grad,
        totals[0],
        totals[1],
        totals[2],
        totals[3],
        totals[4],
        totals[5],
        totals[6],
        totals[7],
        totals[8],
        totals[9],
    )


def solution(mesh):
    n = mesh.shape["dp"]
    whole, both = P(), P(("tower", "dp"), None, None)
    fits = n & (n - 1) == 0 and n >= 4 and D // n % 16 == 0
    body = functools.partial(on_device, n) if fits else plain_on_device
    out_specs = (P(), both, P(None, "dp"), P(None, "dp"), P("dp", None), P("dp"), P("dp", None), P("dp"), P(None, "dp"), P("dp"), P("dp", None), P("dp"))
    return jax.shard_map(body, mesh=mesh, in_specs=(both, both) + (whole,) * 22, out_specs=out_specs, check_vma=False)
```

```python
import functools
import jax
import jax.numpy as jnp
import numpy as np
from jax import lax
from jax.experimental import pallas as pl
from jax.experimental.pallas import tpu as pltpu
from jax.sharding import PartitionSpec as P

F32, BF16 = jnp.float32, jnp.bfloat16
D, HD, FF = 768, 64, 3072
PAIRS = D // (2 * HD)
KW = 128
NORM_EPS, EMBED_EPS, LOGIT_SCALE = 1e-5, 1e-6, 64.0
NEG = -1e30
ANY = pl.BlockSpec(memory_space=pl.ANY)
VM = pl.BlockSpec(memory_space=pltpu.VMEM)
GELU_C, GELU_A = float(np.sqrt(2 / np.pi)), 0.044715


def dot(a, b):
    return jnp.dot(a, b, preferred_element_type=F32)


def dot_t(a, b):
    return lax.dot_general(a, b, (((1,), (1,)), ((), ())), preferred_element_type=F32)


def t_dot(a, b):
    return lax.dot_general(a, b, (((0,), (0,)), ((), ())), preferred_element_type=F32)


def unit_rows(v):
    centre = v - jnp.mean(v, -1, keepdims=True)
    inv = lax.rsqrt(jnp.mean(centre * centre, -1, keepdims=True) + NORM_EPS)
    return centre * inv, inv


def head_masks():
    lane = lax.broadcasted_iota(jnp.int32, (1, 2 * HD), 1)
    even = (lane < HD).astype(F32)
    return even.astype(BF16), (1.0 - even).astype(BF16)


def pair_mask(rows, per, real):
    r = lax.broadcasted_iota(jnp.int32, (rows, 2 * KW), 0)
    c = lax.broadcasted_iota(jnp.int32, (rows, 2 * KW), 1) % KW
    ok = (r // per == c // per) & (c % per < real) & (c < rows)
    return jnp.where(ok, 0.0, NEG).astype(F32)


def split_heads(a, even, odd):
    return jnp.concatenate([a * even, a * odd], axis=0)


def softmax_half(s):
    m = jnp.max(s, -1, keepdims=True)
    p = jnp.exp(s - m)
    return p / jnp.sum(p, -1, keepdims=True)


def exp_half(s):
    return jnp.exp(s - jnp.max(s, -1, keepdims=True)).astype(BF16)


def block_forward(x, rows, groups, small, W, wait, proj, ctx, mask, att_out, keep):
    attend, output, expand, contract = W
    unit, _ = unit_rows(x)
    n1 = (unit * small[0:1, :] + small[2:3, :]).astype(BF16)
    keep("n1", n1)
    wait("attend")
    M = rows * groups
    step = 256
    for c in range(3 * D // step):
        y = dot(n1, attend[:, c * step:(c + 1) * step])
        if c * step < D:
            y = y + small[4:5, c * step:(c + 1) * step]
        elif c * step >= 2 * D:
            y = y + small[5:6, c * step - 2 * D:(c + 1) * step - 2 * D]
        proj[0:M, c * step:(c + 1) * step] = y.astype(BF16)
    even, odd = head_masks()
    ones = split_heads(jnp.ones((KW, 2 * HD), BF16), even, odd)

    def group(g, _):
        r0 = pl.multiple_of(g * rows, 16)
        for j in range(PAIRS):
            lanes = slice(j * 2 * HD, (j + 1) * 2 * HD)
            q = proj[pl.ds(r0, rows), j * 128:(j + 1) * 128]
            kk = split_heads(proj[pl.ds(r0, KW), D + j * 128:D + (j + 1) * 128], even, odd)
            vv = split_heads(proj[pl.ds(r0, KW), 2 * D + j * 128:2 * D + (j + 1) * 128], even, odd)
            s = dot_t(q, kk) * HD ** -0.5 + mask[...]
            if att_out is None:
                p = jnp.concatenate([exp_half(s[:, :KW]), exp_half(s[:, KW:])], axis=1)
                both = dot(p, jnp.concatenate([vv, ones], axis=1))
                ctx[pl.ds(r0, rows), lanes] = (both[:, :128] / both[:, 128:]).astype(BF16)
            else:
                a = jnp.concatenate([softmax_half(s[:, :KW]), softmax_half(s[:, KW:])], axis=1)
                att_out[g * PAIRS + j] = a
                ctx[pl.ds(r0, rows), lanes] = dot(a.astype(BF16), vv).astype(BF16)
        return 0

    lax.fori_loop(0, groups, group, 0)
    wait("output")
    middle = x + (dot(ctx[...], output[...]) + small[6:7, :])
    keep("middle", middle)
    unit, _ = unit_rows(middle)
    n2 = (unit * small[1:2, :] + small[3:4, :]).astype(BF16)
    keep("n2", n2)
    wait("expand")
    acc = middle + small[11:12, :]
    step = 768
    for c in range(FF // step):
        pre = dot(n2, expand[:, c * step:(c + 1) * step]) + small[7 + c:8 + c, :]
        sq = pre * pre
        th = jnp.tanh(pre * (GELU_C + GELU_C * GELU_A * sq))
        cdf = 0.5 + 0.5 * th
        act = (pre * cdf).astype(BF16)
        keep("act", act, c, pre, sq, th, cdf)
        if c == 0:
            wait("contract")
        acc = acc + dot(act, contract[c * step:(c + 1) * step, :])
    return acc


def embed_rows(pooled):
    inv = lax.rsqrt(jnp.sum(pooled * pooled, -1, keepdims=True) + EMBED_EPS)
    return pooled * inv, inv


def image_kernel(per, real, pairs_step, x_ref, small, attend_h, output_h, expand_h, contract_h, low_ref,
                 attend, output, expand, contract, sems, xs, proj, ctx, mask):
    rows = 2 * per
    ex = 2 * pairs_step
    copies = {}
    for k, (n, h, v) in enumerate((("attend", attend_h, attend), ("output", output_h, output), ("expand", expand_h, expand), ("contract", contract_h, contract))):
        copies[n] = pltpu.make_async_copy(h, v, sems.at[k])
        copies[n].start()
    M = rows * pairs_step
    xs[...] = jnp.zeros_like(xs)
    proj[M:, :] = jnp.zeros((proj.shape[0] - M, 3 * D), BF16)
    mask[...] = pair_mask(rows, per, real)

    def chunk(i, _):
        def wait(n):
            @pl.when(i == 0)
            def _():
                copies[n].wait()
        for e in range(ex):
            xs[e * per:e * per + real, :] = x_ref[i * ex + e].astype(F32)
        out = block_forward(xs[...], rows, pairs_step, small, (attend, output, expand, contract), wait, proj, ctx, mask, None, lambda *a: None)
        out = out.reshape(ex, per, D)
        ok = lax.broadcasted_iota(jnp.int32, (ex, per, D), 1) < real
        pooled = jnp.sum(jnp.where(ok, out, 0.0), 1) * (1.0 / real)
        emb, _ = embed_rows(pooled)
        low_ref[i] = emb.astype(BF16)
        return 0

    lax.fori_loop(0, x_ref.shape[0] // ex, chunk, 0)


def image_forward(tokens, small, attend, output, expand, contract, pairs_step=8):
    n, real, _ = tokens.shape
    per = -(-real // 8) * 8
    rows = 2 * per
    ex = 2 * pairs_step
    M = rows * pairs_step
    low = pl.pallas_call(
        functools.partial(image_kernel, per, real, pairs_step),
        out_shape=jax.ShapeDtypeStruct((n // ex, ex, D), BF16),
        in_specs=[VM, VM, ANY, ANY, ANY, ANY], out_specs=VM,
        scratch_shapes=[pltpu.VMEM((D, 3 * D), BF16), pltpu.VMEM((D, D), BF16), pltpu.VMEM((D, FF), BF16), pltpu.VMEM((FF, D), BF16),
                        pltpu.SemaphoreType.DMA((4,)), pltpu.VMEM((M, D), F32), pltpu.VMEM((M + 16, 3 * D), BF16), pltpu.VMEM((M, D), BF16), pltpu.VMEM((rows, 2 * KW), F32)],
        compiler_params=pltpu.CompilerParams(vmem_limit_bytes=56 << 20),
        name="image_forward",
    )(tokens, small, attend, output, expand, contract)
    return low.reshape(n, D)


def text_kernel(per, n_dp, x_ref, small, attend_h, output_h, expand_h, contract_h,
                low_ref, emb_ref, inv_ref, asum_ref, n1_ref, proj_ref, att_ref, ctx_ref, mid_ref, n2_ref, gp_ref,
                attend, output, expand, contract, sems, mask):
    copies = {}
    for k, (n, h, v) in enumerate((("attend", attend_h, attend), ("output", output_h, output), ("expand", expand_h, expand), ("contract", contract_h, contract))):
        copies[n] = pltpu.make_async_copy(h, v, sems.at[k])
        copies[n].start()
    rows = KW
    M = x_ref.shape[0]
    ex = M // per
    mask[...] = pair_mask(rows, per, per)
    shard = FF // n_dp
    wide = asum_ref.shape[1] // n_dp
    for k in range(n_dp):
        asum_ref[:, k * wide + shard:(k + 1) * wide] = jnp.full((ex, wide - shard), per, BF16)

    def keep(name, value, *extra):
        if name == "n1":
            n1_ref[...] = value
        elif name == "middle":
            mid_ref[...] = value
        elif name == "n2":
            n2_ref[...] = value
        else:
            c, pre, sq, th, cdf = extra
            w = value.shape[1]
            total = jnp.sum(value.astype(F32).reshape(ex, per, w), 1).astype(BF16)
            for k in range(c * w // shard, (c + 1) * w // shard):
                asum_ref[:, k * wide:k * wide + shard] = total[:, k * shard - c * w:(k + 1) * shard - c * w]
            gp_ref[:, c * w:(c + 1) * w] = (cdf + (0.5 * GELU_C) * pre * (1.0 - th * th) * (1.0 + (3 * GELU_A) * sq)).astype(BF16)

    out = block_forward(x_ref[...].astype(F32), rows, M // rows, small, (attend, output, expand, contract), lambda n: copies[n].wait(), proj_ref, ctx_ref, mask, att_ref, keep)
    pooled = jnp.sum(out.reshape(ex, per, D), 1) * (1.0 / per)
    emb, inv = embed_rows(pooled)
    low_ref[...] = emb.astype(BF16)
    emb_ref[...] = emb
    inv_ref[...] = jnp.broadcast_to(inv, inv_ref.shape)


def wide_of(n_dp):
    return -(-(FF // n_dp + 1) // 128) * 128


def text_forward(tokens, small, attend, output, expand, contract, n_dp):
    n, per, _ = tokens.shape
    M = n * per
    S = jax.ShapeDtypeStruct
    outs = [S((n, D), BF16), S((n, D), F32), S((n, 128), F32), S((n, n_dp * wide_of(n_dp)), BF16), S((M, D), BF16), S((M, 3 * D), BF16),
            S((M // KW * PAIRS, KW, 2 * KW), F32), S((M, D), BF16), S((M, D), F32), S((M, D), BF16), S((M, FF), BF16)]
    return pl.pallas_call(
        functools.partial(text_kernel, per, n_dp), out_shape=outs,
        in_specs=[VM, VM, ANY, ANY, ANY, ANY], out_specs=[VM] * len(outs),
        scratch_shapes=[pltpu.VMEM((D, 3 * D), BF16), pltpu.VMEM((D, D), BF16), pltpu.VMEM((D, FF), BF16), pltpu.VMEM((FF, D), BF16),
                        pltpu.SemaphoreType.DMA((4,)), pltpu.VMEM((KW, 2 * KW), F32)],
        compiler_params=pltpu.CompilerParams(vmem_limit_bytes=60 << 20),
        name="text_forward",
    )(tokens.reshape(M, D), small, attend, output, expand, contract)


def pack_small(gains, shifts, attend_bias, output_bias, expand_bias, contract_bias):
    parts = [gains, shifts, attend_bias.reshape(2, D), output_bias.reshape(1, D), expand_bias.reshape(FF // D, D), contract_bias.reshape(1, D)]
    return jnp.concatenate([p.astype(F32) for p in parts], 0)


MESH_ID = pl.DeviceIdType.MESH


def place():
    return lax.axis_index("tower"), lax.axis_index("dp")


def greet(n):
    t, d = place()
    barrier = pltpu.get_barrier_semaphore()

    def one(k, _):
        who = (lax.rem(t + k // n, 2), lax.rem(d + lax.rem(k, n), n))
        pl.semaphore_signal(barrier, inc=1, device_id=who, device_id_type=MESH_ID)
        return 0

    lax.fori_loop(1, 2 * n, one, 0)


def spread(n, src, dst, send, recv):
    t, d = place()

    def one(k, _):
        pltpu.make_async_remote_copy(src_ref=src, dst_ref=dst.at[d], send_sem=send, recv_sem=recv,
                                     device_id=(t, lax.rem(d + k, n)), device_id_type=MESH_ID).start()
        return 0

    lax.fori_loop(1, n, one, 0)


def settle(n, dst, send, recv):
    part = dst.at[pl.ds(0, n - 1)]
    pltpu.make_async_copy(part, part, send).wait()
    pltpu.make_async_copy(part, part, recv).wait()


def contrast_rows(fl, allowed, live_rows):
    filled = jnp.where(allowed, fl, NEG)
    largest = jnp.max(filled, -1, keepdims=True)
    weights = jnp.where(allowed, jnp.exp(filled - largest), 0.0)
    total = jnp.sum(weights, -1, keepdims=True) + (1.0 - live_rows)
    return weights / total, largest + jnp.log(total)


def loss_kernel(n, low_ref, asum_ref, meta_ref, emb_ref, inv_ref,
                g_ref, grow_ref, loss_ref, ag_ref, lows, own_rows, sems):
    t, d = place()
    ex = low_ref.shape[1]
    wide = ag_ref.shape[2]
    greet(n)
    pl.semaphore_wait(pltpu.get_barrier_semaphore(), 2 * n - 1)
    spread(n, low_ref, lows.at[t], sems.at[0], sems.at[1])

    def one(k, _):
        to = lax.rem(d + k, n)
        pltpu.make_async_remote_copy(src_ref=asum_ref.at[to], dst_ref=ag_ref.at[d], send_sem=sems.at[2], recv_sem=sems.at[3],
                                     device_id=(t, to), device_id_type=MESH_ID).start()
        return 0

    lax.fori_loop(1, n, one, 0)
    lows[t, d] = low_ref[...]
    ag_ref[d] = asum_ref[d]
    settle(n, lows.at[t], sems.at[0], sems.at[1])
    over = pltpu.make_async_remote_copy(src_ref=lows.at[t], dst_ref=lows.at[t], send_sem=sems.at[4], recv_sem=sems.at[5],
                                        device_id=(1 - t, d), device_id_type=MESH_ID)
    over.start()
    over.wait()
    settle(n, ag_ref, sems.at[2], sems.at[3])

    every = 2 * n * ex
    both = lows[...].reshape(2 * n, 2, ex, D)
    texts, images = both[:, 0].reshape(every, D), both[:, 1].reshape(every, D)
    rank = t * n + d
    row_group, row_live = meta_ref[0:1, :], meta_ref[1:2, :]
    position = lax.broadcasted_iota(jnp.int32, (ex, every), 1)
    diagonal = (position == lax.broadcasted_iota(jnp.int32, (ex, every), 0) + rank * ex).astype(F32)
    columns = jnp.transpose(jnp.broadcast_to(meta_ref[0:1, :], (128, every)))[:, 0:1], jnp.transpose(jnp.broadcast_to(meta_ref[1:2, :], (128, every)))[:, 0:1]
    logits = dot_t(texts, images) * LOGIT_SCALE
    same = lax.broadcasted_iota(jnp.int32, (every, every), 0) == lax.broadcasted_iota(jnp.int32, (every, every), 1)
    allowed = (columns[1] * row_live > 0.0) & ((columns[0] != row_group) | same)
    filled = jnp.where(allowed, logits, NEG)
    largest = jnp.max(filled, 0, keepdims=True)
    total = jnp.sum(jnp.where(allowed, jnp.exp(filled - largest), 0.0), 0, keepdims=True) + (1.0 - row_live)
    image_lse = largest + jnp.log(total)
    own_rows[...] = dot_t(low_ref[0], images) * LOGIT_SCALE
    fl = own_rows[...]
    live_own = jnp.sum(diagonal * row_live, -1, keepdims=True)
    group_own = jnp.sum(diagonal * row_group, -1, keepdims=True)
    allowed = (live_own * row_live > 0.0) & ((group_own != row_group) | (diagonal > 0.0))
    probs, text_lse = contrast_rows(fl, allowed, live_own)
    own_diag = fl * diagonal
    terms = live_own * (text_lse - jnp.sum(own_diag, -1, keepdims=True))
    terms2 = jnp.sum(diagonal * (live_own * image_lse) - live_own * own_diag, -1, keepdims=True)
    loss_ref[...] = jnp.broadcast_to(0.5 * jnp.sum(terms + terms2, 0, keepdims=True), loss_ref.shape)
    forward_coef = (0.5 * live_own * (probs - diagonal)).astype(BF16)
    shifted = jnp.where(allowed, jnp.exp(jnp.where(allowed, fl - image_lse, NEG)), 0.0)
    column_coef = (0.5 * row_live * (shifted - diagonal)).astype(BF16)
    grad = LOGIT_SCALE * dot(forward_coef, images) + LOGIT_SCALE * dot(column_coef, images)
    emb = emb_ref[...]
    pooled = inv_ref[:, 0:1] * (grad - emb * jnp.sum(grad * emb, -1, keepdims=True))
    rows = pooled * meta_ref[2:3, 0:1]
    grow_ref[...] = rows
    g_ref[...] = rows.astype(BF16)


def exchange_and_loss(n, lows, asum, meta, emb, inv):
    _, ex, _ = lows.shape
    wide = asum.shape[1] // n
    S = jax.ShapeDtypeStruct
    return pl.pallas_call(
        functools.partial(loss_kernel, n),
        out_shape=[S((ex, D), BF16), S((ex, D), F32), S((8, 128), F32), S((n, ex, wide), BF16)],
        in_specs=[VM] * 5, out_specs=[VM] * 4,
        scratch_shapes=[pltpu.VMEM((2, n, 2, ex, D), BF16), pltpu.VMEM((ex, 2 * n * ex), F32), pltpu.SemaphoreType.DMA((6,))],
        compiler_params=pltpu.CompilerParams(collective_id=0, has_side_effects=True, vmem_limit_bytes=56 << 20),
        name="gather_and_loss",
    )(lows, asum.reshape(ex, n, wide).transpose(1, 0, 2), meta, emb, inv)


def norm_back(grad, unit, inv, gain):
    gu = grad * gain
    out = inv * (gu - jnp.mean(gu, -1, keepdims=True) - unit * jnp.mean(gu * unit, -1, keepdims=True))
    return out, jnp.sum(grad * unit, 0, keepdims=True), jnp.sum(grad, 0, keepdims=True)


def back_kernel(per, n, small, g_ref, grow_ref, ag_ref, loss_ref, x_h, n1_h, proj_h, att_h, ctx_h, mid_h, n2_h, gp_h, contract_h, expand_h, output_h, attend_h,
                tg_ref, oe_ref, oa_ref, oo_ref, os_ref, oc_ref, ol_ref,
                xb, n1, proj, att, ctx, mid, n2, gp, contract, expand, output, attend, gctx, gproj, rowsums,
                grads, core_in, in1, in2, red, zin_e, zin_a, fin_e, fin_a, s_out, s_in, s_fin, gall, pc, pc_in, lossall,
                load, csem_s, csem_r, sem1_s, sem1_r, sem2_s, sem2_r, zsem_s, zsem_r, fsem_s, fsem_r, gsem, lsem, ssem):
    t, d = place()
    dx, dy, dz, nz = lax.rem(d, 2), lax.rem(d // 2, 2), d // 4, n // 4
    other = (1 - t, d)
    partner = ((t, d + 1 - 2 * dx), (t, d + 2 - 4 * dy))
    greet(n)
    copies = {}
    for k, (name, h, v) in enumerate((("contract", contract_h, contract), ("gp", gp_h, gp), ("n2", n2_h, n2), ("expand", expand_h, expand), ("mid", mid_h, mid), ("ctx", ctx_h, ctx),
                                      ("output", output_h, output), ("proj", proj_h, proj), ("att", att_h, att), ("n1", n1_h, n1), ("attend", attend_h, attend), ("x", x_h, xb))):
        copies[name] = pltpu.make_async_copy(h, v, load.at[k])
        copies[name].start()
    M = xb.shape[0]
    ex = M // per
    rows_e, rows_a, H = FF // n, D // n, D // 2
    B = D // 2
    Q, E8 = B // 4, B // 2

    def remote(src, dst, ss, rs, who):
        return pltpu.make_async_remote_copy(src_ref=src, dst_ref=dst, send_sem=ss, recv_sem=rs, device_id=who, device_id_type=MESH_ID)

    def core_copy(q):
        return remote(grads.at[q, 1 - t], core_in.at[q], csem_s.at[q], csem_r.at[q], other)

    def first_copy(q, b):
        away = pl.multiple_of(b * B + (1 - (dx, dy)[b]) * E8, 16)
        return remote(grads.at[q, t, pl.ds(away, E8)], in1.at[q, b], sem1_s.at[q, b], sem1_r.at[q, b], partner[b])

    def second_copy(q, b):
        away = pl.multiple_of(b * B + (dx, dy)[b] * E8 + (1 - (dy, dx)[b]) * Q, 16)
        return remote(grads.at[q, t, pl.ds(away, Q)], in2.at[q, b], sem2_s.at[q, b], sem2_r.at[q, b], partner[1 - b])

    def step0(q):
        core_copy(q).start()

    def step1(q):
        core_copy(q).wait()
        grads[q, t] = (grads[q, t].astype(F32) + core_in[q].astype(F32)).astype(BF16)
        for b in range(2):
            first_copy(q, b).start()

    def step2(q):
        for b in range(2):
            first_copy(q, b).wait()
            keep = pl.multiple_of(b * B + (dx, dy)[b] * E8, 16)
            grads[q, t, pl.ds(keep, E8)] = (grads[q, t, pl.ds(keep, E8)].astype(F32) + in1[q, b].astype(F32)).astype(BF16)
            second_copy(q, b).start()

    def step3(q):
        for b in range(2):
            second_copy(q, b).wait()
            keep = pl.multiple_of(b * B + (dx, dy)[b] * E8 + (dy, dx)[b] * Q, 16)
            red[q, b * Q:(b + 1) * Q] = (grads[q, t, pl.ds(keep, Q)].astype(F32) + in2[q, b].astype(F32)).astype(BF16)

    def over_z(k):
        to = lax.rem(dz + k, nz)
        return to, (t, to * 4 + lax.rem(d, 4))

    def z_expand():
        for k in range(1, nz):
            to, who = over_z(k)
            remote(red.at[to], zin_e.at[dz], zsem_s.at[nz], zsem_r.at[nz], who).start()
        zin_e[dz] = red[dz]

    def z_attend(a):
        for k in range(1, nz):
            to, who = over_z(k)
            remote(red.at[nz + a, pl.ds(pl.multiple_of(to * rows_a, 16), rows_a)], zin_a.at[a, dz], zsem_s.at[a], zsem_r.at[a], who).start()
        zin_a[a, dz] = red[nz + a, pl.ds(pl.multiple_of(dz * rows_a, 16), rows_a)]

    def all_but_one(ref, count, ss, rs):
        part = ref.at[pl.ds(0, count)]
        pltpu.make_async_copy(part, part, ss).wait()
        pltpu.make_async_copy(part, part, rs).wait()

    def fin_copy(k):
        ref = fin_e if k == 4 else fin_a.at[k]
        return remote(ref.at[t], ref.at[t], fsem_s.at[k], fsem_r.at[k], other)

    def last_expand():
        all_but_one(zin_e, nz - 1, zsem_s.at[nz], zsem_r.at[nz])
        fin_e[t] = jnp.sum(zin_e[...].astype(F32), 0).astype(BF16)
        fin_copy(4).start()

    def last_attend(a):
        all_but_one(zin_a.at[a], nz - 1, zsem_s.at[a], zsem_r.at[a])
        fin_a[a, t] = jnp.sum(zin_a[a].astype(F32), 0).astype(BF16)
        fin_copy(a).start()

    def put_rows(q, value, lanes):
        for s in range(n):
            z, y, x = s // 4, s // 2 % 2, s % 2
            p = (2 * x + y) * Q + z * rows_a if z < nz // 2 else B + (2 * y + x) * Q + (z - nz // 2) * rows_a
            for h in range(2):
                for src, dst, w in lanes(h):
                    grads[q, h, p:p + rows_a, dst:dst + w] = value[s * rows_a:(s + 1) * rows_a, src:src + w]

    g_low = g_ref[...]
    step = FF // nz
    gn2 = None
    for c in range(nz):
        cols = slice(c * step, (c + 1) * step)
        if c == 0:
            copies["contract"].wait()
        ga = dot_t(g_low, contract[cols, :])
        if c == 0:
            copies["gp"].wait()
            copies["n2"].wait()
        pre = (ga[:, None, :] * gp[:, cols].astype(F32).reshape(ex, per, step)).reshape(M, step).astype(BF16)
        rowsums[8 + c:9 + c, :] = jnp.sum(pre.astype(F32), 0, keepdims=True)
        ge = t_dot(pre, n2[...]).astype(BF16)
        for y in range(2):
            for x in range(2):
                at = (2 * y + x) * rows_e
                for h in range(2):
                    grads[c, h, (2 * x + y) * Q:(2 * x + y + 1) * Q, :] = ge[at:at + Q, h * H:(h + 1) * H]
                    grads[c, h, B + (2 * y + x) * Q:B + (2 * y + x + 1) * Q, :] = ge[at + Q:at + 2 * Q, h * H:(h + 1) * H]
        if c == 0:
            pl.semaphore_wait(pltpu.get_barrier_semaphore(), 2 * n - 1)
        step0(c)
        if c == 0:
            spread(n, g_ref, gall, gsem.at[0], gsem.at[1])
            copies["expand"].wait()
        part = dot_t(pre, expand[:, cols])
        gn2 = part if gn2 is None else gn2 + part
        if c >= 1:
            step1(c - 1)
        if c >= 2:
            step2(c - 2)
    gall[d] = g_ref[...]
    copies["mid"].wait()
    unit, inv = unit_rows(mid[...])
    gm, gain_two, shift_two = norm_back(gn2, unit, inv, small[1:2, :])
    rowsums[1:2, :] = gain_two
    rowsums[3:4, :] = shift_two
    gm = (gm.reshape(ex, per, D) + grow_ref[...][:, None, :]).reshape(M, D)
    tg_ref[...] = gm
    gb = gm.astype(BF16)
    rowsums[12:13, :] = jnp.sum(gb.astype(F32), 0, keepdims=True)
    step1(nz - 1)
    copies["ctx"].wait()
    put_rows(nz, t_dot(ctx[...], gb).astype(BF16), lambda h: [(h * H, 0, H)])
    step0(nz)
    step2(nz - 2)
    copies["output"].wait()
    gctx[...] = dot_t(gb, output[...]).astype(BF16)
    even, odd = head_masks()
    lane = lax.broadcasted_iota(jnp.int32, (KW, 2 * HD), 1)
    copies["proj"].wait()
    copies["att"].wait()

    for third in range(3):
        def group(i, _):
            r0 = pl.multiple_of(i * KW, KW)
            for j in (2 * third, 2 * third + 1):
                L = slice(j * 128, (j + 1) * 128)
                gc = gctx[pl.ds(r0, KW), L]
                q = proj[pl.ds(r0, KW), j * 128:(j + 1) * 128]
                kk = split_heads(proj[pl.ds(r0, KW), D + j * 128:D + (j + 1) * 128], even, odd)
                vv = split_heads(proj[pl.ds(r0, KW), 2 * D + j * 128:2 * D + (j + 1) * 128], even, odd)
                a = att[i * PAIRS + j]
                gatt = dot_t(gc, vv)
                prod = gatt * a
                gs = jnp.concatenate([a[:, h * KW:(h + 1) * KW] * (gatt[:, h * KW:(h + 1) * KW] - jnp.sum(prod[:, h * KW:(h + 1) * KW], -1, keepdims=True)) for h in range(2)], axis=1).astype(BF16)
                gv = t_dot(a.astype(BF16), gc)
                gk = t_dot(gs, q) * HD ** -0.5
                gproj[pl.ds(r0, KW), j * 128:(j + 1) * 128] = (dot(gs, kk) * HD ** -0.5).astype(BF16)
                gproj[pl.ds(r0, KW), D + j * 128:D + (j + 1) * 128] = jnp.where(lane < HD, gk[:KW], gk[KW:]).astype(BF16)
                gproj[pl.ds(r0, KW), 2 * D + j * 128:2 * D + (j + 1) * 128] = jnp.where(lane < HD, gv[:KW], gv[KW:]).astype(BF16)
            return 0

        lax.fori_loop(0, M // KW, group, 0)
        if third == 0:
            step1(nz)
            copies["n1"].wait()
        wide3 = jnp.concatenate([gproj[:, part * D + 256 * third:part * D + 256 * (third + 1)] for part in range(3)], axis=1)
        put_rows(nz + 1 + third, t_dot(n1[...], wide3).astype(BF16), lambda h: [(256 * part + 128 * h, 128 * part, 128) for part in range(3)])
        step0(nz + 1 + third)
        if third == 0:
            step2(nz - 1)
            for c in range(nz - 2):
                step3(c)
        elif third == 1:
            step1(nz + 1)
            step2(nz)
            step3(nz - 2)
        else:
            step3(nz - 1)
            z_expand()
            step1(nz + 2)
            step2(nz + 1)
            step3(nz)
            z_attend(0)
    rowsums[4:5, :] = jnp.sum(gproj[:, 0:D].astype(F32), 0, keepdims=True)
    rowsums[5:6, :] = rowsums[4:5, :]
    rowsums[6:7, :] = jnp.sum(gproj[:, 2 * D:3 * D].astype(F32), 0, keepdims=True)
    rowsums[7:8, :] = rowsums[6:7, :]
    step1(nz + 3)
    copies["attend"].wait()
    gn1 = dot_t(gproj[...], attend[...])
    step2(nz + 2)
    copies["x"].wait()
    unit, inv = unit_rows(xb[...].astype(F32))
    gx, gain_one, shift_one = norm_back(gn1, unit, inv, small[0:1, :])
    tg_ref[...] += gx
    rowsums[0:1, :] = gain_one
    rowsums[2:3, :] = shift_one
    sums = rowsums[...]
    parts = [sums[0:8, :]] + [jnp.broadcast_to(sums[8 + r:9 + r, :], (4, D)) for r in range(4)] + [sums[12:13, :], jnp.zeros((128 - 25, D), F32)]
    cols = jnp.transpose(jnp.concatenate(parts, 0))
    at = lax.broadcasted_iota(jnp.int32, (rows_a, 128), 1)
    for s in range(n):
        piece = jnp.where((at < 4) | (at == 24), cols[s * rows_a:(s + 1) * rows_a, :], 0.0)
        r0, first = 2 * s * rows_a % D, 2 * s * rows_a // D * 2
        for c in range(2):
            piece = jnp.where(at == 4 + first + c, cols[r0 + c * rows_a:r0 + (c + 1) * rows_a, :], piece)
        r0, first = 4 * s * rows_a % D, 4 * s * rows_a // D * 4
        for c in range(4):
            piece = jnp.where(at == 8 + first + c, cols[r0 + c * rows_a:r0 + (c + 1) * rows_a, :], piece)
        s_out[s] = piece.astype(BF16)

    def small_send(k, _):
        to = lax.rem(d + k, n)
        remote(s_out.at[to], s_in.at[d], ssem.at[0], ssem.at[1], (t, to)).start()
        return 0

    lax.fori_loop(1, n, small_send, 0)
    s_in[d] = s_out[d]

    def tell(k, _):
        who = (lax.rem(t + k // n, 2), lax.rem(d + lax.rem(k, n), n))
        remote(loss_ref, lossall.at[t * n + d], lsem.at[0], lsem.at[1], who).start()
        return 0

    lax.fori_loop(1, 2 * n, tell, 0)
    lossall[t * n + d] = loss_ref[...]
    step3(nz + 1)
    z_attend(1)
    step2(nz + 3)
    settle(n, gall, gsem.at[0], gsem.at[1])
    wide = ag_ref.shape[2]
    pc[...] = t_dot(ag_ref[...].reshape(n * ex, wide), gall[...].reshape(n * ex, D)).astype(BF16)
    pc_copy = remote(pc, pc_in, fsem_s.at[5], fsem_r.at[5], other)
    pc_copy.start()
    last_expand()
    last_attend(0)
    step3(nz + 2)
    z_attend(2)
    step3(nz + 3)
    z_attend(3)
    all_but_one(s_in, n - 1, ssem.at[0], ssem.at[1])
    s_fin[t] = jnp.sum(s_in[...].astype(F32), 0).astype(BF16)
    s_copy = remote(s_fin.at[t], s_fin.at[t], fsem_s.at[6], fsem_r.at[6], other)
    s_copy.start()
    all_but_one(lossall, 2 * n - 1, lsem.at[0], lsem.at[1])
    ol_ref[...] = jnp.sum(lossall[...], 0)
    last_attend(1)
    pc_copy.wait()
    oc_ref[...] = pc[...].astype(F32) + pc_in[...].astype(F32)
    fin_copy(4).wait()
    for h in range(2):
        oe_ref[:, h * H:(h + 1) * H] = fin_e[h].astype(F32)
    s_copy.wait()
    os_ref[...] = s_fin[0].astype(F32) + s_fin[1].astype(F32)
    last_attend(2)
    last_attend(3)
    fin_copy(0).wait()
    for h in range(2):
        oo_ref[:, h * H:(h + 1) * H] = fin_a[0, h].astype(F32)
    for third in range(3):
        fin_copy(1 + third).wait()
        for h in range(2):
            for part in range(3):
                lo = part * D + 256 * third + 128 * h
                oa_ref[:, lo:lo + 128] = fin_a[1 + third, h, :, 128 * part:128 * (part + 1)].astype(F32)


def text_backward(per, n, x, small, g, grow, ag, loss, saved, attend, output, expand, contract):
    n1, proj, att, ctx, mid, n2, gp = saved
    M = x.shape[0]
    ex, wide, nz = g.shape[0], ag.shape[2], n // 4
    rows_e, rows_a, H = FF // n, D // n, D // 2
    S = jax.ShapeDtypeStruct
    V = lambda *shape: pltpu.VMEM(shape, BF16)
    like = lambda a: pltpu.VMEM(a.shape, a.dtype)
    outs = [S((M, D), F32), S((rows_e, D), F32), S((rows_a, 3 * D), F32), S((rows_a, D), F32), S((rows_a, 128), F32), S((wide, D), F32), S((8, 128), F32)]
    q = nz + 4
    dma = pltpu.SemaphoreType.DMA
    held = (x, n1, proj, att, ctx, mid, n2, gp, contract, expand, output, attend)
    scratch = [like(a) for a in held] + [V(M, D), V(M, 3 * D), pltpu.VMEM((16, D), F32)]
    scratch += [V(q, 2, D, H), V(q, D, H), V(q, 2, D // 4, H), V(q, 2, D // 8, H), V(q, D // 4, H), V(nz, D // 4, H), V(4, nz, rows_a, H), V(2, D // 4, H), V(4, 2, rows_a, H),
                V(n, rows_a, 128), V(n, rows_a, 128), V(2, rows_a, 128), V(n, ex, D), V(wide, D), V(wide, D), pltpu.VMEM((2 * n, 8, 128), F32)]
    scratch += [dma((12,)), dma((q,)), dma((q,)), dma((q, 2)), dma((q, 2)), dma((q, 2)), dma((q, 2)), dma((nz + 4,)), dma((nz + 4,)), dma((7,)), dma((7,)), dma((2,)), dma((2,)), dma((2,))]
    return pl.pallas_call(
        functools.partial(back_kernel, per, n), out_shape=outs, in_specs=[VM] * 5 + [ANY] * 12, out_specs=[VM] * 7, scratch_shapes=scratch,
        compiler_params=pltpu.CompilerParams(collective_id=1, has_side_effects=True, vmem_limit_bytes=63 << 20),
        name="text_backward",
    )(small, g, grow, ag, loss, x, n1, proj, att, ctx, mid, n2, gp, contract, expand, output, attend)


def on_device(n, text_tokens, image_tokens, counts, caption_group, *weights):
    (image_gains, image_shifts, image_attend, image_attend_bias, image_output, image_output_bias, image_expand, image_expand_bias, image_contract, image_contract_bias,
     text_gains, text_shifts, text_attend, text_attend_bias, text_output, text_output_bias, text_expand, text_expand_bias, text_contract, text_contract_bias) = weights
    ex, per, _ = text_tokens.shape
    image_small = pack_small(image_gains, image_shifts, image_attend_bias, image_output_bias, image_expand_bias, image_contract_bias)
    text_small = pack_small(text_gains, text_shifts, text_attend_bias, text_output_bias, text_expand_bias, text_contract_bias)
    every = caption_group.shape[0]
    live = (jnp.arange(ex, dtype=jnp.int32)[None, :] < counts[:, None]).reshape(1, every).astype(F32)
    meta = jnp.concatenate([caption_group.astype(F32)[None, :], live, jnp.full((6, every), 1.0 / per, F32)], 0)
    low, emb, inv, asum, *saved = text_forward(text_tokens, text_small, text_attend, text_output, text_expand, text_contract, n)
    image_low = image_forward(image_tokens, image_small, image_attend, image_output, image_expand, image_contract)
    g, grow, loss, ag = exchange_and_loss(n, jnp.stack([low, image_low]), asum, meta, emb, inv)
    text_grad, oe, oa, oo, os, oc, ol = text_backward(per, n, text_tokens.reshape(ex * per, D), text_small, g, grow, ag, loss, saved, text_attend, text_output, text_expand, text_contract)
    d = lax.axis_index("dp")
    rows_e, rows_a = FF // n, D // n
    loss_value = ol[0, 0] / jnp.sum(counts).astype(F32)
    low_bias, high_bias = os[:, 4:6] + os[:, 6:8], os[:, 8:12] + os[:, 12:16] + os[:, 16:20] + os[:, 20:24]
    return (loss_value, text_grad.reshape(ex, per, D), os[:, 0:2].T, os[:, 2:4].T, oa, low_bias.T.reshape(2 * rows_a), oo, os[:, 24],
            oe.T, high_bias.T.reshape(4 * rows_a), oc[:rows_e], lax.dynamic_slice(oc[rows_e], (d * rows_a,), (rows_a,)))


HEADS = 12
HEAD_DIM = 64


def multiply(left, right):
    return jnp.dot(left, right, preferred_element_type=jnp.float32)


def left_inner(left, right):
    return lax.dot_general(
        left, right, (((0,), (0,)), ((), ())), preferred_element_type=jnp.float32
    )


def right_inner(left, right):
    return lax.dot_general(
        left, right, (((1,), (1,)), ((), ())), preferred_element_type=jnp.float32
    )


def normalize(rows_in, gain, shift):
    centre = rows_in - jnp.mean(rows_in, -1, keepdims=True)
    inverse_std = lax.rsqrt(jnp.mean(centre * centre, -1, keepdims=True) + NORM_EPS)
    unit_rows = centre * inverse_std
    return (unit_rows * gain + shift, unit_rows, inverse_std)


def normalize_back(grad_rows, unit_rows, inverse_std, gain):
    grad_unit = grad_rows * gain
    grad_in = inverse_std * (
        grad_unit
        - jnp.mean(grad_unit, -1, keepdims=True)
        - unit_rows * jnp.mean(grad_unit * unit_rows, -1, keepdims=True)
    )
    return (grad_in, jnp.sum(grad_rows * unit_rows, 0), jnp.sum(grad_rows, 0))


def plain_forward(tokens, params):
    (
        gains,
        shifts,
        attend,
        attend_bias,
        output,
        output_bias,
        expand,
        expand_bias,
        contract,
        contract_bias,
    ) = params
    examples, row_count, features = tokens.shape
    inputs = tokens.astype(jnp.float32).reshape(examples * row_count, features)
    normed, unit_one, inverse_one = normalize(
        inputs, gains[0].astype(jnp.float32), shifts[0].astype(jnp.float32)
    )
    normed_one = normed.astype(jnp.bfloat16)
    full_bias = jnp.concatenate(
        [attend_bias[:features], jnp.zeros_like(output_bias), attend_bias[features:]]
    ).astype(jnp.float32)
    projected = (multiply(normed_one, attend) + full_bias).astype(jnp.bfloat16)
    projected = projected.reshape(examples, row_count, 3, HEADS, HEAD_DIM)
    queries = projected[:, :, 0]
    keys = projected[:, :, 1]
    values = projected[:, :, 2]
    scores = jnp.einsum(
        "erhd,eshd->ehrs", queries, keys, preferred_element_type=jnp.float32
    ) * HEAD_DIM ** (-0.5)
    attention = jax.nn.softmax(scores, axis=-1)
    attention_low = attention.astype(jnp.bfloat16)
    context = jnp.einsum(
        "ehrs,eshd->erhd", attention_low, values, preferred_element_type=jnp.float32
    )
    context = context.astype(jnp.bfloat16).reshape(examples * row_count, features)
    middle = inputs + (multiply(context, output) + output_bias.astype(jnp.float32))
    normed, unit_two, inverse_two = normalize(
        middle, gains[1].astype(jnp.float32), shifts[1].astype(jnp.float32)
    )
    normed_two = normed.astype(jnp.bfloat16)
    pre_gelu = multiply(normed_two, expand) + expand_bias.astype(jnp.float32)
    activated = jax.nn.gelu(pre_gelu).astype(jnp.bfloat16)
    block_out = middle + (multiply(activated, contract) + contract_bias.astype(jnp.float32))
    pooled = jnp.mean(block_out.reshape(examples, row_count, features), axis=1)
    inverse_norm = lax.rsqrt(jnp.sum(pooled * pooled, -1, keepdims=True) + EMBED_EPS)
    embedding = pooled * inverse_norm
    saved = (
        normed_one,
        unit_one,
        inverse_one,
        queries,
        keys,
        values,
        attention,
        attention_low,
        context,
        unit_two,
        inverse_two,
        normed_two,
        pre_gelu,
        activated,
        embedding,
        inverse_norm,
    )
    return (embedding, saved)


def backward(params, saved, grad_embedding, row_count):
    (
        gains,
        shifts,
        attend,
        attend_bias,
        output,
        output_bias,
        expand,
        expand_bias,
        contract,
        contract_bias,
    ) = params
    (
        normed_one,
        unit_one,
        inverse_one,
        queries,
        keys,
        values,
        attention,
        attention_low,
        context,
        unit_two,
        inverse_two,
        normed_two,
        pre_gelu,
        activated,
        embedding,
        inverse_norm,
    ) = saved
    examples, features = embedding.shape
    grad_pooled = inverse_norm * (
        grad_embedding - embedding * jnp.sum(grad_embedding * embedding, -1, keepdims=True)
    )
    grad_rows = jnp.broadcast_to(
        (grad_pooled / row_count)[:, None, :], (examples, row_count, features)
    ).reshape(examples * row_count, features)
    grad_mlp = grad_rows.astype(jnp.bfloat16)
    grad_contract = left_inner(activated, grad_mlp)
    grad_contract_bias = jnp.sum(grad_mlp.astype(jnp.float32), 0)
    grad_activated = right_inner(grad_mlp, contract)
    gelu_back = jax.vjp(jax.nn.gelu, pre_gelu)[1]
    grad_pre = gelu_back(grad_activated)[0].astype(jnp.bfloat16)
    grad_expand = left_inner(normed_two, grad_pre)
    grad_expand_bias = jnp.sum(grad_pre.astype(jnp.float32), 0)
    grad_normed_two = right_inner(grad_pre, expand)
    grad_middle, gain_two, shift_two = normalize_back(
        grad_normed_two, unit_two, inverse_two, gains[1].astype(jnp.float32)
    )
    grad_middle = grad_middle + grad_rows
    grad_branch = grad_middle.astype(jnp.bfloat16)
    grad_output = left_inner(context, grad_branch)
    grad_output_bias = jnp.sum(grad_branch.astype(jnp.float32), 0)
    grad_context = (
        right_inner(grad_branch, output)
        .astype(jnp.bfloat16)
        .reshape(examples, row_count, HEADS, HEAD_DIM)
    )
    grad_attention = jnp.einsum(
        "erhd,eshd->ehrs", grad_context, values, preferred_element_type=jnp.float32
    )
    grad_values = jnp.einsum(
        "ehrs,erhd->eshd", attention_low, grad_context, preferred_element_type=jnp.float32
    )
    grad_scores = (
        attention * (grad_attention - jnp.sum(grad_attention * attention, -1, keepdims=True))
    ).astype(jnp.bfloat16)
    grad_queries = jnp.einsum(
        "ehrs,eshd->erhd", grad_scores, keys, preferred_element_type=jnp.float32
    ) * HEAD_DIM ** (-0.5)
    grad_keys = jnp.einsum(
        "ehrs,erhd->eshd", grad_scores, queries, preferred_element_type=jnp.float32
    ) * HEAD_DIM ** (-0.5)
    grad_projected = (
        jnp.stack([grad_queries, grad_keys, grad_values], 2)
        .astype(jnp.bfloat16)
        .reshape(examples * row_count, 3 * features)
    )
    grad_attend = left_inner(normed_one, grad_projected)
    column_sums = jnp.sum(grad_projected.astype(jnp.float32), 0)
    grad_attend_bias = jnp.concatenate([column_sums[:features], column_sums[2 * features :]])
    grad_normed_one = right_inner(grad_projected, attend)
    grad_inputs, gain_one, shift_one = normalize_back(
        grad_normed_one, unit_one, inverse_one, gains[0].astype(jnp.float32)
    )
    grad_inputs = grad_inputs + grad_middle
    grads = (
        jnp.stack([gain_one, gain_two]),
        jnp.stack([shift_one, shift_two]),
        grad_attend,
        grad_attend_bias,
        grad_output,
        grad_output_bias,
        grad_expand,
        grad_expand_bias,
        grad_contract,
        grad_contract_bias,
    )
    return (grad_inputs.reshape(examples, row_count, features), grads)


def masked_softmax(logits, allowed, live_rows):
    filled = jnp.where(allowed, logits, -1e30)
    largest = jnp.max(filled, -1, keepdims=True)
    weights = jnp.exp(filled - largest) * allowed.astype(jnp.float32)
    safe_total = jnp.sum(weights, -1, keepdims=True) + (1.0 - live_rows)[:, None]
    return (weights / safe_total, largest[:, 0] + jnp.log(safe_total[:, 0]))


def plain_on_device(
    text_tokens,
    image_tokens,
    counts,
    caption_group,
    image_gains,
    image_shifts,
    image_attend,
    image_attend_bias,
    image_output,
    image_output_bias,
    image_expand,
    image_expand_bias,
    image_contract,
    image_contract_bias,
    text_gains,
    text_shifts,
    text_attend,
    text_attend_bias,
    text_output,
    text_output_bias,
    text_expand,
    text_expand_bias,
    text_contract,
    text_contract_bias,
):
    image_params = (
        image_gains,
        image_shifts,
        image_attend,
        image_attend_bias,
        image_output,
        image_output_bias,
        image_expand,
        image_expand_bias,
        image_contract,
        image_contract_bias,
    )
    text_params = (
        text_gains,
        text_shifts,
        text_attend,
        text_attend_bias,
        text_output,
        text_output_bias,
        text_expand,
        text_expand_bias,
        text_contract,
        text_contract_bias,
    )
    image_embedding, image_saved = plain_forward(image_tokens, image_params)
    text_embedding, text_saved = plain_forward(text_tokens, text_params)
    image_low = image_embedding.astype(jnp.bfloat16)
    text_low = text_embedding.astype(jnp.bfloat16)
    all_images, all_texts = (
        lax.all_gather(image_low, ("tower", "dp"), axis=0, tiled=True),
        lax.all_gather(text_low, ("tower", "dp"), axis=0, tiled=True),
    )
    per_device = image_low.shape[0]
    everyone = all_images.shape[0]
    device_rank = lax.axis_index(("tower", "dp"))
    positions = jnp.arange(everyone, dtype=jnp.int32)
    owned = device_rank * per_device + jnp.arange(per_device, dtype=jnp.int32)
    live_all = positions % per_device < jnp.repeat(counts, per_device, total_repeat_length=everyone)
    live_own = lax.dynamic_slice_in_dim(live_all, device_rank * per_device, per_device)
    group_own = lax.dynamic_slice_in_dim(caption_group, device_rank * per_device, per_device)
    diagonal = owned[:, None] == positions[None, :]
    allowed = (
        live_own[:, None]
        & live_all[None, :]
        & ((group_own[:, None] != caption_group[None, :]) | diagonal)
    )
    live_rows = live_own.astype(jnp.float32)
    diagonal_float = diagonal.astype(jnp.float32)
    forward_logits = right_inner(text_low, all_images) * LOGIT_SCALE
    backward_logits = right_inner(image_low, all_texts) * LOGIT_SCALE
    forward_probs, forward_lse = masked_softmax(forward_logits, allowed, live_rows)
    backward_probs, backward_lse = masked_softmax(backward_logits, allowed, live_rows)
    forward_terms = forward_lse - jnp.sum(forward_logits * diagonal_float, -1)
    backward_terms = backward_lse - jnp.sum(backward_logits * diagonal_float, -1)
    local_sum = 0.5 * (jnp.sum(live_rows * forward_terms) + jnp.sum(live_rows * backward_terms))
    loss_sum = lax.psum(local_sum, ("tower", "dp"))
    loss_value = loss_sum / jnp.sum(counts).astype(jnp.float32)
    forward_coef = (0.5 * live_rows[:, None] * (forward_probs - diagonal_float)).astype(
        jnp.bfloat16
    )
    grad_embedding = LOGIT_SCALE * multiply(forward_coef, all_images)
    lse_everyone = lax.all_gather(backward_lse, ("tower", "dp"), axis=0, tiled=True)
    shifted = jnp.where(allowed, forward_logits - lse_everyone[None, :], -1e30)
    live_columns = live_all.astype(jnp.float32)
    column_coef = (0.5 * live_columns[None, :] * (jnp.exp(shifted) - diagonal_float)).astype(
        jnp.bfloat16
    )
    grad_embedding = grad_embedding + LOGIT_SCALE * multiply(column_coef, all_images)
    text_grad, grads = backward(text_params, text_saved, grad_embedding, text_tokens.shape[1])
    shards = (
        lax.psum_scatter(grads[0], "dp", scatter_dimension=1, tiled=True),
        lax.psum_scatter(grads[1], "dp", scatter_dimension=1, tiled=True),
        lax.psum_scatter(grads[2], "dp", scatter_dimension=0, tiled=True),
        lax.psum_scatter(grads[3], "dp", scatter_dimension=0, tiled=True),
        lax.psum_scatter(grads[4], "dp", scatter_dimension=0, tiled=True),
        lax.psum_scatter(grads[5], "dp", scatter_dimension=0, tiled=True),
        lax.psum_scatter(grads[6], "dp", scatter_dimension=1, tiled=True),
        lax.psum_scatter(grads[7], "dp", scatter_dimension=0, tiled=True),
        lax.psum_scatter(grads[8], "dp", scatter_dimension=0, tiled=True),
        lax.psum_scatter(grads[9], "dp", scatter_dimension=0, tiled=True),
    )
    totals = (
        lax.psum(shards[0].astype(jnp.bfloat16), "tower").astype(jnp.float32),
        lax.psum(shards[1].astype(jnp.bfloat16), "tower").astype(jnp.float32),
        lax.psum(shards[2].astype(jnp.bfloat16), "tower").astype(jnp.float32),
        lax.psum(shards[3].astype(jnp.bfloat16), "tower").astype(jnp.float32),
        lax.psum(shards[4].astype(jnp.bfloat16), "tower").astype(jnp.float32),
        lax.psum(shards[5].astype(jnp.bfloat16), "tower").astype(jnp.float32),
        lax.psum(shards[6].astype(jnp.bfloat16), "tower").astype(jnp.float32),
        lax.psum(shards[7].astype(jnp.bfloat16), "tower").astype(jnp.float32),
        lax.psum(shards[8].astype(jnp.bfloat16), "tower").astype(jnp.float32),
        lax.psum(shards[9].astype(jnp.bfloat16), "tower").astype(jnp.float32),
    )
    return (
        loss_value,
        text_grad,
        totals[0],
        totals[1],
        totals[2],
        totals[3],
        totals[4],
        totals[5],
        totals[6],
        totals[7],
        totals[8],
        totals[9],
    )


def solution(mesh):
    n = mesh.shape["dp"]
    whole, both = P(), P(("tower", "dp"), None, None)
    fits = FF // n * 4 == D and n % 8 == 0
    body = functools.partial(on_device, n) if fits else plain_on_device
    out_specs = (P(), both, P(None, "dp"), P(None, "dp"), P("dp", None), P("dp"), P("dp", None), P("dp"), P(None, "dp"), P("dp"), P("dp", None), P("dp"))
    return jax.shard_map(body, mesh=mesh, in_specs=(both, both) + (whole,) * 22, out_specs=out_specs, check_vma=False)
```

```python
import functools
import jax
import jax.numpy as jnp
import numpy as np
from jax import lax
from jax.experimental import pallas as pl
from jax.experimental.pallas import tpu as pltpu
from jax.sharding import PartitionSpec as P

F32, BF16 = jnp.float32, jnp.bfloat16
D, HD, FF = 768, 64, 3072
PAIRS = D // (2 * HD)
KW = 128
NORM_EPS, EMBED_EPS, LOGIT_SCALE = 1e-5, 1e-6, 64.0
NEG = -1e30
ANY = pl.BlockSpec(memory_space=pl.ANY)
VM = pl.BlockSpec(memory_space=pltpu.VMEM)
PLAN = ((0, 8), (16, 4), (24, 4))
GELU_C, GELU_A = float(np.sqrt(2 / np.pi)), 0.044715


def dot(a, b):
    return jnp.dot(a, b, preferred_element_type=F32)


def dot_t(a, b):
    return lax.dot_general(a, b, (((1,), (1,)), ((), ())), preferred_element_type=F32)


def t_dot(a, b):
    return lax.dot_general(a, b, (((0,), (0,)), ((), ())), preferred_element_type=F32)


def unit_rows(v):
    centre = v - jnp.mean(v, -1, keepdims=True)
    inv = lax.rsqrt(jnp.mean(centre * centre, -1, keepdims=True) + NORM_EPS)
    return centre * inv, inv


def head_masks():
    lane = lax.broadcasted_iota(jnp.int32, (1, 2 * HD), 1)
    even = (lane < HD).astype(F32)
    return even.astype(BF16), (1.0 - even).astype(BF16)


def pair_mask(rows, per, real):
    r = lax.broadcasted_iota(jnp.int32, (rows, 2 * KW), 0)
    c = lax.broadcasted_iota(jnp.int32, (rows, 2 * KW), 1) % KW
    ok = (r // per == c // per) & (c % per < real) & (c < rows)
    return jnp.where(ok, 0.0, NEG).astype(F32)


def split_heads(a, even, odd):
    return jnp.concatenate([a * even, a * odd], axis=0)


def softmax_half(s):
    m = jnp.max(s, -1, keepdims=True)
    p = jnp.exp(s - m)
    return p / jnp.sum(p, -1, keepdims=True)


def exp_half(s):
    return jnp.exp(s - jnp.max(s, -1, keepdims=True)).astype(BF16)


def block_forward(x, rows, groups, small, W, wait, done, proj, ctx, mask, att_out, keep):
    attend, output, expand, contract = W
    unit, _ = unit_rows(x)
    n1 = (unit * small[0:1, :] + small[2:3, :]).astype(BF16)
    keep("n1", n1)
    wait("attend")
    M = rows * groups
    step = 256
    for c in range(3 * D // step):
        y = dot(n1, attend[:, c * step:(c + 1) * step])
        if c * step < D:
            y = y + small[4:5, c * step:(c + 1) * step]
        elif c * step >= 2 * D:
            y = y + small[5:6, c * step - 2 * D:(c + 1) * step - 2 * D]
        proj[0:M, c * step:(c + 1) * step] = y.astype(BF16)
    done("attend")
    keep("proj", None)
    even, odd = head_masks()
    ones = split_heads(jnp.ones((KW, 2 * HD), BF16), even, odd)

    def group(g, _):
        r0 = pl.multiple_of(g * rows, 16)
        for j in range(PAIRS):
            lanes = slice(j * 2 * HD, (j + 1) * 2 * HD)
            q = proj[pl.ds(r0, rows), j * 128:(j + 1) * 128]
            kk = split_heads(proj[pl.ds(r0, KW), D + j * 128:D + (j + 1) * 128], even, odd)
            vv = split_heads(proj[pl.ds(r0, KW), 2 * D + j * 128:2 * D + (j + 1) * 128], even, odd)
            s = dot_t(q, kk) * HD ** -0.5 + mask[...]
            if att_out is None:
                p = jnp.concatenate([exp_half(s[:, :KW]), exp_half(s[:, KW:])], axis=1)
                both = dot(p, jnp.concatenate([vv, ones], axis=1))
                ctx[pl.ds(r0, rows), lanes] = (both[:, :128] / both[:, 128:]).astype(BF16)
            else:
                a = jnp.concatenate([softmax_half(s[:, :KW]), softmax_half(s[:, KW:])], axis=1)
                att_out[g * PAIRS + j] = a
                ctx[pl.ds(r0, rows), lanes] = dot(a.astype(BF16), vv).astype(BF16)
        return 0

    lax.fori_loop(0, groups, group, 0)
    wait("output")
    middle = x + (dot(ctx[0:M, :], output[...]) + small[6:7, :])
    done("output")
    keep("middle", middle)
    unit, _ = unit_rows(middle)
    n2 = (unit * small[1:2, :] + small[3:4, :]).astype(BF16)
    keep("n2", n2)
    wait("expand")
    acc = middle + small[11:12, :]
    step = 768
    for c in range(FF // step):
        pre = dot(n2, expand[:, c * step:(c + 1) * step]) + small[7 + c:8 + c, :]
        sq = pre * pre
        th = jnp.tanh(pre * (GELU_C + GELU_C * GELU_A * sq))
        cdf = 0.5 + 0.5 * th
        act = (pre * cdf).astype(BF16)
        keep("act", act, c, pre, sq, th, cdf)
        if c == 0:
            wait("contract")
        acc = acc + dot(act, contract[c * step:(c + 1) * step, :])
    done("expand")
    done("contract")
    return acc


def embed_rows(pooled):
    inv = lax.rsqrt(jnp.sum(pooled * pooled, -1, keepdims=True) + EMBED_EPS)
    return pooled * inv, inv


def wide_of(n_dp):
    return -(-(FF // n_dp + 1) // 128) * 128


MESH_ID = pl.DeviceIdType.MESH


def place():
    return lax.axis_index("tower"), lax.axis_index("dp")


def greet(n):
    t, d = place()
    barrier = pltpu.get_barrier_semaphore()

    def one(k, _):
        who = (lax.rem(t + k // n, 2), lax.rem(d + lax.rem(k, n), n))
        pl.semaphore_signal(barrier, inc=1, device_id=who, device_id_type=MESH_ID)
        return 0

    lax.fori_loop(1, 2 * n, one, 0)


def spread(n, src, dst, send, recv):
    t, d = place()

    def one(k, _):
        pltpu.make_async_remote_copy(src_ref=src, dst_ref=dst.at[d], send_sem=send, recv_sem=recv,
                                     device_id=(t, lax.rem(d + k, n)), device_id_type=MESH_ID).start()
        return 0

    lax.fori_loop(1, n, one, 0)


def settle(n, dst, send, recv):
    part = dst.at[pl.ds(0, n - 1)]
    pltpu.make_async_copy(part, part, send).wait()
    pltpu.make_async_copy(part, part, recv).wait()


def contrast_rows(fl, allowed, live_rows):
    filled = jnp.where(allowed, fl, NEG)
    largest = jnp.max(filled, -1, keepdims=True)
    weights = jnp.where(allowed, jnp.exp(filled - largest), 0.0)
    total = jnp.sum(weights, -1, keepdims=True) + (1.0 - live_rows)
    return weights / total, largest + jnp.log(total)


def contrast_rows(fl, allowed, live_rows):
    filled = jnp.where(allowed, fl, NEG)
    largest = jnp.max(filled, -1, keepdims=True)
    weights = jnp.where(allowed, jnp.exp(filled - largest), 0.0)
    total = jnp.sum(weights, -1, keepdims=True) + (1.0 - live_rows)
    return weights / total, largest + jnp.log(total)


def fill_small(small, refs):
    gains, shifts, attend_bias, output_bias, expand_bias, contract_bias = refs
    small[0:2, :] = gains[...].astype(F32)
    small[2:4, :] = shifts[...].astype(F32)
    row = 4
    for ref in (attend_bias, output_bias, expand_bias, contract_bias):
        for k in range(ref.shape[0] // D):
            small[row:row + 1, :] = ref[pl.ds(k * D, D)].astype(F32).reshape(1, D)
            row += 1


def front_kernel(per_text, real, plan, n, *refs):
    it = iter(refs)
    take = lambda k: [next(it) for _ in range(k)]
    x_ref, counts_ref, group_ref, group2_ref = take(4)
    image_small, text_small = take(6), take(6)
    image_w, text_w = take(4), take(4)
    tokens_h, = take(1)
    g_ref, grow_ref, loss_ref, ag_ref = take(4)
    saved_h = take(7)
    weights = take(4)
    saved = take(7)
    tokens, xs, proj_i, ctx_i, mask_t, mask_i, small_t, small_i = take(8)
    lows_t, asum, emb_ref, own_rows, lse, = take(5)
    lows_i = take(len(plan))
    load, out_sem, tok_sem, ssem, rsem, osem_s, osem_r = take(7)
    t, d = place()
    greet(n)
    names = ("attend", "output", "expand", "contract")
    copies = {}
    for k, name in enumerate(names):
        copies["text", name] = pltpu.make_async_copy(text_w[k], weights[k], load.at[k])
        copies["text", name].start()
        copies["image", name] = pltpu.make_async_copy(image_w[k], weights[k], load.at[4 + k])
    token_copy = pltpu.make_async_copy(tokens_h, tokens, tok_sem)
    token_copy.start()
    n1, proj, att, ctx, mid, n2, gp = saved
    outs = dict(zip(("n1", "proj", "att", "ctx", "mid", "n2", "gp"), [pltpu.make_async_copy(v, h, out_sem.at[k]) for k, (v, h) in enumerate(zip(saved, saved_h))]))
    fill_small(small_t, text_small)
    fill_small(small_i, image_small)
    M = x_ref.shape[0]
    ex = M // per_text
    mask_t[...] = pair_mask(KW, per_text, per_text)
    shard, wide = FF // n, asum.shape[2]
    for k in range(n):
        asum[k, :, shard:] = jnp.full((ex, wide - shard), per_text, BF16)

    def keep(name, value, *extra):
        if name == "n1":
            n1[...] = value
            outs["n1"].start()
        elif name == "proj":
            outs["proj"].start()
        elif name == "middle":
            mid[...] = value
            for o in ("att", "ctx", "mid"):
                outs[o].start()
        elif name == "n2":
            n2[...] = value
            outs["n2"].start()
        else:
            c, pre, sq, th, cdf = extra
            w = value.shape[1]
            total = jnp.sum(value.astype(F32).reshape(ex, per_text, w), 1).astype(BF16)
            for k in range(c * w // shard, (c + 1) * w // shard):
                asum[k, :, 0:shard] = total[:, k * shard - c * w:(k + 1) * shard - c * w]
            gp[:, c * w:(c + 1) * w] = (cdf + (0.5 * GELU_C) * pre * (1.0 - th * th) * (1.0 + (3 * GELU_A) * sq)).astype(BF16)

    out = block_forward(x_ref[...].astype(F32), KW, M // KW, small_t, weights, lambda name: copies["text", name].wait(), lambda name: copies["image", name].start(),
                        proj, ctx, mask_t, att, keep)
    outs["gp"].start()
    emb, inv = embed_rows(jnp.sum(out.reshape(ex, per_text, D), 1) * (1.0 / per_text))
    emb_ref[0] = emb
    emb_ref[1] = jnp.broadcast_to(inv, emb.shape)
    lows_t[t, d] = emb.astype(BF16)

    def send(src, dst, s, r, who):
        return pltpu.make_async_remote_copy(src_ref=src, dst_ref=dst, send_sem=s, recv_sem=r, device_id=who, device_id_type=MESH_ID)

    pl.semaphore_wait(pltpu.get_barrier_semaphore(), 2 * n - 1)
    spread(n, lows_t.at[t, d], lows_t.at[t], ssem.at[0], rsem.at[0])

    def one(k, _):
        to = lax.rem(d + k, n)
        send(asum.at[to], ag_ref.at[d], ssem.at[1], rsem.at[1], (t, to)).start()
        return 0

    lax.fori_loop(1, n, one, 0)
    ag_ref[d] = asum[d]

    def pass_over(buf, k):
        return send(buf.at[t], buf.at[t], osem_s.at[k], osem_r.at[k], (1 - t, d))

    per = -(-real // 8) * 8
    rows = 2 * per
    xs[...] = jnp.zeros_like(xs)
    proj_i[proj_i.shape[0] - 16:, :] = jnp.zeros((16, 3 * D), BF16)
    mask_i[...] = pair_mask(rows, per, real)
    bufs = [lows_t] + lows_i
    slots = [0] + [2 + k for k in range(len(plan))]

    def arrive(k):
        settle(n, bufs[k].at[t], ssem.at[slots[k]], rsem.at[slots[k]])
        pass_over(bufs[k], k).start()

    for k, (first, pairs) in enumerate(plan):
        def wait(name):
            if k == 0:
                copies["image", name].wait()
        if k == 0:
            token_copy.wait()
        rows_k, ex_k = rows * pairs, 2 * pairs
        for e in range(ex_k):
            xs[e * per:e * per + real, :] = tokens[first + e].astype(F32)
        out = block_forward(xs[0:rows_k, :], rows, pairs, small_i, weights, wait, lambda name: None, proj_i, ctx_i, mask_i, None, lambda *a: None)
        out = out.reshape(ex_k, per, D)
        ok = lax.broadcasted_iota(jnp.int32, (ex_k, per, D), 1) < real
        emb, _ = embed_rows(jnp.sum(jnp.where(ok, out, 0.0), 1) * (1.0 / real))
        lows_i[k][t, d] = emb.astype(BF16)
        spread(n, lows_i[k].at[t, d], lows_i[k].at[t], ssem.at[slots[k + 1]], rsem.at[slots[k + 1]])
        arrive(k)
        if k > 0:
            pass_over(bufs[k - 1], k - 1).wait()

    every, nd = 2 * n * ex, 2 * n
    rank = t * n + d
    counts_row = jnp.broadcast_to(counts_ref[...].astype(F32).reshape(1, nd), (8, nd)).astype(BF16)

    def live_of(device, row):
        hot = (lax.broadcasted_iota(jnp.int32, (nd, device.shape[1]), 0) == device).astype(F32).astype(BF16)
        return (row.astype(F32) < dot(counts_row, hot)[0:1, :]).astype(F32), hot

    natural = lax.broadcasted_iota(jnp.int32, (1, every), 1)
    group_row = group_ref[...].astype(F32).reshape(1, every)
    live_row, _ = live_of(natural // ex, natural % ex)
    text_group = jnp.transpose(jnp.broadcast_to(group_row, (128, every)))[:, 0:1]
    text_live = jnp.transpose(jnp.broadcast_to(live_row, (128, every)))[:, 0:1]
    own_text = lows_t[t, d]
    groups, lives, places = [], [], []
    at = 0
    for k, (first, pairs) in enumerate(plan):
        ek = 2 * pairs
        w = nd * ek
        col = lax.broadcasted_iota(jnp.int32, (1, w), 1)
        device, row = col // ek, first + col % ek
        live, hot = live_of(device, row)
        by_row = lax.dot_general(group2_ref[...].astype(F32).astype(BF16), hot, (((0,), (0,)), ((), ())), preferred_element_type=F32)
        groups.append(jnp.sum(jnp.where(lax.broadcasted_iota(jnp.int32, (ex, w), 0) == row, by_row, 0.0), 0, keepdims=True))
        lives.append(live)
        places.append(device * ex + row)
    texts = lows_t[...].reshape(every, D)

    def chunk_logits(k, at):
        w = nd * 2 * plan[k][1]
        images = lows_i[k][...].reshape(w, D)
        own_rows[:, at:at + w] = dot_t(own_text, images) * LOGIT_SCALE
        for lo in range(0, w, 256):
            part = slice(lo, min(lo + 256, w))
            logits = dot_t(texts, images[part]) * LOGIT_SCALE
            same = lax.broadcasted_iota(jnp.int32, logits.shape, 0) == places[k][:, part]
            allowed = (text_live * lives[k][:, part] > 0.0) & ((text_group != groups[k][:, part]) | same)
            filled = jnp.where(allowed, logits, NEG)
            largest = jnp.max(filled, 0, keepdims=True)
            total = jnp.sum(jnp.where(allowed, jnp.exp(filled - largest), 0.0), 0, keepdims=True) + (1.0 - lives[k][:, part])
            lse[:, at + lo:at + lo + logits.shape[1]] = jnp.broadcast_to(largest + jnp.log(total), (8, logits.shape[1]))
        return at + w

    for k in range(len(plan)):
        if k == len(plan) - 1:
            arrive(k + 1)
            pass_over(bufs[k + 1], k + 1).wait()
        elif k == len(plan) - 2:
            pass_over(bufs[k + 1], k + 1).wait()
        at = chunk_logits(k, at)
    column_group, column_live, column_place = (jnp.concatenate(v, 1) for v in (groups, lives, places))
    diag_b = column_place == lax.broadcasted_iota(jnp.int32, (ex, every), 0) + rank * ex
    diagonal = diag_b.astype(F32)
    image_lse = lse[0:1, :]
    fl = own_rows[...]
    live_own = jnp.sum(diagonal * column_live, -1, keepdims=True)
    group_own = jnp.sum(diagonal * column_group, -1, keepdims=True)
    allowed = (live_own * column_live > 0.0) & ((group_own != column_group) | diag_b)
    probs, text_lse = contrast_rows(fl, allowed, live_own)
    own_diag = fl * diagonal
    terms = live_own * (text_lse - jnp.sum(own_diag, -1, keepdims=True)) + jnp.sum(diagonal * (live_own * image_lse) - live_own * own_diag, -1, keepdims=True)
    loss_ref[...] = jnp.broadcast_to(0.5 * jnp.sum(terms, 0, keepdims=True), loss_ref.shape)
    forward_coef = (0.5 * live_own * (probs - diagonal)).astype(BF16)
    shifted = jnp.where(allowed, jnp.exp(jnp.where(allowed, fl - image_lse, NEG)), 0.0)
    column_coef = (0.5 * column_live * (shifted - diagonal)).astype(BF16)
    coefs = jnp.concatenate([forward_coef, column_coef], 0)
    at, grad = 0, None
    for k, (first, pairs) in enumerate(plan):
        w = nd * 2 * pairs
        part = dot(coefs[:, at:at + w], lows_i[k][...].reshape(w, D))
        grad = part if grad is None else grad + part
        at += w
    grad = LOGIT_SCALE * grad[0:ex] + LOGIT_SCALE * grad[ex:]
    emb = emb_ref[0]
    pooled = emb_ref[1] * (grad - emb * jnp.sum(grad * emb, -1, keepdims=True))
    rows_out = pooled * (1.0 / per_text)
    grow_ref[...] = rows_out
    g_ref[...] = rows_out.astype(BF16)
    settle(n, ag_ref, ssem.at[1], rsem.at[1])
    for o in outs.values():
        o.wait()


def front(n, text_tokens, image_tokens, counts, group, image_params, text_params, plan):
    ex, per, _ = text_tokens.shape
    real = image_tokens.shape[1]
    M = ex * per
    wide = wide_of(n)
    S = jax.ShapeDtypeStruct
    small_of = lambda p: [p[0], p[1], p[3], p[5], p[7], p[9]]
    weights_of = lambda p: [p[2], p[4], p[6], p[8]]
    kept = [S((M, D), BF16), S((M, 3 * D), BF16), S((M // KW * PAIRS, KW, 2 * KW), F32), S((M, D), BF16), S((M, D), F32), S((M, D), BF16), S((M, FF), BF16)]
    like = lambda a: pltpu.VMEM(a.shape, a.dtype)
    per_i = -(-real // 8) * 8
    big = max(p for _, p in plan) * 2 * per_i
    scratch = [like(a) for a in weights_of(text_params)] + [like(a) for a in kept]
    scratch += [like(image_tokens), pltpu.VMEM((big, D), F32), pltpu.VMEM((big + 16, 3 * D), BF16), pltpu.VMEM((big, D), BF16),
                pltpu.VMEM((KW, 2 * KW), F32), pltpu.VMEM((2 * per_i, 2 * KW), F32), pltpu.VMEM((16, D), F32), pltpu.VMEM((16, D), F32)]
    scratch += [pltpu.VMEM((2, n, ex, D), BF16), pltpu.VMEM((n, ex, wide), BF16), pltpu.VMEM((2, ex, D), F32), pltpu.VMEM((ex, 2 * n * ex), F32), pltpu.VMEM((8, 2 * n * ex), F32)]
    scratch += [pltpu.VMEM((2, n, 2 * p, D), BF16) for _, p in plan]
    dma = pltpu.SemaphoreType.DMA
    k = len(plan)
    scratch += [dma((8,)), dma((7,)), dma, dma((k + 2,)), dma((k + 2,)), dma((k + 1,)), dma((k + 1,))]
    return pl.pallas_call(
        functools.partial(front_kernel, per, real, plan, n),
        out_shape=[S((ex, D), BF16), S((ex, D), F32), S((8, 128), F32), S((n, ex, wide), BF16)] + kept,
        in_specs=[VM] * 16 + [ANY] * 9, out_specs=[VM] * 4 + [ANY] * 7, scratch_shapes=scratch,
        compiler_params=pltpu.CompilerParams(collective_id=0, has_side_effects=True, vmem_limit_bytes=63 << 20),
        name="forward_and_loss",
    )(text_tokens.reshape(M, D), counts, group, group.reshape(2 * n, ex), *small_of(image_params), *small_of(text_params), *weights_of(image_params), *weights_of(text_params), image_tokens)


def norm_back(grad, unit, inv, gain):
    gu = grad * gain
    out = inv * (gu - jnp.mean(gu, -1, keepdims=True) - unit * jnp.mean(gu * unit, -1, keepdims=True))
    return out, jnp.sum(grad * unit, 0, keepdims=True), jnp.sum(grad, 0, keepdims=True)


def back_kernel(per, n, small, g_ref, grow_ref, ag_ref, loss_ref, x_h, n1_h, proj_h, att_h, ctx_h, mid_h, n2_h, gp_h, contract_h, expand_h, output_h, attend_h,
                tg_ref, oe_ref, oa_ref, oo_ref, os_ref, oc_ref, ol_ref,
                xb, n1, proj, att, ctx, mid, n2, gp, contract, expand, output, attend, gctx, gproj, rowsums,
                grads, core_in, in1, in2, red, zin_e, zin_a, fin_e, fin_a, s_out, s_in, s_fin, gall, pc, pc_in, lossall,
                load, csem_s, csem_r, sem1_s, sem1_r, sem2_s, sem2_r, zsem_s, zsem_r, fsem_s, fsem_r, gsem, lsem, ssem):
    t, d = place()
    dx, dy, dz, nz = lax.rem(d, 2), lax.rem(d // 2, 2), d // 4, n // 4
    other = (1 - t, d)
    partner = ((t, d + 1 - 2 * dx), (t, d + 2 - 4 * dy))
    greet(n)
    copies = {}
    for k, (name, h, v) in enumerate((("contract", contract_h, contract), ("gp", gp_h, gp), ("n2", n2_h, n2), ("expand", expand_h, expand), ("mid", mid_h, mid), ("ctx", ctx_h, ctx),
                                      ("output", output_h, output), ("proj", proj_h, proj), ("att", att_h, att), ("n1", n1_h, n1), ("attend", attend_h, attend), ("x", x_h, xb))):
        copies[name] = pltpu.make_async_copy(h, v, load.at[k])
        copies[name].start()
    M = xb.shape[0]
    ex = M // per
    rows_e, rows_a, H = FF // n, D // n, D // 2
    B = D // 2
    Q, E8 = B // 4, B // 2

    def remote(src, dst, ss, rs, who):
        return pltpu.make_async_remote_copy(src_ref=src, dst_ref=dst, send_sem=ss, recv_sem=rs, device_id=who, device_id_type=MESH_ID)

    def core_copy(q):
        return remote(grads.at[q, 1 - t], core_in.at[q], csem_s.at[q], csem_r.at[q], other)

    def first_copy(q, b):
        away = pl.multiple_of(b * B + (1 - (dx, dy)[b]) * E8, 16)
        return remote(grads.at[q, t, pl.ds(away, E8)], in1.at[q, b], sem1_s.at[q, b], sem1_r.at[q, b], partner[b])

    def second_copy(q, b):
        away = pl.multiple_of(b * B + (dx, dy)[b] * E8 + (1 - (dy, dx)[b]) * Q, 16)
        return remote(grads.at[q, t, pl.ds(away, Q)], in2.at[q, b], sem2_s.at[q, b], sem2_r.at[q, b], partner[1 - b])

    def step0(q):
        core_copy(q).start()

    def step1(q):
        core_copy(q).wait()
        grads[q, t] = (grads[q, t].astype(F32) + core_in[q].astype(F32)).astype(BF16)
        for b in range(2):
            first_copy(q, b).start()

    def step2(q):
        for b in range(2):
            first_copy(q, b).wait()
            keep = pl.multiple_of(b * B + (dx, dy)[b] * E8, 16)
            grads[q, t, pl.ds(keep, E8)] = (grads[q, t, pl.ds(keep, E8)].astype(F32) + in1[q, b].astype(F32)).astype(BF16)
            second_copy(q, b).start()

    def step3(q):
        for b in range(2):
            second_copy(q, b).wait()
            keep = pl.multiple_of(b * B + (dx, dy)[b] * E8 + (dy, dx)[b] * Q, 16)
            red[q, b * Q:(b + 1) * Q] = (grads[q, t, pl.ds(keep, Q)].astype(F32) + in2[q, b].astype(F32)).astype(BF16)

    def over_z(k):
        to = lax.rem(dz + k, nz)
        return to, (t, to * 4 + lax.rem(d, 4))

    def z_expand():
        for k in range(1, nz):
            to, who = over_z(k)
            remote(red.at[to], zin_e.at[dz], zsem_s.at[nz], zsem_r.at[nz], who).start()
        zin_e[dz] = red[dz]

    def z_attend(a):
        for k in range(1, nz):
            to, who = over_z(k)
            remote(red.at[nz + a, pl.ds(pl.multiple_of(to * rows_a, 16), rows_a)], zin_a.at[a, dz], zsem_s.at[a], zsem_r.at[a], who).start()
        zin_a[a, dz] = red[nz + a, pl.ds(pl.multiple_of(dz * rows_a, 16), rows_a)]

    def all_but_one(ref, count, ss, rs):
        part = ref.at[pl.ds(0, count)]
        pltpu.make_async_copy(part, part, ss).wait()
        pltpu.make_async_copy(part, part, rs).wait()

    def fin_copy(k):
        ref = fin_e if k == 4 else fin_a.at[k]
        return remote(ref.at[t], ref.at[t], fsem_s.at[k], fsem_r.at[k], other)

    def last_expand():
        all_but_one(zin_e, nz - 1, zsem_s.at[nz], zsem_r.at[nz])
        fin_e[t] = jnp.sum(zin_e[...].astype(F32), 0).astype(BF16)
        fin_copy(4).start()

    def last_attend(a):
        all_but_one(zin_a.at[a], nz - 1, zsem_s.at[a], zsem_r.at[a])
        fin_a[a, t] = jnp.sum(zin_a[a].astype(F32), 0).astype(BF16)
        fin_copy(a).start()

    def put_rows(q, value, lanes):
        for s in range(n):
            z, y, x = s // 4, s // 2 % 2, s % 2
            p = (2 * x + y) * Q + z * rows_a if z < nz // 2 else B + (2 * y + x) * Q + (z - nz // 2) * rows_a
            for h in range(2):
                for src, dst, w in lanes(h):
                    grads[q, h, p:p + rows_a, dst:dst + w] = value[s * rows_a:(s + 1) * rows_a, src:src + w]

    g_low = g_ref[...]
    step = FF // nz
    gn2 = None
    for c in range(nz):
        cols = slice(c * step, (c + 1) * step)
        if c == 0:
            copies["contract"].wait()
        ga = dot_t(g_low, contract[cols, :])
        if c == 0:
            copies["gp"].wait()
            copies["n2"].wait()
        pre = (ga[:, None, :] * gp[:, cols].astype(F32).reshape(ex, per, step)).reshape(M, step).astype(BF16)
        rowsums[8 + c:9 + c, :] = jnp.sum(pre.astype(F32), 0, keepdims=True)
        ge = t_dot(pre, n2[...]).astype(BF16)
        for y in range(2):
            for x in range(2):
                at = (2 * y + x) * rows_e
                for h in range(2):
                    grads[c, h, (2 * x + y) * Q:(2 * x + y + 1) * Q, :] = ge[at:at + Q, h * H:(h + 1) * H]
                    grads[c, h, B + (2 * y + x) * Q:B + (2 * y + x + 1) * Q, :] = ge[at + Q:at + 2 * Q, h * H:(h + 1) * H]
        if c == 0:
            pl.semaphore_wait(pltpu.get_barrier_semaphore(), 2 * n - 1)
        step0(c)
        if c == 0:
            spread(n, g_ref, gall, gsem.at[0], gsem.at[1])
            copies["expand"].wait()
        part = dot_t(pre, expand[:, cols])
        gn2 = part if gn2 is None else gn2 + part
        if c >= 1:
            step1(c - 1)
        if c >= 2:
            step2(c - 2)
    gall[d] = g_ref[...]
    copies["mid"].wait()
    unit, inv = unit_rows(mid[...])
    gm, gain_two, shift_two = norm_back(gn2, unit, inv, small[1:2, :].astype(F32))
    rowsums[1:2, :] = gain_two
    rowsums[3:4, :] = shift_two
    gm = (gm.reshape(ex, per, D) + grow_ref[...][:, None, :]).reshape(M, D)
    tg_ref[...] = gm
    gb = gm.astype(BF16)
    rowsums[12:13, :] = jnp.sum(gb.astype(F32), 0, keepdims=True)
    step1(nz - 1)
    copies["ctx"].wait()
    put_rows(nz, t_dot(ctx[...], gb).astype(BF16), lambda h: [(h * H, 0, H)])
    step0(nz)
    step2(nz - 2)
    copies["output"].wait()
    gctx[...] = dot_t(gb, output[...]).astype(BF16)
    even, odd = head_masks()
    lane = lax.broadcasted_iota(jnp.int32, (KW, 2 * HD), 1)
    copies["proj"].wait()
    copies["att"].wait()

    for third in range(3):
        def group(i, _):
            r0 = pl.multiple_of(i * KW, KW)
            for j in (2 * third, 2 * third + 1):
                L = slice(j * 128, (j + 1) * 128)
                gc = gctx[pl.ds(r0, KW), L]
                q = proj[pl.ds(r0, KW), j * 128:(j + 1) * 128]
                kk = split_heads(proj[pl.ds(r0, KW), D + j * 128:D + (j + 1) * 128], even, odd)
                vv = split_heads(proj[pl.ds(r0, KW), 2 * D + j * 128:2 * D + (j + 1) * 128], even, odd)
                a = att[i * PAIRS + j]
                gatt = dot_t(gc, vv)
                prod = gatt * a
                gs = jnp.concatenate([a[:, h * KW:(h + 1) * KW] * (gatt[:, h * KW:(h + 1) * KW] - jnp.sum(prod[:, h * KW:(h + 1) * KW], -1, keepdims=True)) for h in range(2)], axis=1).astype(BF16)
                gv = t_dot(a.astype(BF16), gc)
                gk = t_dot(gs, q) * HD ** -0.5
                gproj[pl.ds(r0, KW), j * 128:(j + 1) * 128] = (dot(gs, kk) * HD ** -0.5).astype(BF16)
                gproj[pl.ds(r0, KW), D + j * 128:D + (j + 1) * 128] = jnp.where(lane < HD, gk[:KW], gk[KW:]).astype(BF16)
                gproj[pl.ds(r0, KW), 2 * D + j * 128:2 * D + (j + 1) * 128] = jnp.where(lane < HD, gv[:KW], gv[KW:]).astype(BF16)
            return 0

        lax.fori_loop(0, M // KW, group, 0)
        if third == 0:
            step1(nz)
            copies["n1"].wait()
        wide3 = jnp.concatenate([gproj[:, part * D + 256 * third:part * D + 256 * (third + 1)] for part in range(3)], axis=1)
        put_rows(nz + 1 + third, t_dot(n1[...], wide3).astype(BF16), lambda h: [(256 * part + 128 * h, 128 * part, 128) for part in range(3)])
        step0(nz + 1 + third)
        if third == 0:
            step2(nz - 1)
            for c in range(nz - 2):
                step3(c)
        elif third == 1:
            step1(nz + 1)
            step2(nz)
            step3(nz - 2)
        else:
            step3(nz - 1)
            z_expand()
            step1(nz + 2)
            step2(nz + 1)
            step3(nz)
            z_attend(0)
    rowsums[4:5, :] = jnp.sum(gproj[:, 0:D].astype(F32), 0, keepdims=True)
    rowsums[5:6, :] = rowsums[4:5, :]
    rowsums[6:7, :] = jnp.sum(gproj[:, 2 * D:3 * D].astype(F32), 0, keepdims=True)
    rowsums[7:8, :] = rowsums[6:7, :]
    step1(nz + 3)
    copies["attend"].wait()
    gn1 = dot_t(gproj[...], attend[...])
    step2(nz + 2)
    copies["x"].wait()
    unit, inv = unit_rows(xb[...].astype(F32))
    gx, gain_one, shift_one = norm_back(gn1, unit, inv, small[0:1, :].astype(F32))
    tg_ref[...] += gx
    rowsums[0:1, :] = gain_one
    rowsums[2:3, :] = shift_one
    sums = rowsums[...]
    parts = [sums[0:8, :]] + [jnp.broadcast_to(sums[8 + r:9 + r, :], (4, D)) for r in range(4)] + [sums[12:13, :], jnp.zeros((128 - 25, D), F32)]
    cols = jnp.transpose(jnp.concatenate(parts, 0))
    at = lax.broadcasted_iota(jnp.int32, (rows_a, 128), 1)
    for s in range(n):
        piece = jnp.where((at < 4) | (at == 24), cols[s * rows_a:(s + 1) * rows_a, :], 0.0)
        r0, first = 2 * s * rows_a % D, 2 * s * rows_a // D * 2
        for c in range(2):
            piece = jnp.where(at == 4 + first + c, cols[r0 + c * rows_a:r0 + (c + 1) * rows_a, :], piece)
        r0, first = 4 * s * rows_a % D, 4 * s * rows_a // D * 4
        for c in range(4):
            piece = jnp.where(at == 8 + first + c, cols[r0 + c * rows_a:r0 + (c + 1) * rows_a, :], piece)
        s_out[s] = piece.astype(BF16)

    def small_send(k, _):
        to = lax.rem(d + k, n)
        remote(s_out.at[to], s_in.at[d], ssem.at[0], ssem.at[1], (t, to)).start()
        return 0

    lax.fori_loop(1, n, small_send, 0)
    s_in[d] = s_out[d]

    def tell(k, _):
        who = (lax.rem(t + k // n, 2), lax.rem(d + lax.rem(k, n), n))
        remote(loss_ref, lossall.at[t * n + d], lsem.at[0], lsem.at[1], who).start()
        return 0

    lax.fori_loop(1, 2 * n, tell, 0)
    lossall[t * n + d] = loss_ref[...]
    step3(nz + 1)
    z_attend(1)
    step2(nz + 3)
    settle(n, gall, gsem.at[0], gsem.at[1])
    wide = ag_ref.shape[2]
    pc[...] = t_dot(ag_ref[...].reshape(n * ex, wide), gall[...].reshape(n * ex, D)).astype(BF16)
    pc_copy = remote(pc, pc_in, fsem_s.at[5], fsem_r.at[5], other)
    pc_copy.start()
    last_expand()
    last_attend(0)
    step3(nz + 2)
    z_attend(2)
    step3(nz + 3)
    z_attend(3)
    all_but_one(s_in, n - 1, ssem.at[0], ssem.at[1])
    s_fin[t] = jnp.sum(s_in[...].astype(F32), 0).astype(BF16)
    s_copy = remote(s_fin.at[t], s_fin.at[t], fsem_s.at[6], fsem_r.at[6], other)
    s_copy.start()
    all_but_one(lossall, 2 * n - 1, lsem.at[0], lsem.at[1])
    ol_ref[...] = jnp.sum(lossall[...], 0)
    last_attend(1)
    pc_copy.wait()
    oc_ref[...] = pc[...].astype(F32) + pc_in[...].astype(F32)
    fin_copy(4).wait()
    for h in range(2):
        oe_ref[:, h * H:(h + 1) * H] = fin_e[h].astype(F32)
    s_copy.wait()
    os_ref[...] = s_fin[0].astype(F32) + s_fin[1].astype(F32)
    last_attend(2)
    last_attend(3)
    fin_copy(0).wait()
    for h in range(2):
        oo_ref[:, h * H:(h + 1) * H] = fin_a[0, h].astype(F32)
    for third in range(3):
        fin_copy(1 + third).wait()
        for h in range(2):
            for part in range(3):
                lo = part * D + 256 * third + 128 * h
                oa_ref[:, lo:lo + 128] = fin_a[1 + third, h, :, 128 * part:128 * (part + 1)].astype(F32)


def text_backward(per, n, x, small, g, grow, ag, loss, saved, attend, output, expand, contract):
    n1, proj, att, ctx, mid, n2, gp = saved
    M = x.shape[0]
    ex, wide, nz = g.shape[0], ag.shape[2], n // 4
    rows_e, rows_a, H = FF // n, D // n, D // 2
    S = jax.ShapeDtypeStruct
    V = lambda *shape: pltpu.VMEM(shape, BF16)
    like = lambda a: pltpu.VMEM(a.shape, a.dtype)
    outs = [S((M, D), F32), S((rows_e, D), F32), S((rows_a, 3 * D), F32), S((rows_a, D), F32), S((rows_a, 128), F32), S((wide, D), F32), S((8, 128), F32)]
    q = nz + 4
    dma = pltpu.SemaphoreType.DMA
    held = (x, n1, proj, att, ctx, mid, n2, gp, contract, expand, output, attend)
    scratch = [like(a) for a in held] + [V(M, D), V(M, 3 * D), pltpu.VMEM((16, D), F32)]
    scratch += [V(q, 2, D, H), V(q, D, H), V(q, 2, D // 4, H), V(q, 2, D // 8, H), V(q, D // 4, H), V(nz, D // 4, H), V(4, nz, rows_a, H), V(2, D // 4, H), V(4, 2, rows_a, H),
                V(n, rows_a, 128), V(n, rows_a, 128), V(2, rows_a, 128), V(n, ex, D), V(wide, D), V(wide, D), pltpu.VMEM((2 * n, 8, 128), F32)]
    scratch += [dma((12,)), dma((q,)), dma((q,)), dma((q, 2)), dma((q, 2)), dma((q, 2)), dma((q, 2)), dma((nz + 4,)), dma((nz + 4,)), dma((7,)), dma((7,)), dma((2,)), dma((2,)), dma((2,))]
    return pl.pallas_call(
        functools.partial(back_kernel, per, n), out_shape=outs, in_specs=[VM] * 5 + [ANY] * 12, out_specs=[VM] * 7, scratch_shapes=scratch,
        compiler_params=pltpu.CompilerParams(collective_id=1, has_side_effects=True, vmem_limit_bytes=63 << 20),
        name="text_backward",
    )(small, g, grow, ag, loss, x, n1, proj, att, ctx, mid, n2, gp, contract, expand, output, attend)


def finish_kernel(n, per, counts_ref, tg, oe, oa, oo, os, oc, ol, loss_ref, tg_out, gains, shifts, attend, attend_bias, output, output_bias, expand_t, expand_bias, contract, contract_bias):
    d = lax.axis_index("dp")
    rows_e, rows_a = FF // n, D // n
    loss_ref[...] = ol[0:1, 0:1] / jnp.sum(counts_ref[...].astype(F32).reshape(1, -1), -1, keepdims=True)
    tg_out[...] = tg[...]
    attend[...] = oa[...]
    output[...] = oo[...]
    expand_t[...] = oe[...]
    contract[...] = oc[0:rows_e, :]
    rows = jnp.transpose(jnp.concatenate([os[...], jnp.zeros((128 - rows_a, 128), F32)], 0))
    gains[...] = rows[0:2, 0:rows_a]
    shifts[...] = rows[2:4, 0:rows_a]

    def joined(pieces):
        total = None
        for c, piece in enumerate(pieces):
            line = jnp.concatenate([jnp.broadcast_to(piece, (8, 128)), jnp.zeros((8, 128), F32)], 1)
            line = pltpu.roll(line, c * rows_a, 1) if c else line
            total = line if total is None else total + line
        return total[0:1, 0:len(pieces) * rows_a].reshape(len(pieces) * rows_a)

    attend_bias[...] = joined([rows[4 + c:5 + c] + rows[6 + c:7 + c] for c in range(2)])
    expand_bias[...] = joined([rows[8 + c:9 + c] + rows[12 + c:13 + c] + rows[16 + c:17 + c] + rows[20 + c:21 + c] for c in range(4)])
    output_bias[...] = joined([rows[24:25]])
    line = pltpu.roll(jnp.broadcast_to(oc[rows_e:rows_e + 1, :], (8, D)), lax.rem(D - d * rows_a, D), 1)
    contract_bias[...] = line[0:1, 0:rows_a].reshape(rows_a)


def finish(n, per, counts, *parts):
    tg, oe, oa, oo = parts[:4]
    S = jax.ShapeDtypeStruct
    rows_e, rows_a = FF // n, D // n
    f = lambda *shape: S(shape, F32)
    outs = [f(1, 1), f(*tg.shape), f(2, rows_a), f(2, rows_a), f(*oa.shape), f(2 * rows_a), f(*oo.shape), f(rows_a), f(*oe.shape), f(4 * rows_a), f(rows_e, D), f(rows_a)]
    return pl.pallas_call(functools.partial(finish_kernel, n, per), out_shape=outs, in_specs=[VM] * 8, out_specs=[VM] * 12,
                          compiler_params=pltpu.CompilerParams(vmem_limit_bytes=40 << 20), name="finish")(counts, *parts)


def on_device(n, text_tokens, image_tokens, counts, caption_group, *params):
    image_params, text_params = params[:10], params[10:]
    ex, per, _ = text_tokens.shape
    g, grow, loss, ag, *saved = front(n, text_tokens, image_tokens, counts, caption_group, image_params, text_params, PLAN)
    parts = text_backward(per, n, text_tokens.reshape(ex * per, D), text_params[0], g, grow, ag, loss, saved, *(text_params[k] for k in (2, 4, 6, 8)))
    out = list(finish(n, per, counts, *parts))
    out[0] = out[0].reshape(())
    out[1] = out[1].reshape(ex, per, D)
    out[8] = out[8].T
    return tuple(out)


HEADS = 12
HEAD_DIM = 64


def multiply(left, right):
    return jnp.dot(left, right, preferred_element_type=jnp.float32)


def left_inner(left, right):
    return lax.dot_general(
        left, right, (((0,), (0,)), ((), ())), preferred_element_type=jnp.float32
    )


def right_inner(left, right):
    return lax.dot_general(
        left, right, (((1,), (1,)), ((), ())), preferred_element_type=jnp.float32
    )


def normalize(rows_in, gain, shift):
    centre = rows_in - jnp.mean(rows_in, -1, keepdims=True)
    inverse_std = lax.rsqrt(jnp.mean(centre * centre, -1, keepdims=True) + NORM_EPS)
    unit_rows = centre * inverse_std
    return (unit_rows * gain + shift, unit_rows, inverse_std)


def normalize_back(grad_rows, unit_rows, inverse_std, gain):
    grad_unit = grad_rows * gain
    grad_in = inverse_std * (
        grad_unit
        - jnp.mean(grad_unit, -1, keepdims=True)
        - unit_rows * jnp.mean(grad_unit * unit_rows, -1, keepdims=True)
    )
    return (grad_in, jnp.sum(grad_rows * unit_rows, 0), jnp.sum(grad_rows, 0))


def plain_forward(tokens, params):
    (
        gains,
        shifts,
        attend,
        attend_bias,
        output,
        output_bias,
        expand,
        expand_bias,
        contract,
        contract_bias,
    ) = params
    examples, row_count, features = tokens.shape
    inputs = tokens.astype(jnp.float32).reshape(examples * row_count, features)
    normed, unit_one, inverse_one = normalize(
        inputs, gains[0].astype(jnp.float32), shifts[0].astype(jnp.float32)
    )
    normed_one = normed.astype(jnp.bfloat16)
    full_bias = jnp.concatenate(
        [attend_bias[:features], jnp.zeros_like(output_bias), attend_bias[features:]]
    ).astype(jnp.float32)
    projected = (multiply(normed_one, attend) + full_bias).astype(jnp.bfloat16)
    projected = projected.reshape(examples, row_count, 3, HEADS, HEAD_DIM)
    queries = projected[:, :, 0]
    keys = projected[:, :, 1]
    values = projected[:, :, 2]
    scores = jnp.einsum(
        "erhd,eshd->ehrs", queries, keys, preferred_element_type=jnp.float32
    ) * HEAD_DIM ** (-0.5)
    attention = jax.nn.softmax(scores, axis=-1)
    attention_low = attention.astype(jnp.bfloat16)
    context = jnp.einsum(
        "ehrs,eshd->erhd", attention_low, values, preferred_element_type=jnp.float32
    )
    context = context.astype(jnp.bfloat16).reshape(examples * row_count, features)
    middle = inputs + (multiply(context, output) + output_bias.astype(jnp.float32))
    normed, unit_two, inverse_two = normalize(
        middle, gains[1].astype(jnp.float32), shifts[1].astype(jnp.float32)
    )
    normed_two = normed.astype(jnp.bfloat16)
    pre_gelu = multiply(normed_two, expand) + expand_bias.astype(jnp.float32)
    activated = jax.nn.gelu(pre_gelu).astype(jnp.bfloat16)
    block_out = middle + (multiply(activated, contract) + contract_bias.astype(jnp.float32))
    pooled = jnp.mean(block_out.reshape(examples, row_count, features), axis=1)
    inverse_norm = lax.rsqrt(jnp.sum(pooled * pooled, -1, keepdims=True) + EMBED_EPS)
    embedding = pooled * inverse_norm
    saved = (
        normed_one,
        unit_one,
        inverse_one,
        queries,
        keys,
        values,
        attention,
        attention_low,
        context,
        unit_two,
        inverse_two,
        normed_two,
        pre_gelu,
        activated,
        embedding,
        inverse_norm,
    )
    return (embedding, saved)


def backward(params, saved, grad_embedding, row_count):
    (
        gains,
        shifts,
        attend,
        attend_bias,
        output,
        output_bias,
        expand,
        expand_bias,
        contract,
        contract_bias,
    ) = params
    (
        normed_one,
        unit_one,
        inverse_one,
        queries,
        keys,
        values,
        attention,
        attention_low,
        context,
        unit_two,
        inverse_two,
        normed_two,
        pre_gelu,
        activated,
        embedding,
        inverse_norm,
    ) = saved
    examples, features = embedding.shape
    grad_pooled = inverse_norm * (
        grad_embedding - embedding * jnp.sum(grad_embedding * embedding, -1, keepdims=True)
    )
    grad_rows = jnp.broadcast_to(
        (grad_pooled / row_count)[:, None, :], (examples, row_count, features)
    ).reshape(examples * row_count, features)
    grad_mlp = grad_rows.astype(jnp.bfloat16)
    grad_contract = left_inner(activated, grad_mlp)
    grad_contract_bias = jnp.sum(grad_mlp.astype(jnp.float32), 0)
    grad_activated = right_inner(grad_mlp, contract)
    gelu_back = jax.vjp(jax.nn.gelu, pre_gelu)[1]
    grad_pre = gelu_back(grad_activated)[0].astype(jnp.bfloat16)
    grad_expand = left_inner(normed_two, grad_pre)
    grad_expand_bias = jnp.sum(grad_pre.astype(jnp.float32), 0)
    grad_normed_two = right_inner(grad_pre, expand)
    grad_middle, gain_two, shift_two = normalize_back(
        grad_normed_two, unit_two, inverse_two, gains[1].astype(jnp.float32)
    )
    grad_middle = grad_middle + grad_rows
    grad_branch = grad_middle.astype(jnp.bfloat16)
    grad_output = left_inner(context, grad_branch)
    grad_output_bias = jnp.sum(grad_branch.astype(jnp.float32), 0)
    grad_context = (
        right_inner(grad_branch, output)
        .astype(jnp.bfloat16)
        .reshape(examples, row_count, HEADS, HEAD_DIM)
    )
    grad_attention = jnp.einsum(
        "erhd,eshd->ehrs", grad_context, values, preferred_element_type=jnp.float32
    )
    grad_values = jnp.einsum(
        "ehrs,erhd->eshd", attention_low, grad_context, preferred_element_type=jnp.float32
    )
    grad_scores = (
        attention * (grad_attention - jnp.sum(grad_attention * attention, -1, keepdims=True))
    ).astype(jnp.bfloat16)
    grad_queries = jnp.einsum(
        "ehrs,eshd->erhd", grad_scores, keys, preferred_element_type=jnp.float32
    ) * HEAD_DIM ** (-0.5)
    grad_keys = jnp.einsum(
        "ehrs,erhd->eshd", grad_scores, queries, preferred_element_type=jnp.float32
    ) * HEAD_DIM ** (-0.5)
    grad_projected = (
        jnp.stack([grad_queries, grad_keys, grad_values], 2)
        .astype(jnp.bfloat16)
        .reshape(examples * row_count, 3 * features)
    )
    grad_attend = left_inner(normed_one, grad_projected)
    column_sums = jnp.sum(grad_projected.astype(jnp.float32), 0)
    grad_attend_bias = jnp.concatenate([column_sums[:features], column_sums[2 * features :]])
    grad_normed_one = right_inner(grad_projected, attend)
    grad_inputs, gain_one, shift_one = normalize_back(
        grad_normed_one, unit_one, inverse_one, gains[0].astype(jnp.float32)
    )
    grad_inputs = grad_inputs + grad_middle
    grads = (
        jnp.stack([gain_one, gain_two]),
        jnp.stack([shift_one, shift_two]),
        grad_attend,
        grad_attend_bias,
        grad_output,
        grad_output_bias,
        grad_expand,
        grad_expand_bias,
        grad_contract,
        grad_contract_bias,
    )
    return (grad_inputs.reshape(examples, row_count, features), grads)


def masked_softmax(logits, allowed, live_rows):
    filled = jnp.where(allowed, logits, -1e30)
    largest = jnp.max(filled, -1, keepdims=True)
    weights = jnp.exp(filled - largest) * allowed.astype(jnp.float32)
    safe_total = jnp.sum(weights, -1, keepdims=True) + (1.0 - live_rows)[:, None]
    return (weights / safe_total, largest[:, 0] + jnp.log(safe_total[:, 0]))


def plain_on_device(
    text_tokens,
    image_tokens,
    counts,
    caption_group,
    image_gains,
    image_shifts,
    image_attend,
    image_attend_bias,
    image_output,
    image_output_bias,
    image_expand,
    image_expand_bias,
    image_contract,
    image_contract_bias,
    text_gains,
    text_shifts,
    text_attend,
    text_attend_bias,
    text_output,
    text_output_bias,
    text_expand,
    text_expand_bias,
    text_contract,
    text_contract_bias,
):
    image_params = (
        image_gains,
        image_shifts,
        image_attend,
        image_attend_bias,
        image_output,
        image_output_bias,
        image_expand,
        image_expand_bias,
        image_contract,
        image_contract_bias,
    )
    text_params = (
        text_gains,
        text_shifts,
        text_attend,
        text_attend_bias,
        text_output,
        text_output_bias,
        text_expand,
        text_expand_bias,
        text_contract,
        text_contract_bias,
    )
    image_embedding, image_saved = plain_forward(image_tokens, image_params)
    text_embedding, text_saved = plain_forward(text_tokens, text_params)
    image_low = image_embedding.astype(jnp.bfloat16)
    text_low = text_embedding.astype(jnp.bfloat16)
    all_images, all_texts = (
        lax.all_gather(image_low, ("tower", "dp"), axis=0, tiled=True),
        lax.all_gather(text_low, ("tower", "dp"), axis=0, tiled=True),
    )
    per_device = image_low.shape[0]
    everyone = all_images.shape[0]
    device_rank = lax.axis_index(("tower", "dp"))
    positions = jnp.arange(everyone, dtype=jnp.int32)
    owned = device_rank * per_device + jnp.arange(per_device, dtype=jnp.int32)
    live_all = positions % per_device < jnp.repeat(counts, per_device, total_repeat_length=everyone)
    live_own = lax.dynamic_slice_in_dim(live_all, device_rank * per_device, per_device)
    group_own = lax.dynamic_slice_in_dim(caption_group, device_rank * per_device, per_device)
    diagonal = owned[:, None] == positions[None, :]
    allowed = (
        live_own[:, None]
        & live_all[None, :]
        & ((group_own[:, None] != caption_group[None, :]) | diagonal)
    )
    live_rows = live_own.astype(jnp.float32)
    diagonal_float = diagonal.astype(jnp.float32)
    forward_logits = right_inner(text_low, all_images) * LOGIT_SCALE
    backward_logits = right_inner(image_low, all_texts) * LOGIT_SCALE
    forward_probs, forward_lse = masked_softmax(forward_logits, allowed, live_rows)
    backward_probs, backward_lse = masked_softmax(backward_logits, allowed, live_rows)
    forward_terms = forward_lse - jnp.sum(forward_logits * diagonal_float, -1)
    backward_terms = backward_lse - jnp.sum(backward_logits * diagonal_float, -1)
    local_sum = 0.5 * (jnp.sum(live_rows * forward_terms) + jnp.sum(live_rows * backward_terms))
    loss_sum = lax.psum(local_sum, ("tower", "dp"))
    loss_value = loss_sum / jnp.sum(counts).astype(jnp.float32)
    forward_coef = (0.5 * live_rows[:, None] * (forward_probs - diagonal_float)).astype(
        jnp.bfloat16
    )
    grad_embedding = LOGIT_SCALE * multiply(forward_coef, all_images)
    lse_everyone = lax.all_gather(backward_lse, ("tower", "dp"), axis=0, tiled=True)
    shifted = jnp.where(allowed, forward_logits - lse_everyone[None, :], -1e30)
    live_columns = live_all.astype(jnp.float32)
    column_coef = (0.5 * live_columns[None, :] * (jnp.exp(shifted) - diagonal_float)).astype(
        jnp.bfloat16
    )
    grad_embedding = grad_embedding + LOGIT_SCALE * multiply(column_coef, all_images)
    text_grad, grads = backward(text_params, text_saved, grad_embedding, text_tokens.shape[1])
    shards = (
        lax.psum_scatter(grads[0], "dp", scatter_dimension=1, tiled=True),
        lax.psum_scatter(grads[1], "dp", scatter_dimension=1, tiled=True),
        lax.psum_scatter(grads[2], "dp", scatter_dimension=0, tiled=True),
        lax.psum_scatter(grads[3], "dp", scatter_dimension=0, tiled=True),
        lax.psum_scatter(grads[4], "dp", scatter_dimension=0, tiled=True),
        lax.psum_scatter(grads[5], "dp", scatter_dimension=0, tiled=True),
        lax.psum_scatter(grads[6], "dp", scatter_dimension=1, tiled=True),
        lax.psum_scatter(grads[7], "dp", scatter_dimension=0, tiled=True),
        lax.psum_scatter(grads[8], "dp", scatter_dimension=0, tiled=True),
        lax.psum_scatter(grads[9], "dp", scatter_dimension=0, tiled=True),
    )
    totals = (
        lax.psum(shards[0].astype(jnp.bfloat16), "tower").astype(jnp.float32),
        lax.psum(shards[1].astype(jnp.bfloat16), "tower").astype(jnp.float32),
        lax.psum(shards[2].astype(jnp.bfloat16), "tower").astype(jnp.float32),
        lax.psum(shards[3].astype(jnp.bfloat16), "tower").astype(jnp.float32),
        lax.psum(shards[4].astype(jnp.bfloat16), "tower").astype(jnp.float32),
        lax.psum(shards[5].astype(jnp.bfloat16), "tower").astype(jnp.float32),
        lax.psum(shards[6].astype(jnp.bfloat16), "tower").astype(jnp.float32),
        lax.psum(shards[7].astype(jnp.bfloat16), "tower").astype(jnp.float32),
        lax.psum(shards[8].astype(jnp.bfloat16), "tower").astype(jnp.float32),
        lax.psum(shards[9].astype(jnp.bfloat16), "tower").astype(jnp.float32),
    )
    return (
        loss_value,
        text_grad,
        totals[0],
        totals[1],
        totals[2],
        totals[3],
        totals[4],
        totals[5],
        totals[6],
        totals[7],
        totals[8],
        totals[9],
    )


def solution(mesh):
    n = mesh.shape["dp"]
    whole, both = P(), P(("tower", "dp"), None, None)
    fits = FF // n * 4 == D and n % 8 == 0
    body = functools.partial(on_device, n) if fits else plain_on_device
    out_specs = (P(), both, P(None, "dp"), P(None, "dp"), P("dp", None), P("dp"), P("dp", None), P("dp"), P(None, "dp"), P("dp"), P("dp", None), P("dp"))
    return jax.shard_map(body, mesh=mesh, in_specs=(both, both) + (whole,) * 22, out_specs=out_specs, check_vma=False)
```

```python
import functools
import jax
import jax.numpy as jnp
import numpy as np
from jax import lax
from jax.experimental import pallas as pl
from jax.experimental.pallas import tpu as pltpu
from jax.sharding import PartitionSpec as P

F32, BF16 = jnp.float32, jnp.bfloat16
D, HD, FF = 768, 64, 3072
PAIRS = D // (2 * HD)
KW = 128
NORM_EPS, EMBED_EPS, LOGIT_SCALE = 1e-5, 1e-6, 64.0
NEG = -1e30
ANY = pl.BlockSpec(memory_space=pl.ANY)
VM = pl.BlockSpec(memory_space=pltpu.VMEM)
GELU_C, GELU_A = float(np.sqrt(2 / np.pi)), 0.044715


def dot(a, b):
    return jnp.dot(a, b, preferred_element_type=F32)


def dot_t(a, b):
    return lax.dot_general(a, b, (((1,), (1,)), ((), ())), preferred_element_type=F32)


def t_dot(a, b):
    return lax.dot_general(a, b, (((0,), (0,)), ((), ())), preferred_element_type=F32)


def unit_rows(v):
    centre = v - jnp.mean(v, -1, keepdims=True)
    inv = lax.rsqrt(jnp.mean(centre * centre, -1, keepdims=True) + NORM_EPS)
    return centre * inv, inv


def head_masks():
    lane = lax.broadcasted_iota(jnp.int32, (1, 2 * HD), 1)
    even = (lane < HD).astype(F32)
    return even.astype(BF16), (1.0 - even).astype(BF16)


def pair_mask(rows, per, real):
    r = lax.broadcasted_iota(jnp.int32, (rows, 2 * KW), 0)
    c = lax.broadcasted_iota(jnp.int32, (rows, 2 * KW), 1) % KW
    ok = (r // per == c // per) & (c % per < real) & (c < rows)
    return jnp.where(ok, 0.0, NEG).astype(F32)


def split_heads(a, even, odd):
    return jnp.concatenate([a * even, a * odd], axis=0)


def softmax_half(s):
    m = jnp.max(s, -1, keepdims=True)
    p = jnp.exp(s - m)
    return p / jnp.sum(p, -1, keepdims=True)


def exp_half(s):
    return jnp.exp(s - jnp.max(s, -1, keepdims=True)).astype(BF16)


def block_forward(x, rows, groups, small, W, wait, done, proj, ctx, mask, att_out, keep):
    attend, output, expand, contract = W
    unit, _ = unit_rows(x)
    n1 = (unit * small[0:1, :] + small[2:3, :]).astype(BF16)
    keep("n1", n1)
    wait("attend")
    M = rows * groups
    step = 256
    for c in range(3 * D // step):
        y = dot(n1, attend[:, c * step:(c + 1) * step])
        if c * step < D:
            y = y + small[4:5, c * step:(c + 1) * step]
        elif c * step >= 2 * D:
            y = y + small[5:6, c * step - 2 * D:(c + 1) * step - 2 * D]
        proj[0:M, c * step:(c + 1) * step] = y.astype(BF16)
    done("attend")
    keep("proj", None)
    even, odd = head_masks()
    ones = split_heads(jnp.ones((KW, 2 * HD), BF16), even, odd)

    def group(g, _):
        r0 = pl.multiple_of(g * rows, 16)
        for j in range(PAIRS):
            lanes = slice(j * 2 * HD, (j + 1) * 2 * HD)
            q = proj[pl.ds(r0, rows), j * 128:(j + 1) * 128]
            kk = split_heads(proj[pl.ds(r0, KW), D + j * 128:D + (j + 1) * 128], even, odd)
            vv = split_heads(proj[pl.ds(r0, KW), 2 * D + j * 128:2 * D + (j + 1) * 128], even, odd)
            s = dot_t(q, kk) * HD ** -0.5 + mask[...]
            if att_out is None:
                p = jnp.concatenate([exp_half(s[:, :KW]), exp_half(s[:, KW:])], axis=1)
                both = dot(p, jnp.concatenate([vv, ones], axis=1))
                ctx[pl.ds(r0, rows), lanes] = (both[:, :128] / both[:, 128:]).astype(BF16)
            else:
                a = jnp.concatenate([softmax_half(s[:, :KW]), softmax_half(s[:, KW:])], axis=1)
                att_out[g * PAIRS + j] = a
                ctx[pl.ds(r0, rows), lanes] = dot(a.astype(BF16), vv).astype(BF16)
        return 0

    lax.fori_loop(0, groups, group, 0)
    wait("output")
    middle = x + (dot(ctx[0:M, :], output[...]) + small[6:7, :])
    done("output")
    keep("middle", middle)
    unit, _ = unit_rows(middle)
    n2 = (unit * small[1:2, :] + small[3:4, :]).astype(BF16)
    keep("n2", n2)
    wait("expand")
    acc = middle + small[11:12, :]
    step = 768
    for c in range(FF // step):
        pre = dot(n2, expand[:, c * step:(c + 1) * step]) + small[7 + c:8 + c, :]
        sq = pre * pre
        th = jnp.tanh(pre * (GELU_C + GELU_C * GELU_A * sq))
        cdf = 0.5 + 0.5 * th
        act = (pre * cdf).astype(BF16)
        keep("act", act, c, pre, sq, th, cdf)
        if c == 0:
            wait("contract")
        acc = acc + dot(act, contract[c * step:(c + 1) * step, :])
    done("expand")
    done("contract")
    return acc


def embed_rows(pooled):
    inv = lax.rsqrt(jnp.sum(pooled * pooled, -1, keepdims=True) + EMBED_EPS)
    return pooled * inv, inv


def wide_of(n_dp):
    return -(-(FF // n_dp + 1) // 128) * 128


MESH_ID = pl.DeviceIdType.MESH


def place():
    return lax.axis_index("tower"), lax.axis_index("dp")


def greet(n):
    t, d = place()
    barrier = pltpu.get_barrier_semaphore()

    def one(k, _):
        who = (lax.rem(t + k // n, 2), lax.rem(d + lax.rem(k, n), n))
        pl.semaphore_signal(barrier, inc=1, device_id=who, device_id_type=MESH_ID)
        return 0

    lax.fori_loop(1, 2 * n, one, 0)


def spread(n, src, dst, send, recv):
    t, d = place()

    def one(k, _):
        pltpu.make_async_remote_copy(src_ref=src, dst_ref=dst.at[d], send_sem=send, recv_sem=recv,
                                     device_id=(t, lax.rem(d + k, n)), device_id_type=MESH_ID).start()
        return 0

    lax.fori_loop(1, n, one, 0)


def settle(n, dst, send, recv):
    part = dst.at[pl.ds(0, n - 1)]
    pltpu.make_async_copy(part, part, send).wait()
    pltpu.make_async_copy(part, part, recv).wait()


def contrast_rows(fl, allowed, live_rows):
    filled = jnp.where(allowed, fl, NEG)
    largest = jnp.max(filled, -1, keepdims=True)
    weights = jnp.where(allowed, jnp.exp(filled - largest), 0.0)
    total = jnp.sum(weights, -1, keepdims=True) + (1.0 - live_rows)
    return weights / total, largest + jnp.log(total)


def contrast_rows(fl, allowed, live_rows):
    filled = jnp.where(allowed, fl, NEG)
    largest = jnp.max(filled, -1, keepdims=True)
    weights = jnp.where(allowed, jnp.exp(filled - largest), 0.0)
    total = jnp.sum(weights, -1, keepdims=True) + (1.0 - live_rows)
    return weights / total, largest + jnp.log(total)


def fill_small(small, refs):
    gains, shifts, attend_bias, output_bias, expand_bias, contract_bias = refs
    small[0:2, :] = gains[...].astype(F32)
    small[2:4, :] = shifts[...].astype(F32)
    row = 4
    for ref in (attend_bias, output_bias, expand_bias, contract_bias):
        for k in range(ref.shape[0] // D):
            small[row:row + 1, :] = ref[pl.ds(k * D, D)].astype(F32).reshape(1, D)
            row += 1


def front_kernel(per_text, real, plan, n, *refs):
    it = iter(refs)
    take = lambda k: [next(it) for _ in range(k)]
    x_ref, counts_ref, group_ref = take(3)
    image_small, text_small = take(6), take(6)
    image_w, text_w = take(4), take(4)
    tokens_h, = take(1)
    g_ref, grow_ref, loss_ref, ag_ref = take(4)
    saved_h = take(7)
    weights = take(4)
    saved = take(7)
    tokens, by_place, xs, proj_i, ctx_i, mask_t, mask_i, small_t, small_i = take(9)
    lows_t, asum, emb_ref, own_rows, lse, = take(5)
    lows_i = take(len(plan))
    load, out_sem, tok_sem, ssem, rsem, osem_s, osem_r = take(7)
    t, d = place()
    greet(n)
    names = ("attend", "output", "expand", "contract")
    copies = {}
    for k, name in enumerate(names):
        copies["text", name] = pltpu.make_async_copy(text_w[k], weights[k], load.at[k])
        copies["text", name].start()
        copies["image", name] = pltpu.make_async_copy(image_w[k], weights[k], load.at[4 + k])
    token_copy = pltpu.make_async_copy(tokens_h, tokens, tok_sem)
    token_copy.start()
    n1, proj, att, ctx, mid, n2, gp = saved
    outs = dict(zip(("n1", "proj", "att", "ctx", "mid", "n2", "gp"), [pltpu.make_async_copy(v, h, out_sem.at[k]) for k, (v, h) in enumerate(zip(saved, saved_h))]))
    fill_small(small_t, text_small)
    fill_small(small_i, image_small)
    M = x_ref.shape[0]
    ex = M // per_text
    mask_t[...] = pair_mask(KW, per_text, per_text)
    shard, wide = FF // n, asum.shape[2]
    for k in range(n):
        asum[k, :, shard:] = jnp.full((ex, wide - shard), per_text, BF16)

    def keep(name, value, *extra):
        if name == "n1":
            n1[...] = value
            outs["n1"].start()
        elif name == "proj":
            outs["proj"].start()
        elif name == "middle":
            mid[...] = value
            for o in ("att", "ctx", "mid"):
                outs[o].start()
        elif name == "n2":
            n2[...] = value
            outs["n2"].start()
        else:
            c, pre, sq, th, cdf = extra
            w = value.shape[1]
            total = jnp.sum(value.astype(F32).reshape(ex, per_text, w), 1).astype(BF16)
            for k in range(c * w // shard, (c + 1) * w // shard):
                asum[k, :, 0:shard] = total[:, k * shard - c * w:(k + 1) * shard - c * w]
            gp[:, c * w:(c + 1) * w] = (cdf + (0.5 * GELU_C) * pre * (1.0 - th * th) * (1.0 + (3 * GELU_A) * sq)).astype(BF16)

    out = block_forward(x_ref[...].astype(F32), KW, M // KW, small_t, weights, lambda name: copies["text", name].wait(), lambda name: copies["image", name].start(),
                        proj, ctx, mask_t, att, keep)
    outs["gp"].start()
    emb, inv = embed_rows(jnp.sum(out.reshape(ex, per_text, D), 1) * (1.0 / per_text))
    emb_ref[0] = emb
    emb_ref[1] = jnp.broadcast_to(inv, emb.shape)
    lows_t[t, d] = emb.astype(BF16)

    def send(src, dst, s, r, who):
        return pltpu.make_async_remote_copy(src_ref=src, dst_ref=dst, send_sem=s, recv_sem=r, device_id=who, device_id_type=MESH_ID)

    pl.semaphore_wait(pltpu.get_barrier_semaphore(), 2 * n - 1)
    spread(n, lows_t.at[t, d], lows_t.at[t], ssem.at[0], rsem.at[0])
    slot = lax.rem(d, 4) * (n // 4) + d // 4

    def one(k, _):
        to = lax.rem(d + k, n)
        send(asum.at[to], ag_ref.at[slot], ssem.at[1], rsem.at[1], (t, to)).start()
        return 0

    lax.fori_loop(1, n, one, 0)
    ag_ref[slot] = asum[d]

    def pass_over(buf, k):
        return send(buf.at[t], buf.at[t], osem_s.at[k], osem_r.at[k], (1 - t, d))

    per = -(-real // 8) * 8
    rows = 2 * per
    xs[...] = jnp.zeros_like(xs)
    proj_i[proj_i.shape[0] - 16:, :] = jnp.zeros((16, 3 * D), BF16)
    mask_i[...] = pair_mask(rows, per, real)
    bufs = [lows_t] + lows_i
    slots = [0] + [2 + k for k in range(len(plan))]

    def arrive(k):
        settle(n, bufs[k].at[t], ssem.at[slots[k]], rsem.at[slots[k]])
        pass_over(bufs[k], k).start()

    for k, (first, pairs) in enumerate(plan):
        def wait(name):
            if k == 0:
                copies["image", name].wait()
        if k == 0:
            token_copy.wait()
        rows_k, ex_k = rows * pairs, 2 * pairs
        held = ex // 2
        if first % held == 0:
            for v in range(D // 128):
                by_place[v] = tokens[:, first:first + held, v * 128:(v + 1) * 128].astype(F32).reshape(real * held, 128)
        for e in range(ex_k):
            for lo in range(0, real, 8):
                count = min(8, real - lo)
                for v in range(D // 128):
                    xs[e * per + lo:e * per + lo + count, v * 128:(v + 1) * 128] = by_place[v, pl.ds(first % held + e + lo * held, count, stride=held), :]
        out = block_forward(xs[0:rows_k, :], rows, pairs, small_i, weights, wait, lambda name: None, proj_i, ctx_i, mask_i, None, lambda *a: None)
        out = out.reshape(ex_k, per, D)
        ok = lax.broadcasted_iota(jnp.int32, (ex_k, per, D), 1) < real
        emb, _ = embed_rows(jnp.sum(jnp.where(ok, out, 0.0), 1) * (1.0 / real))
        lows_i[k][t, d] = emb.astype(BF16)
        spread(n, lows_i[k].at[t, d], lows_i[k].at[t], ssem.at[slots[k + 1]], rsem.at[slots[k + 1]])
        arrive(k)
        if k > 0:
            pass_over(bufs[k - 1], k - 1).wait()

    every, nd = 2 * n * ex, 2 * n
    rank = t * n + d
    counts_row = jnp.broadcast_to(counts_ref[...].astype(F32).reshape(1, nd), (8, nd)).astype(BF16)

    def live_of(device, row):
        hot = (lax.broadcasted_iota(jnp.int32, (nd, device.shape[1]), 0) == device).astype(F32).astype(BF16)
        return (row.astype(F32) < dot(counts_row, hot)[0:1, :]).astype(F32), hot

    natural = lax.broadcasted_iota(jnp.int32, (1, every), 1)
    group_row = group_ref[...].astype(F32).reshape(1, every)
    live_row, _ = live_of(natural // ex, natural % ex)
    text_group = jnp.transpose(jnp.broadcast_to(group_row, (128, every)))[:, 0:1]
    text_live = jnp.transpose(jnp.broadcast_to(live_row, (128, every)))[:, 0:1]
    own_text = lows_t[t, d]
    groups, lives, places = [], [], []
    at = 0
    for k, (first, pairs) in enumerate(plan):
        ek = 2 * pairs
        w = nd * ek
        col = lax.broadcasted_iota(jnp.int32, (1, w), 1)
        device, row = col // ek, first + col % ek
        live, hot = live_of(device, row)
        pick = (lax.broadcasted_iota(jnp.int32, (every, w), 0) == device * ex + row).astype(F32).astype(BF16)
        groups.append(dot(jnp.broadcast_to(group_row, (8, every)).astype(BF16), pick)[0:1, :])
        lives.append(live)
        places.append(device * ex + row)
    texts = lows_t[...].reshape(every, D)

    def chunk_logits(k, at):
        w = nd * 2 * plan[k][1]
        images = lows_i[k][...].reshape(w, D)
        own_rows[:, at:at + w] = dot_t(own_text, images) * LOGIT_SCALE
        for lo in range(0, w, 256):
            part = slice(lo, min(lo + 256, w))
            logits = dot_t(texts, images[part]) * LOGIT_SCALE
            same = lax.broadcasted_iota(jnp.int32, logits.shape, 0) == places[k][:, part]
            allowed = (text_live * lives[k][:, part] > 0.0) & ((text_group != groups[k][:, part]) | same)
            filled = jnp.where(allowed, logits, NEG)
            largest = jnp.max(filled, 0, keepdims=True)
            total = jnp.sum(jnp.where(allowed, jnp.exp(filled - largest), 0.0), 0, keepdims=True) + (1.0 - lives[k][:, part])
            lse[:, at + lo:at + lo + logits.shape[1]] = jnp.broadcast_to(largest + jnp.log(total), (8, logits.shape[1]))
        return at + w

    for k in range(len(plan)):
        if k == len(plan) - 1:
            arrive(k + 1)
            pass_over(bufs[k + 1], k + 1).wait()
        elif k == len(plan) - 2:
            pass_over(bufs[k + 1], k + 1).wait()
        at = chunk_logits(k, at)
    column_group, column_live, column_place = (jnp.concatenate(v, 1) for v in (groups, lives, places))
    diag_b = column_place == lax.broadcasted_iota(jnp.int32, (ex, every), 0) + rank * ex
    diagonal = diag_b.astype(F32)
    image_lse = lse[0:1, :]
    fl = own_rows[...]
    live_own = jnp.sum(diagonal * column_live, -1, keepdims=True)
    group_own = jnp.sum(diagonal * column_group, -1, keepdims=True)
    allowed = (live_own * column_live > 0.0) & ((group_own != column_group) | diag_b)
    probs, text_lse = contrast_rows(fl, allowed, live_own)
    own_diag = fl * diagonal
    terms = live_own * (text_lse - jnp.sum(own_diag, -1, keepdims=True)) + jnp.sum(diagonal * (live_own * image_lse) - live_own * own_diag, -1, keepdims=True)
    loss_ref[...] = jnp.broadcast_to(0.5 * jnp.sum(terms, 0, keepdims=True), loss_ref.shape)
    forward_coef = (0.5 * live_own * (probs - diagonal)).astype(BF16)
    shifted = jnp.where(allowed, jnp.exp(jnp.where(allowed, fl - image_lse, NEG)), 0.0)
    column_coef = (0.5 * column_live * (shifted - diagonal)).astype(BF16)
    coefs = jnp.concatenate([forward_coef, column_coef], 0)
    at, grad = 0, None
    for k, (first, pairs) in enumerate(plan):
        w = nd * 2 * pairs
        part = dot(coefs[:, at:at + w], lows_i[k][...].reshape(w, D))
        grad = part if grad is None else grad + part
        at += w
    grad = LOGIT_SCALE * grad[0:ex] + LOGIT_SCALE * grad[ex:]
    emb = emb_ref[0]
    pooled = emb_ref[1] * (grad - emb * jnp.sum(grad * emb, -1, keepdims=True))
    rows_out = pooled * (1.0 / per_text)
    grow_ref[...] = rows_out
    g_ref[...] = rows_out.astype(BF16)
    settle(n, ag_ref, ssem.at[1], rsem.at[1])
    for o in outs.values():
        o.wait()


def front(n, text_tokens, image_tokens, counts, group, image_params, text_params, plan):
    ex, per, _ = text_tokens.shape
    real = image_tokens.shape[1]
    M = ex * per
    wide = wide_of(n)
    S = jax.ShapeDtypeStruct
    small_of = lambda p: [p[0], p[1], p[3], p[5], p[7], p[9]]
    weights_of = lambda p: [p[2], p[4], p[6], p[8]]
    kept = [S((M, D), BF16), S((M, 3 * D), BF16), S((M // KW * PAIRS, KW, 2 * KW), F32), S((M, D), BF16), S((M, D), F32), S((M, D), BF16), S((M, FF), BF16)]
    like = lambda a: pltpu.VMEM(a.shape, a.dtype)
    per_i = -(-real // 8) * 8
    big = max(p for _, p in plan) * 2 * per_i
    scratch = [like(a) for a in weights_of(text_params)] + [like(a) for a in kept]
    scratch += [pltpu.VMEM((real, ex, D), BF16), pltpu.VMEM((D // 128, real * ex // 2, 128), F32), pltpu.VMEM((big, D), F32), pltpu.VMEM((big + 16, 3 * D), BF16), pltpu.VMEM((big, D), BF16),
                pltpu.VMEM((KW, 2 * KW), F32), pltpu.VMEM((2 * per_i, 2 * KW), F32), pltpu.VMEM((16, D), F32), pltpu.VMEM((16, D), F32)]
    scratch += [pltpu.VMEM((2, n, ex, D), BF16), pltpu.VMEM((n, ex, wide), BF16), pltpu.VMEM((2, ex, D), F32), pltpu.VMEM((ex, 2 * n * ex), F32), pltpu.VMEM((8, 2 * n * ex), F32)]
    scratch += [pltpu.VMEM((2, n, 2 * p, D), BF16) for _, p in plan]
    dma = pltpu.SemaphoreType.DMA
    k = len(plan)
    scratch += [dma((8,)), dma((7,)), dma, dma((k + 2,)), dma((k + 2,)), dma((k + 1,)), dma((k + 1,))]
    return pl.pallas_call(
        functools.partial(front_kernel, per, real, plan, n),
        out_shape=[S((ex, D), BF16), S((ex, D), F32), S((8, 128), F32), S((n, ex, wide), BF16)] + kept,
        in_specs=[VM] * 15 + [ANY] * 9, out_specs=[VM] * 4 + [ANY] * 7, scratch_shapes=scratch,
        compiler_params=pltpu.CompilerParams(collective_id=0, has_side_effects=True, vmem_limit_bytes=63 << 20),
        name="forward_and_loss",
    )(text_tokens.reshape(M, D), counts, group, *small_of(image_params), *small_of(text_params), *weights_of(image_params), *weights_of(text_params), image_tokens.transpose(1, 0, 2))


def norm_back(grad, unit, inv, gain):
    gu = grad * gain
    out = inv * (gu - jnp.mean(gu, -1, keepdims=True) - unit * jnp.mean(gu * unit, -1, keepdims=True))
    return out, jnp.sum(grad * unit, 0, keepdims=True), jnp.sum(grad, 0, keepdims=True)


def back_kernel(per, n, small, g_ref, grow_ref, ag_ref, loss_ref, x_h, n1_h, proj_h, att_h, ctx_h, mid_h, n2_h, gp_h, contract_h, expand_h, output_h, attend_h,
                tg_ref, oe_ref, oa_ref, oo_ref, os_ref, oc_ref,
                xb, n1, proj, att, ctx, mid, n2, gp, contract, expand, output, attend, gctx, gproj, rowsums,
                grads, core_in, in1, in2, red, zin_e, zin_a, fin_e, fin_a, s_out, s_in, s_fin, gall, pc, pc_in,
                load, csem_s, csem_r, sem1_s, sem1_r, sem2_s, sem2_r, zsem_s, zsem_r, fsem_s, fsem_r, gsem, ssem):
    t, d = place()
    dx, dy, dz, nz = lax.rem(d, 2), lax.rem(d // 2, 2), d // 4, n // 4
    xy = lax.rem(d, 4)
    other = (1 - t, d)
    partner = ((t, d + 1 - 2 * dx), (t, d + 2 - 4 * dy))
    greet(n)
    copies = {}
    for k, (name, h, v) in enumerate((("contract", contract_h, contract), ("gp", gp_h, gp), ("n2", n2_h, n2), ("expand", expand_h, expand), ("mid", mid_h, mid), ("ctx", ctx_h, ctx),
                                      ("output", output_h, output), ("proj", proj_h, proj), ("att", att_h, att), ("n1", n1_h, n1), ("attend", attend_h, attend), ("x", x_h, xb))):
        copies[name] = pltpu.make_async_copy(h, v, load.at[k])
        copies[name].start()
    M = xb.shape[0]
    ex = M // per
    rows_e, rows_a, H = FF // n, D // n, D // 2
    B = D // 2
    Q, E8 = B // 4, B // 2

    def remote(src, dst, ss, rs, who):
        return pltpu.make_async_remote_copy(src_ref=src, dst_ref=dst, send_sem=ss, recv_sem=rs, device_id=who, device_id_type=MESH_ID)

    def core_copy(q):
        return remote(grads.at[q, 1 - t], core_in.at[q], csem_s.at[q], csem_r.at[q], other)

    def first_copy(q, b):
        away = pl.multiple_of(b * B + (1 - (dx, dy)[b]) * E8, 16)
        return remote(grads.at[q, t, pl.ds(away, E8)], in1.at[q, b], sem1_s.at[q, b], sem1_r.at[q, b], partner[b])

    def second_copy(q, b):
        away = pl.multiple_of(b * B + (dx, dy)[b] * E8 + (1 - (dy, dx)[b]) * Q, 16)
        return remote(grads.at[q, t, pl.ds(away, Q)], in2.at[q, b], sem2_s.at[q, b], sem2_r.at[q, b], partner[1 - b])

    def step0(q):
        core_copy(q).start()

    def step1(q):
        core_copy(q).wait()
        grads[q, t] = (grads[q, t].astype(F32) + core_in[q].astype(F32)).astype(BF16)
        for b in range(2):
            first_copy(q, b).start()

    def step2(q):
        for b in range(2):
            first_copy(q, b).wait()
            keep = pl.multiple_of(b * B + (dx, dy)[b] * E8, 16)
            grads[q, t, pl.ds(keep, E8)] = (grads[q, t, pl.ds(keep, E8)].astype(F32) + in1[q, b].astype(F32)).astype(BF16)
            second_copy(q, b).start()

    def step3(q):
        for b in range(2):
            second_copy(q, b).wait()
            keep = pl.multiple_of(b * B + (dx, dy)[b] * E8 + (dy, dx)[b] * Q, 16)
            red[q, b * Q:(b + 1) * Q] = (grads[q, t, pl.ds(keep, Q)].astype(F32) + in2[q, b].astype(F32)).astype(BF16)

    def over_z(k):
        to = lax.rem(dz + k, nz)
        return to, (t, to * 4 + lax.rem(d, 4))

    def z_expand(c):
        @pl.when(dz != c)
        def _():
            remote(red.at[c], zin_e.at[dz], zsem_s.at[nz], zsem_r.at[nz], (t, c * 4 + xy)).start()

    def z_attend(a):
        for k in range(1, nz):
            to, who = over_z(k)
            remote(red.at[nz + a, pl.ds(pl.multiple_of(to * rows_a, 16), rows_a)], zin_a.at[a, dz], zsem_s.at[a], zsem_r.at[a], who).start()
        zin_a[a, dz] = red[nz + a, pl.ds(pl.multiple_of(dz * rows_a, 16), rows_a)]

    def all_but_one(ref, count, ss, rs):
        part = ref.at[pl.ds(0, count)]
        pltpu.make_async_copy(part, part, ss).wait()
        pltpu.make_async_copy(part, part, rs).wait()

    def fin_copy(k):
        ref = fin_e if k == 4 else fin_a.at[k]
        return remote(ref.at[t], ref.at[t], fsem_s.at[k], fsem_r.at[k], other)

    def last_expand():
        all_but_one(zin_e, nz - 1, zsem_s.at[nz], zsem_r.at[nz])
        zin_e[dz] = red[dz]
        fin_e[t] = jnp.sum(zin_e[...].astype(F32), 0).astype(BF16)
        fin_copy(4).start()

    def last_attend(a):
        all_but_one(zin_a.at[a], nz - 1, zsem_s.at[a], zsem_r.at[a])
        fin_a[a, t] = jnp.sum(zin_a[a].astype(F32), 0).astype(BF16)
        fin_copy(a).start()

    def put_rows(q, value, lanes):
        for s in range(n):
            z, y, x = s // 4, s // 2 % 2, s % 2
            p = (2 * x + y) * Q + z * rows_a if z < nz // 2 else B + (2 * y + x) * Q + (z - nz // 2) * rows_a
            for h in range(2):
                for src, dst, w in lanes(h):
                    grads[q, h, p:p + rows_a, dst:dst + w] = value[s * rows_a:(s + 1) * rows_a, src:src + w]

    g_low = g_ref[...]
    step = FF // nz
    gn2 = None
    for c in range(nz):
        cols = slice(c * step, (c + 1) * step)
        if c == 0:
            copies["contract"].wait()
        ga = dot_t(g_low, contract[cols, :])
        if c == 0:
            pl.semaphore_wait(pltpu.get_barrier_semaphore(), 2 * n - 1)
            gall[xy, dz] = g_ref[...]
            for k in range(1, nz):
                remote(g_ref, gall.at[xy, dz], gsem.at[0], gsem.at[1], over_z(k)[1]).start()
            copies["gp"].wait()
            copies["n2"].wait()
        pre = (ga[:, None, :] * gp[:, cols].astype(F32).reshape(ex, per, step)).reshape(M, step).astype(BF16)
        rowsums[8 + c:9 + c, :] = jnp.sum(pre.astype(F32), 0, keepdims=True)
        ge = t_dot(pre, n2[...]).astype(BF16)
        for y in range(2):
            for x in range(2):
                at = (2 * y + x) * rows_e
                for h in range(2):
                    grads[c, h, (2 * x + y) * Q:(2 * x + y + 1) * Q, :] = ge[at:at + Q, h * H:(h + 1) * H]
                    grads[c, h, B + (2 * y + x) * Q:B + (2 * y + x + 1) * Q, :] = ge[at + Q:at + 2 * Q, h * H:(h + 1) * H]
        step0(c)
        if c == 0:
            copies["expand"].wait()
        part = dot_t(pre, expand[:, cols])
        gn2 = part if gn2 is None else gn2 + part
        if c >= 1:
            step1(c - 1)
        if c >= 2:
            step2(c - 2)
        if c == 1:
            all_but_one(gall.at[0], nz - 1, gsem.at[0], gsem.at[1])
            for k in range(1, 4):
                remote(gall.at[xy], gall.at[xy], gsem.at[2], gsem.at[3], (t, d - xy + lax.rem(xy + k, 4))).start()
    copies["mid"].wait()
    unit, inv = unit_rows(mid[...])
    gm, gain_two, shift_two = norm_back(gn2, unit, inv, small[1:2, :].astype(F32))
    rowsums[1:2, :] = gain_two
    rowsums[3:4, :] = shift_two
    gm = (gm.reshape(ex, per, D) + grow_ref[...][:, None, :]).reshape(M, D)
    tg_ref[...] = gm
    gb = gm.astype(BF16)
    rowsums[12:13, :] = jnp.sum(gb.astype(F32), 0, keepdims=True)
    step1(nz - 1)
    copies["ctx"].wait()
    put_rows(nz, t_dot(ctx[...], gb).astype(BF16), lambda h: [(h * H, 0, H)])
    step0(nz)
    step2(nz - 2)
    step3(0)
    z_expand(0)
    copies["output"].wait()
    gctx[...] = dot_t(gb, output[...]).astype(BF16)
    step1(nz)
    step3(1)
    z_expand(1)
    even, odd = head_masks()
    lane = lax.broadcasted_iota(jnp.int32, (KW, 2 * HD), 1)
    copies["proj"].wait()
    copies["att"].wait()

    for third in range(3):
        def group(i, _):
            r0 = pl.multiple_of(i * KW, KW)
            for j in (2 * third, 2 * third + 1):
                L = slice(j * 128, (j + 1) * 128)
                gc = gctx[pl.ds(r0, KW), L]
                q = proj[pl.ds(r0, KW), j * 128:(j + 1) * 128]
                kk = split_heads(proj[pl.ds(r0, KW), D + j * 128:D + (j + 1) * 128], even, odd)
                vv = split_heads(proj[pl.ds(r0, KW), 2 * D + j * 128:2 * D + (j + 1) * 128], even, odd)
                a = att[i * PAIRS + j]
                gatt = dot_t(gc, vv)
                prod = gatt * a
                gs = jnp.concatenate([a[:, h * KW:(h + 1) * KW] * (gatt[:, h * KW:(h + 1) * KW] - jnp.sum(prod[:, h * KW:(h + 1) * KW], -1, keepdims=True)) for h in range(2)], axis=1).astype(BF16)
                gv = t_dot(a.astype(BF16), gc)
                gk = t_dot(gs, q) * HD ** -0.5
                gproj[pl.ds(r0, KW), j * 128:(j + 1) * 128] = (dot(gs, kk) * HD ** -0.5).astype(BF16)
                gproj[pl.ds(r0, KW), D + j * 128:D + (j + 1) * 128] = jnp.where(lane < HD, gk[:KW], gk[KW:]).astype(BF16)
                gproj[pl.ds(r0, KW), 2 * D + j * 128:2 * D + (j + 1) * 128] = jnp.where(lane < HD, gv[:KW], gv[KW:]).astype(BF16)
            return 0

        lax.fori_loop(0, M // KW, group, 0)
        if third == 0:
            copies["n1"].wait()
        else:
            step1(nz + third)
        wide3 = jnp.concatenate([gproj[:, part * D + 256 * third:part * D + 256 * (third + 1)] for part in range(3)], axis=1)
        put_rows(nz + 1 + third, t_dot(n1[...], wide3).astype(BF16), lambda h: [(256 * part + 128 * h, 128 * part, 128) for part in range(3)])
        step0(nz + 1 + third)
        if third == 0:
            step2(nz - 1)
            for c in range(2, nz - 1):
                step3(c)
                z_expand(c)
        elif third == 1:
            step2(nz)
            step3(nz - 1)
            z_expand(nz - 1)
        else:
            step3(nz)
            z_attend(0)
            step2(nz + 1)
    rowsums[4:5, :] = jnp.sum(gproj[:, 0:D].astype(F32), 0, keepdims=True)
    rowsums[5:6, :] = rowsums[4:5, :]
    rowsums[6:7, :] = jnp.sum(gproj[:, 2 * D:3 * D].astype(F32), 0, keepdims=True)
    rowsums[7:8, :] = rowsums[6:7, :]
    step1(nz + 3)
    copies["attend"].wait()
    gn1 = dot_t(gproj[...], attend[...])
    step3(nz + 1)
    z_attend(1)
    step2(nz + 2)
    last_expand()
    copies["x"].wait()
    unit, inv = unit_rows(xb[...].astype(F32))
    gx, gain_one, shift_one = norm_back(gn1, unit, inv, small[0:1, :].astype(F32))
    tg_ref[...] += gx
    rowsums[0:1, :] = gain_one
    rowsums[2:3, :] = shift_one
    step2(nz + 3)
    step3(nz + 2)
    z_attend(2)
    sums = rowsums[...]
    parts = [sums[0:8, :]] + [jnp.broadcast_to(sums[8 + r:9 + r, :], (4, D)) for r in range(4)] + [sums[12:13, :], jnp.zeros((128 - 25, D), F32)]
    cols = jnp.transpose(jnp.concatenate(parts, 0))
    at = lax.broadcasted_iota(jnp.int32, (rows_a, 128), 1)
    loss = loss_ref[0:1, :]
    loss_high = loss.astype(BF16)
    loss_mid = (loss - loss_high.astype(F32)).astype(BF16)
    loss_low = (loss - loss_high.astype(F32) - loss_mid.astype(F32)).astype(BF16)
    for s in range(n):
        piece = jnp.where((at < 4) | (at == 24), cols[s * rows_a:(s + 1) * rows_a, :], 0.0)
        r0, first = 2 * s * rows_a % D, 2 * s * rows_a // D * 2
        for c in range(2):
            piece = jnp.where(at == 4 + first + c, cols[r0 + c * rows_a:r0 + (c + 1) * rows_a, :], piece)
        r0, first = 4 * s * rows_a % D, 4 * s * rows_a // D * 4
        for c in range(4):
            piece = jnp.where(at == 8 + first + c, cols[r0 + c * rows_a:r0 + (c + 1) * rows_a, :], piece)
        for k, v in enumerate((loss_high, loss_mid, loss_low)):
            piece = jnp.where(at == 25 + k, v.astype(F32), piece)
        s_out[s] = piece.astype(BF16)

    def small_send(k, _):
        to = lax.rem(d + k, n)
        remote(s_out.at[to], s_in.at[d], ssem.at[0], ssem.at[1], (t, to)).start()
        return 0

    lax.fori_loop(1, n, small_send, 0)
    s_in[d] = s_out[d]

    last_attend(0)
    step3(nz + 3)
    z_attend(3)
    all_but_one(gall, 3, gsem.at[2], gsem.at[3])
    wide = ag_ref.shape[2]
    pc[...] = t_dot(ag_ref[...].reshape(n * ex, wide), gall[...].reshape(n * ex, D)).astype(BF16)
    pc_copy = remote(pc, pc_in, fsem_s.at[5], fsem_r.at[5], other)
    pc_copy.start()
    last_attend(1)
    all_but_one(s_in, n - 1, ssem.at[0], ssem.at[1])
    s_fin[t] = jnp.sum(s_in[...].astype(F32), 0)
    s_copy = remote(s_fin.at[t], s_fin.at[t], fsem_s.at[6], fsem_r.at[6], other)
    s_copy.start()
    last_attend(2)
    pc_copy.wait()
    oc_ref[...] = pc[...].astype(F32) + pc_in[...].astype(F32)
    fin_copy(4).wait()
    for h in range(2):
        oe_ref[:, h * H:(h + 1) * H] = fin_e[h].astype(F32)
    s_copy.wait()
    os_ref[...] = s_fin[0] + s_fin[1]
    last_attend(3)
    fin_copy(0).wait()
    for h in range(2):
        oo_ref[:, h * H:(h + 1) * H] = fin_a[0, h].astype(F32)
    for third in range(3):
        fin_copy(1 + third).wait()
        for h in range(2):
            for part in range(3):
                lo = part * D + 256 * third + 128 * h
                oa_ref[:, lo:lo + 128] = fin_a[1 + third, h, :, 128 * part:128 * (part + 1)].astype(F32)


def text_backward(per, n, x, small, g, grow, ag, loss, saved, attend, output, expand, contract):
    n1, proj, att, ctx, mid, n2, gp = saved
    M = x.shape[0]
    ex, wide, nz = g.shape[0], ag.shape[2], n // 4
    rows_e, rows_a, H = FF // n, D // n, D // 2
    S = jax.ShapeDtypeStruct
    V = lambda *shape: pltpu.VMEM(shape, BF16)
    like = lambda a: pltpu.VMEM(a.shape, a.dtype)
    outs = [S((M, D), F32), S((rows_e, D), F32), S((rows_a, 3 * D), F32), S((rows_a, D), F32), S((rows_a, 128), F32), S((wide, D), F32)]
    q = nz + 4
    dma = pltpu.SemaphoreType.DMA
    held = (x, n1, proj, att, ctx, mid, n2, gp, contract, expand, output, attend)
    scratch = [like(a) for a in held] + [V(M, D), V(M, 3 * D), pltpu.VMEM((16, D), F32)]
    scratch += [V(q, 2, D, H), V(q, D, H), V(q, 2, D // 4, H), V(q, 2, D // 8, H), V(q, D // 4, H), V(nz, D // 4, H), V(4, nz, rows_a, H), V(2, D // 4, H), V(4, 2, rows_a, H),
                V(n, rows_a, 128), V(n, rows_a, 128), pltpu.VMEM((2, rows_a, 128), F32), V(4, nz, ex, D), V(wide, D), V(wide, D)]
    scratch += [dma((12,)), dma((q,)), dma((q,)), dma((q, 2)), dma((q, 2)), dma((q, 2)), dma((q, 2)), dma((nz + 4,)), dma((nz + 4,)), dma((7,)), dma((7,)), dma((4,)), dma((2,))]
    return pl.pallas_call(
        functools.partial(back_kernel, per, n), out_shape=outs, in_specs=[VM] * 5 + [ANY] * 12, out_specs=[VM] * 6, scratch_shapes=scratch,
        compiler_params=pltpu.CompilerParams(collective_id=1, has_side_effects=True, vmem_limit_bytes=63 << 20),
        name="text_backward",
    )(small, g, grow, ag, loss, x, n1, proj, att, ctx, mid, n2, gp, contract, expand, output, attend)


def finish_kernel(n, per, counts_ref, tg, oe, oa, oo, os, oc, loss_ref, tg_out, gains, shifts, attend, attend_bias, output, output_bias, expand_t, expand_bias, contract, contract_bias):
    d = lax.axis_index("dp")
    rows_e, rows_a = FF // n, D // n
    loss_ref[...] = (os[0:1, 25:26] + os[0:1, 26:27] + os[0:1, 27:28]) / jnp.sum(counts_ref[...].astype(F32).reshape(1, -1), -1, keepdims=True)
    tg_out[...] = tg[...]
    attend[...] = oa[...]
    output[...] = oo[...]
    expand_t[...] = oe[...]
    contract[...] = oc[0:rows_e, :]
    rows = jnp.transpose(jnp.concatenate([os[...], jnp.zeros((128 - rows_a, 128), F32)], 0))
    gains[...] = rows[0:2, 0:rows_a]
    shifts[...] = rows[2:4, 0:rows_a]

    def joined(pieces):
        total = None
        for c, piece in enumerate(pieces):
            line = jnp.concatenate([jnp.broadcast_to(piece, (8, 128)), jnp.zeros((8, 128), F32)], 1)
            line = pltpu.roll(line, c * rows_a, 1) if c else line
            total = line if total is None else total + line
        return total[0:1, 0:len(pieces) * rows_a].reshape(len(pieces) * rows_a)

    attend_bias[...] = joined([rows[4 + c:5 + c] + rows[6 + c:7 + c] for c in range(2)])
    expand_bias[...] = joined([rows[8 + c:9 + c] + rows[12 + c:13 + c] + rows[16 + c:17 + c] + rows[20 + c:21 + c] for c in range(4)])
    output_bias[...] = joined([rows[24:25]])
    line = pltpu.roll(jnp.broadcast_to(oc[rows_e:rows_e + 1, :], (8, D)), lax.rem(D - d * rows_a, D), 1)
    contract_bias[...] = line[0:1, 0:rows_a].reshape(rows_a)


def finish(n, per, counts, *parts):
    tg, oe, oa, oo = parts[:4]
    S = jax.ShapeDtypeStruct
    rows_e, rows_a = FF // n, D // n
    f = lambda *shape: S(shape, F32)
    outs = [f(1, 1), f(*tg.shape), f(2, rows_a), f(2, rows_a), f(*oa.shape), f(2 * rows_a), f(*oo.shape), f(rows_a), f(*oe.shape), f(4 * rows_a), f(rows_e, D), f(rows_a)]
    return pl.pallas_call(functools.partial(finish_kernel, n, per), out_shape=outs, in_specs=[VM] * 7, out_specs=[VM] * 12,
                          compiler_params=pltpu.CompilerParams(vmem_limit_bytes=60 << 20), name="finish")(counts, *parts)


def on_device(n, text_tokens, image_tokens, counts, caption_group, *params):
    per_dev = text_tokens.shape[0]
    plan = ((0, per_dev // 4), (per_dev // 2, per_dev // 8), (per_dev * 3 // 4, per_dev // 8))
    image_params, text_params = params[:10], params[10:]
    ex, per, _ = text_tokens.shape
    g, grow, loss, ag, *saved = front(n, text_tokens, image_tokens, counts, caption_group, image_params, text_params, plan)
    parts = text_backward(per, n, text_tokens.reshape(ex * per, D), text_params[0], g, grow, ag, loss, saved, *(text_params[k] for k in (2, 4, 6, 8)))
    out = list(finish(n, per, counts, *parts))
    out[0] = out[0].reshape(())
    out[1] = out[1].reshape(ex, per, D)
    out[8] = out[8].T
    return tuple(out)


HEADS = 12
HEAD_DIM = 64


def multiply(left, right):
    return jnp.dot(left, right, preferred_element_type=jnp.float32)


def left_inner(left, right):
    return lax.dot_general(
        left, right, (((0,), (0,)), ((), ())), preferred_element_type=jnp.float32
    )


def right_inner(left, right):
    return lax.dot_general(
        left, right, (((1,), (1,)), ((), ())), preferred_element_type=jnp.float32
    )


def normalize(rows_in, gain, shift):
    centre = rows_in - jnp.mean(rows_in, -1, keepdims=True)
    inverse_std = lax.rsqrt(jnp.mean(centre * centre, -1, keepdims=True) + NORM_EPS)
    unit_rows = centre * inverse_std
    return (unit_rows * gain + shift, unit_rows, inverse_std)


def normalize_back(grad_rows, unit_rows, inverse_std, gain):
    grad_unit = grad_rows * gain
    grad_in = inverse_std * (
        grad_unit
        - jnp.mean(grad_unit, -1, keepdims=True)
        - unit_rows * jnp.mean(grad_unit * unit_rows, -1, keepdims=True)
    )
    return (grad_in, jnp.sum(grad_rows * unit_rows, 0), jnp.sum(grad_rows, 0))


def plain_forward(tokens, params):
    (
        gains,
        shifts,
        attend,
        attend_bias,
        output,
        output_bias,
        expand,
        expand_bias,
        contract,
        contract_bias,
    ) = params
    examples, row_count, features = tokens.shape
    inputs = tokens.astype(jnp.float32).reshape(examples * row_count, features)
    normed, unit_one, inverse_one = normalize(
        inputs, gains[0].astype(jnp.float32), shifts[0].astype(jnp.float32)
    )
    normed_one = normed.astype(jnp.bfloat16)
    full_bias = jnp.concatenate(
        [attend_bias[:features], jnp.zeros_like(output_bias), attend_bias[features:]]
    ).astype(jnp.float32)
    projected = (multiply(normed_one, attend) + full_bias).astype(jnp.bfloat16)
    projected = projected.reshape(examples, row_count, 3, HEADS, HEAD_DIM)
    queries = projected[:, :, 0]
    keys = projected[:, :, 1]
    values = projected[:, :, 2]
    scores = jnp.einsum(
        "erhd,eshd->ehrs", queries, keys, preferred_element_type=jnp.float32
    ) * HEAD_DIM ** (-0.5)
    attention = jax.nn.softmax(scores, axis=-1)
    attention_low = attention.astype(jnp.bfloat16)
    context = jnp.einsum(
        "ehrs,eshd->erhd", attention_low, values, preferred_element_type=jnp.float32
    )
    context = context.astype(jnp.bfloat16).reshape(examples * row_count, features)
    middle = inputs + (multiply(context, output) + output_bias.astype(jnp.float32))
    normed, unit_two, inverse_two = normalize(
        middle, gains[1].astype(jnp.float32), shifts[1].astype(jnp.float32)
    )
    normed_two = normed.astype(jnp.bfloat16)
    pre_gelu = multiply(normed_two, expand) + expand_bias.astype(jnp.float32)
    activated = jax.nn.gelu(pre_gelu).astype(jnp.bfloat16)
    block_out = middle + (multiply(activated, contract) + contract_bias.astype(jnp.float32))
    pooled = jnp.mean(block_out.reshape(examples, row_count, features), axis=1)
    inverse_norm = lax.rsqrt(jnp.sum(pooled * pooled, -1, keepdims=True) + EMBED_EPS)
    embedding = pooled * inverse_norm
    saved = (
        normed_one,
        unit_one,
        inverse_one,
        queries,
        keys,
        values,
        attention,
        attention_low,
        context,
        unit_two,
        inverse_two,
        normed_two,
        pre_gelu,
        activated,
        embedding,
        inverse_norm,
    )
    return (embedding, saved)


def backward(params, saved, grad_embedding, row_count):
    (
        gains,
        shifts,
        attend,
        attend_bias,
        output,
        output_bias,
        expand,
        expand_bias,
        contract,
        contract_bias,
    ) = params
    (
        normed_one,
        unit_one,
        inverse_one,
        queries,
        keys,
        values,
        attention,
        attention_low,
        context,
        unit_two,
        inverse_two,
        normed_two,
        pre_gelu,
        activated,
        embedding,
        inverse_norm,
    ) = saved
    examples, features = embedding.shape
    grad_pooled = inverse_norm * (
        grad_embedding - embedding * jnp.sum(grad_embedding * embedding, -1, keepdims=True)
    )
    grad_rows = jnp.broadcast_to(
        (grad_pooled / row_count)[:, None, :], (examples, row_count, features)
    ).reshape(examples * row_count, features)
    grad_mlp = grad_rows.astype(jnp.bfloat16)
    grad_contract = left_inner(activated, grad_mlp)
    grad_contract_bias = jnp.sum(grad_mlp.astype(jnp.float32), 0)
    grad_activated = right_inner(grad_mlp, contract)
    gelu_back = jax.vjp(jax.nn.gelu, pre_gelu)[1]
    grad_pre = gelu_back(grad_activated)[0].astype(jnp.bfloat16)
    grad_expand = left_inner(normed_two, grad_pre)
    grad_expand_bias = jnp.sum(grad_pre.astype(jnp.float32), 0)
    grad_normed_two = right_inner(grad_pre, expand)
    grad_middle, gain_two, shift_two = normalize_back(
        grad_normed_two, unit_two, inverse_two, gains[1].astype(jnp.float32)
    )
    grad_middle = grad_middle + grad_rows
    grad_branch = grad_middle.astype(jnp.bfloat16)
    grad_output = left_inner(context, grad_branch)
    grad_output_bias = jnp.sum(grad_branch.astype(jnp.float32), 0)
    grad_context = (
        right_inner(grad_branch, output)
        .astype(jnp.bfloat16)
        .reshape(examples, row_count, HEADS, HEAD_DIM)
    )
    grad_attention = jnp.einsum(
        "erhd,eshd->ehrs", grad_context, values, preferred_element_type=jnp.float32
    )
    grad_values = jnp.einsum(
        "ehrs,erhd->eshd", attention_low, grad_context, preferred_element_type=jnp.float32
    )
    grad_scores = (
        attention * (grad_attention - jnp.sum(grad_attention * attention, -1, keepdims=True))
    ).astype(jnp.bfloat16)
    grad_queries = jnp.einsum(
        "ehrs,eshd->erhd", grad_scores, keys, preferred_element_type=jnp.float32
    ) * HEAD_DIM ** (-0.5)
    grad_keys = jnp.einsum(
        "ehrs,erhd->eshd", grad_scores, queries, preferred_element_type=jnp.float32
    ) * HEAD_DIM ** (-0.5)
    grad_projected = (
        jnp.stack([grad_queries, grad_keys, grad_values], 2)
        .astype(jnp.bfloat16)
        .reshape(examples * row_count, 3 * features)
    )
    grad_attend = left_inner(normed_one, grad_projected)
    column_sums = jnp.sum(grad_projected.astype(jnp.float32), 0)
    grad_attend_bias = jnp.concatenate([column_sums[:features], column_sums[2 * features :]])
    grad_normed_one = right_inner(grad_projected, attend)
    grad_inputs, gain_one, shift_one = normalize_back(
        grad_normed_one, unit_one, inverse_one, gains[0].astype(jnp.float32)
    )
    grad_inputs = grad_inputs + grad_middle
    grads = (
        jnp.stack([gain_one, gain_two]),
        jnp.stack([shift_one, shift_two]),
        grad_attend,
        grad_attend_bias,
        grad_output,
        grad_output_bias,
        grad_expand,
        grad_expand_bias,
        grad_contract,
        grad_contract_bias,
    )
    return (grad_inputs.reshape(examples, row_count, features), grads)


def masked_softmax(logits, allowed, live_rows):
    filled = jnp.where(allowed, logits, -1e30)
    largest = jnp.max(filled, -1, keepdims=True)
    weights = jnp.exp(filled - largest) * allowed.astype(jnp.float32)
    safe_total = jnp.sum(weights, -1, keepdims=True) + (1.0 - live_rows)[:, None]
    return (weights / safe_total, largest[:, 0] + jnp.log(safe_total[:, 0]))


def plain_on_device(
    text_tokens,
    image_tokens,
    counts,
    caption_group,
    image_gains,
    image_shifts,
    image_attend,
    image_attend_bias,
    image_output,
    image_output_bias,
    image_expand,
    image_expand_bias,
    image_contract,
    image_contract_bias,
    text_gains,
    text_shifts,
    text_attend,
    text_attend_bias,
    text_output,
    text_output_bias,
    text_expand,
    text_expand_bias,
    text_contract,
    text_contract_bias,
):
    image_params = (
        image_gains,
        image_shifts,
        image_attend,
        image_attend_bias,
        image_output,
        image_output_bias,
        image_expand,
        image_expand_bias,
        image_contract,
        image_contract_bias,
    )
    text_params = (
        text_gains,
        text_shifts,
        text_attend,
        text_attend_bias,
        text_output,
        text_output_bias,
        text_expand,
        text_expand_bias,
        text_contract,
        text_contract_bias,
    )
    image_embedding, image_saved = plain_forward(image_tokens, image_params)
    text_embedding, text_saved = plain_forward(text_tokens, text_params)
    image_low = image_embedding.astype(jnp.bfloat16)
    text_low = text_embedding.astype(jnp.bfloat16)
    all_images, all_texts = (
        lax.all_gather(image_low, ("tower", "dp"), axis=0, tiled=True),
        lax.all_gather(text_low, ("tower", "dp"), axis=0, tiled=True),
    )
    per_device = image_low.shape[0]
    everyone = all_images.shape[0]
    device_rank = lax.axis_index(("tower", "dp"))
    positions = jnp.arange(everyone, dtype=jnp.int32)
    owned = device_rank * per_device + jnp.arange(per_device, dtype=jnp.int32)
    live_all = positions % per_device < jnp.repeat(counts, per_device, total_repeat_length=everyone)
    live_own = lax.dynamic_slice_in_dim(live_all, device_rank * per_device, per_device)
    group_own = lax.dynamic_slice_in_dim(caption_group, device_rank * per_device, per_device)
    diagonal = owned[:, None] == positions[None, :]
    allowed = (
        live_own[:, None]
        & live_all[None, :]
        & ((group_own[:, None] != caption_group[None, :]) | diagonal)
    )
    live_rows = live_own.astype(jnp.float32)
    diagonal_float = diagonal.astype(jnp.float32)
    forward_logits = right_inner(text_low, all_images) * LOGIT_SCALE
    backward_logits = right_inner(image_low, all_texts) * LOGIT_SCALE
    forward_probs, forward_lse = masked_softmax(forward_logits, allowed, live_rows)
    backward_probs, backward_lse = masked_softmax(backward_logits, allowed, live_rows)
    forward_terms = forward_lse - jnp.sum(forward_logits * diagonal_float, -1)
    backward_terms = backward_lse - jnp.sum(backward_logits * diagonal_float, -1)
    local_sum = 0.5 * (jnp.sum(live_rows * forward_terms) + jnp.sum(live_rows * backward_terms))
    loss_sum = lax.psum(local_sum, ("tower", "dp"))
    loss_value = loss_sum / jnp.sum(counts).astype(jnp.float32)
    forward_coef = (0.5 * live_rows[:, None] * (forward_probs - diagonal_float)).astype(
        jnp.bfloat16
    )
    grad_embedding = LOGIT_SCALE * multiply(forward_coef, all_images)
    lse_everyone = lax.all_gather(backward_lse, ("tower", "dp"), axis=0, tiled=True)
    shifted = jnp.where(allowed, forward_logits - lse_everyone[None, :], -1e30)
    live_columns = live_all.astype(jnp.float32)
    column_coef = (0.5 * live_columns[None, :] * (jnp.exp(shifted) - diagonal_float)).astype(
        jnp.bfloat16
    )
    grad_embedding = grad_embedding + LOGIT_SCALE * multiply(column_coef, all_images)
    text_grad, grads = backward(text_params, text_saved, grad_embedding, text_tokens.shape[1])
    shards = (
        lax.psum_scatter(grads[0], "dp", scatter_dimension=1, tiled=True),
        lax.psum_scatter(grads[1], "dp", scatter_dimension=1, tiled=True),
        lax.psum_scatter(grads[2], "dp", scatter_dimension=0, tiled=True),
        lax.psum_scatter(grads[3], "dp", scatter_dimension=0, tiled=True),
        lax.psum_scatter(grads[4], "dp", scatter_dimension=0, tiled=True),
        lax.psum_scatter(grads[5], "dp", scatter_dimension=0, tiled=True),
        lax.psum_scatter(grads[6], "dp", scatter_dimension=1, tiled=True),
        lax.psum_scatter(grads[7], "dp", scatter_dimension=0, tiled=True),
        lax.psum_scatter(grads[8], "dp", scatter_dimension=0, tiled=True),
        lax.psum_scatter(grads[9], "dp", scatter_dimension=0, tiled=True),
    )
    totals = (
        lax.psum(shards[0].astype(jnp.bfloat16), "tower").astype(jnp.float32),
        lax.psum(shards[1].astype(jnp.bfloat16), "tower").astype(jnp.float32),
        lax.psum(shards[2].astype(jnp.bfloat16), "tower").astype(jnp.float32),
        lax.psum(shards[3].astype(jnp.bfloat16), "tower").astype(jnp.float32),
        lax.psum(shards[4].astype(jnp.bfloat16), "tower").astype(jnp.float32),
        lax.psum(shards[5].astype(jnp.bfloat16), "tower").astype(jnp.float32),
        lax.psum(shards[6].astype(jnp.bfloat16), "tower").astype(jnp.float32),
        lax.psum(shards[7].astype(jnp.bfloat16), "tower").astype(jnp.float32),
        lax.psum(shards[8].astype(jnp.bfloat16), "tower").astype(jnp.float32),
        lax.psum(shards[9].astype(jnp.bfloat16), "tower").astype(jnp.float32),
    )
    return (
        loss_value,
        text_grad,
        totals[0],
        totals[1],
        totals[2],
        totals[3],
        totals[4],
        totals[5],
        totals[6],
        totals[7],
        totals[8],
        totals[9],
    )


def solution(mesh):
    n = mesh.shape["dp"]
    whole, both = P(), P(("tower", "dp"), None, None)
    fits = FF // n * 4 == D and n % 8 == 0
    body = functools.partial(on_device, n) if fits else plain_on_device
    out_specs = (P(), both, P(None, "dp"), P(None, "dp"), P("dp", None), P("dp"), P("dp", None), P("dp"), P(None, "dp"), P("dp"), P("dp", None), P("dp"))
    return jax.shard_map(body, mesh=mesh, in_specs=(both, both) + (whole,) * 22, out_specs=out_specs, check_vma=False)
```

```python
import functools
import jax
import jax.numpy as jnp
import numpy as np
from jax import lax
from jax.experimental import pallas as pl
from jax.experimental.pallas import tpu as pltpu
from jax.sharding import PartitionSpec as P

F32, BF16 = jnp.float32, jnp.bfloat16
D, HD, FF = 768, 64, 3072
PAIRS = D // (2 * HD)
KW = 128
NORM_EPS, EMBED_EPS, LOGIT_SCALE = 1e-5, 1e-6, 64.0
NEG = -1e30
ANY = pl.BlockSpec(memory_space=pl.ANY)
VM = pl.BlockSpec(memory_space=pltpu.VMEM)
GELU_C, GELU_A = float(np.sqrt(2 / np.pi)), 0.044715


def dot(a, b):
    return jnp.dot(a, b, preferred_element_type=F32)


def dot_t(a, b):
    return lax.dot_general(a, b, (((1,), (1,)), ((), ())), preferred_element_type=F32)


def t_dot(a, b):
    return lax.dot_general(a, b, (((0,), (0,)), ((), ())), preferred_element_type=F32)


def unit_rows(v):
    centre = v - jnp.mean(v, -1, keepdims=True)
    inv = lax.rsqrt(jnp.mean(centre * centre, -1, keepdims=True) + NORM_EPS)
    return centre * inv, inv


def head_masks():
    lane = lax.broadcasted_iota(jnp.int32, (1, 2 * HD), 1)
    even = (lane < HD).astype(F32)
    return even.astype(BF16), (1.0 - even).astype(BF16)


def pair_mask(rows, per, real):
    r = lax.broadcasted_iota(jnp.int32, (rows, 2 * KW), 0)
    c = lax.broadcasted_iota(jnp.int32, (rows, 2 * KW), 1) % KW
    ok = (r // per == c // per) & (c % per < real) & (c < rows)
    return jnp.where(ok, 0.0, NEG).astype(F32)


def split_heads(a, even, odd):
    return jnp.concatenate([a * even, a * odd], axis=0)


def softmax_half(s):
    m = jnp.max(s, -1, keepdims=True)
    p = jnp.exp(s - m)
    return p / jnp.sum(p, -1, keepdims=True)


def exp_half(s):
    return jnp.exp(s - jnp.max(s, -1, keepdims=True)).astype(BF16)


def block_forward(x, rows, groups, small, W, wait, done, proj, ctx, mask, att_out, keep):
    attend, output, expand, contract = W
    unit, _ = unit_rows(x)
    n1 = (unit * small[0:1, :] + small[2:3, :]).astype(BF16)
    keep("n1", n1)
    wait("attend")
    M = rows * groups
    step = 256
    for c in range(3 * D // step):
        y = dot(n1, attend[:, c * step:(c + 1) * step])
        if c * step < D:
            y = y + small[4:5, c * step:(c + 1) * step]
        elif c * step >= 2 * D:
            y = y + small[5:6, c * step - 2 * D:(c + 1) * step - 2 * D]
        proj[0:M, c * step:(c + 1) * step] = y.astype(BF16)
    done("attend")
    keep("proj", None)
    even, odd = head_masks()
    ones = split_heads(jnp.ones((KW, 2 * HD), BF16), even, odd)

    def group(g, _):
        r0 = pl.multiple_of(g * rows, 16)
        for j in range(PAIRS):
            lanes = slice(j * 2 * HD, (j + 1) * 2 * HD)
            q = proj[pl.ds(r0, rows), j * 128:(j + 1) * 128]
            kk = split_heads(proj[pl.ds(r0, KW), D + j * 128:D + (j + 1) * 128], even, odd)
            vv = split_heads(proj[pl.ds(r0, KW), 2 * D + j * 128:2 * D + (j + 1) * 128], even, odd)
            s = dot_t(q, kk) * HD ** -0.5 + mask[...]
            if att_out is None:
                p = jnp.concatenate([exp_half(s[:, :KW]), exp_half(s[:, KW:])], axis=1)
                both = dot(p, jnp.concatenate([vv, ones], axis=1))
                ctx[pl.ds(r0, rows), lanes] = (both[:, :128] / both[:, 128:]).astype(BF16)
            else:
                a = jnp.concatenate([softmax_half(s[:, :KW]), softmax_half(s[:, KW:])], axis=1)
                att_out[g * PAIRS + j] = a
                ctx[pl.ds(r0, rows), lanes] = dot(a.astype(BF16), vv).astype(BF16)
        return 0

    lax.fori_loop(0, groups, group, 0)
    wait("output")
    middle = x + (dot(ctx[0:M, :], output[...]) + small[6:7, :])
    done("output")
    keep("middle", middle)
    unit, _ = unit_rows(middle)
    n2 = (unit * small[1:2, :] + small[3:4, :]).astype(BF16)
    keep("n2", n2)
    wait("expand")
    acc = middle + small[11:12, :]
    step = 768
    for c in range(FF // step):
        pre = dot(n2, expand[:, c * step:(c + 1) * step]) + small[7 + c:8 + c, :]
        sq = pre * pre
        th = jnp.tanh(pre * (GELU_C + GELU_C * GELU_A * sq))
        cdf = 0.5 + 0.5 * th
        act = (pre * cdf).astype(BF16)
        keep("act", act, c, pre, sq, th, cdf)
        if c == 0:
            wait("contract")
        acc = acc + dot(act, contract[c * step:(c + 1) * step, :])
    done("expand")
    done("contract")
    return acc


def embed_rows(pooled):
    inv = lax.rsqrt(jnp.sum(pooled * pooled, -1, keepdims=True) + EMBED_EPS)
    return pooled * inv, inv


MESH_ID = pl.DeviceIdType.MESH


def place():
    return lax.axis_index("tower"), lax.axis_index("dp")


def greet(n):
    t, d = place()
    barrier = pltpu.get_barrier_semaphore()

    def one(k, _):
        who = (lax.rem(t + k // n, 2), lax.rem(d + lax.rem(k, n), n))
        pl.semaphore_signal(barrier, inc=1, device_id=who, device_id_type=MESH_ID)
        return 0

    lax.fori_loop(1, 2 * n, one, 0)


def spread(n, src, dst, send, recv):
    t, d = place()

    def one(k, _):
        pltpu.make_async_remote_copy(src_ref=src, dst_ref=dst.at[d], send_sem=send, recv_sem=recv,
                                     device_id=(t, lax.rem(d + k, n)), device_id_type=MESH_ID).start()
        return 0

    lax.fori_loop(1, n, one, 0)


def settle(n, dst, send, recv):
    part = dst.at[pl.ds(0, n - 1)]
    pltpu.make_async_copy(part, part, send).wait()
    pltpu.make_async_copy(part, part, recv).wait()


def contrast_rows(fl, allowed, live_rows):
    filled = jnp.where(allowed, fl, NEG)
    largest = jnp.max(filled, -1, keepdims=True)
    weights = jnp.where(allowed, jnp.exp(filled - largest), 0.0)
    total = jnp.sum(weights, -1, keepdims=True) + (1.0 - live_rows)
    return weights / total, largest + jnp.log(total)


def contrast_rows(fl, allowed, live_rows):
    filled = jnp.where(allowed, fl, NEG)
    largest = jnp.max(filled, -1, keepdims=True)
    weights = jnp.where(allowed, jnp.exp(filled - largest), 0.0)
    total = jnp.sum(weights, -1, keepdims=True) + (1.0 - live_rows)
    return weights / total, largest + jnp.log(total)


def fill_small(small, refs):
    gains, shifts, attend_bias, output_bias, expand_bias, contract_bias = refs
    small[0:2, :] = gains[...].astype(F32)
    small[2:4, :] = shifts[...].astype(F32)
    row = 4
    for ref in (attend_bias, output_bias, expand_bias, contract_bias):
        for k in range(ref.shape[0] // D):
            small[row:row + 1, :] = ref[pl.ds(k * D, D)].astype(F32).reshape(1, D)
            row += 1


def front_kernel(per_text, real, plan, n, *refs):
    it = iter(refs)
    take = lambda k: [next(it) for _ in range(k)]
    x_ref, counts_ref, group_ref = take(3)
    image_small, text_small = take(6), take(6)
    image_w, text_w = take(4), take(4)
    tokens_h, = take(1)
    g_ref, grow_ref, loss_ref, ag_ref = take(4)
    saved_h = take(7)
    weights = take(4)
    saved = take(7)
    tokens, by_place, xs, proj_i, ctx_i, mask_t, mask_i, small_t, small_i = take(9)
    lows_t, asum, emb_ref, own_rows, lse, = take(5)
    lows_i = take(len(plan))
    load, out_sem, tok_sem, ssem, rsem, osem_s, osem_r = take(7)
    t, d = place()
    greet(n)
    names = ("attend", "output", "expand", "contract")
    copies = {}
    for k, name in enumerate(names):
        copies["text", name] = pltpu.make_async_copy(text_w[k], weights[k], load.at[k])
        copies["text", name].start()
        copies["image", name] = pltpu.make_async_copy(image_w[k], weights[k], load.at[4 + k])
    token_copy = pltpu.make_async_copy(tokens_h, tokens, tok_sem)
    token_copy.start()
    n1, proj, att, ctx, mid, n2, gp = saved
    outs = dict(zip(("n1", "proj", "att", "ctx", "mid", "n2", "gp"), [pltpu.make_async_copy(v, h, out_sem.at[k]) for k, (v, h) in enumerate(zip(saved, saved_h))]))
    fill_small(small_t, text_small)
    fill_small(small_i, image_small)
    M = x_ref.shape[0]
    ex = M // per_text
    mask_t[...] = pair_mask(KW, per_text, per_text)

    def keep(name, value, *extra):
        if name == "n1":
            n1[...] = value
            outs["n1"].start()
        elif name == "proj":
            outs["proj"].start()
        elif name == "middle":
            mid[...] = value
            for o in ("att", "ctx", "mid"):
                outs[o].start()
        elif name == "n2":
            n2[...] = value
            outs["n2"].start()
        else:
            c, pre, sq, th, cdf = extra
            w = value.shape[1]
            asum[c] = jnp.sum(value.astype(F32).reshape(ex, per_text, w), 1).astype(BF16)
            gp[:, c * w:(c + 1) * w] = (cdf + (0.5 * GELU_C) * pre * (1.0 - th * th) * (1.0 + (3 * GELU_A) * sq)).astype(BF16)

    out = block_forward(x_ref[...].astype(F32), KW, M // KW, small_t, weights, lambda name: copies["text", name].wait(), lambda name: copies["image", name].start(),
                        proj, ctx, mask_t, att, keep)
    outs["gp"].start()
    emb, inv = embed_rows(jnp.sum(out.reshape(ex, per_text, D), 1) * (1.0 / per_text))
    emb_ref[0] = emb
    emb_ref[1] = jnp.broadcast_to(inv, emb.shape)
    lows_t[t, d] = emb.astype(BF16)

    def send(src, dst, s, r, who):
        return pltpu.make_async_remote_copy(src_ref=src, dst_ref=dst, send_sem=s, recv_sem=r, device_id=who, device_id_type=MESH_ID)

    pl.semaphore_wait(pltpu.get_barrier_semaphore(), 2 * n - 1)
    spread(n, lows_t.at[t, d], lows_t.at[t], ssem.at[0], rsem.at[0])
    nz, dz, xy = n // 4, d // 4, lax.rem(d, 4)
    for k in range(1, nz):
        to = lax.rem(dz + k, nz)
        send(asum.at[to], ag_ref.at[dz], ssem.at[1], rsem.at[1], (t, to * 4 + xy)).start()
    ag_ref[dz] = asum[dz]

    def pass_over(buf, k):
        return send(buf.at[t], buf.at[t], osem_s.at[k], osem_r.at[k], (1 - t, d))

    per = -(-real // 8) * 8
    rows = 2 * per
    xs[...] = jnp.zeros_like(xs)
    proj_i[proj_i.shape[0] - 16:, :] = jnp.zeros((16, 3 * D), BF16)
    mask_i[...] = pair_mask(rows, per, real)
    bufs = [lows_t] + lows_i
    slots = [0] + [2 + k for k in range(len(plan))]

    def arrive(k):
        settle(n, bufs[k].at[t], ssem.at[slots[k]], rsem.at[slots[k]])
        pass_over(bufs[k], k).start()

    for k, (first, pairs) in enumerate(plan):
        def wait(name):
            if k == 0:
                copies["image", name].wait()
        if k == 0:
            token_copy.wait()
        rows_k, ex_k = rows * pairs, 2 * pairs
        held = ex // 2
        if first % held == 0:
            for v in range(D // 128):
                by_place[v] = tokens[:, first:first + held, v * 128:(v + 1) * 128].astype(F32).reshape(real * held, 128)
        for e in range(ex_k):
            for lo in range(0, real, 8):
                count = min(8, real - lo)
                for v in range(D // 128):
                    xs[e * per + lo:e * per + lo + count, v * 128:(v + 1) * 128] = by_place[v, pl.ds(first % held + e + lo * held, count, stride=held), :]
        out = block_forward(xs[0:rows_k, :], rows, pairs, small_i, weights, wait, lambda name: None, proj_i, ctx_i, mask_i, None, lambda *a: None)
        out = out.reshape(ex_k, per, D)
        ok = lax.broadcasted_iota(jnp.int32, (ex_k, per, D), 1) < real
        emb, _ = embed_rows(jnp.sum(jnp.where(ok, out, 0.0), 1) * (1.0 / real))
        lows_i[k][t, d] = emb.astype(BF16)
        spread(n, lows_i[k].at[t, d], lows_i[k].at[t], ssem.at[slots[k + 1]], rsem.at[slots[k + 1]])
        arrive(k)
        if k > 0:
            pass_over(bufs[k - 1], k - 1).wait()

    every, nd = 2 * n * ex, 2 * n
    rank = t * n + d
    counts_row = jnp.broadcast_to(counts_ref[...].astype(F32).reshape(1, nd), (8, nd)).astype(BF16)

    def live_of(device, row):
        hot = (lax.broadcasted_iota(jnp.int32, (nd, device.shape[1]), 0) == device).astype(F32).astype(BF16)
        return (row.astype(F32) < dot(counts_row, hot)[0:1, :]).astype(F32), hot

    natural = lax.broadcasted_iota(jnp.int32, (1, every), 1)
    group_row = group_ref[...].astype(F32).reshape(1, every)
    live_row, _ = live_of(natural // ex, natural % ex)
    text_group = jnp.transpose(jnp.broadcast_to(group_row, (128, every)))[:, 0:1]
    text_live = jnp.transpose(jnp.broadcast_to(live_row, (128, every)))[:, 0:1]
    own_text = lows_t[t, d]
    groups, lives, places = [], [], []
    at = 0
    for k, (first, pairs) in enumerate(plan):
        ek = 2 * pairs
        w = nd * ek
        col = lax.broadcasted_iota(jnp.int32, (1, w), 1)
        device, row = col // ek, first + col % ek
        live, hot = live_of(device, row)
        pick = (lax.broadcasted_iota(jnp.int32, (every, w), 0) == device * ex + row).astype(F32).astype(BF16)
        groups.append(dot(jnp.broadcast_to(group_row, (8, every)).astype(BF16), pick)[0:1, :])
        lives.append(live)
        places.append(device * ex + row)
    texts = lows_t[...].reshape(every, D)

    def chunk_logits(k, at):
        w = nd * 2 * plan[k][1]
        images = lows_i[k][...].reshape(w, D)
        own_rows[:, at:at + w] = dot_t(own_text, images) * LOGIT_SCALE
        for lo in range(0, w, 256):
            part = slice(lo, min(lo + 256, w))
            logits = dot_t(texts, images[part]) * LOGIT_SCALE
            same = lax.broadcasted_iota(jnp.int32, logits.shape, 0) == places[k][:, part]
            allowed = (text_live * lives[k][:, part] > 0.0) & ((text_group != groups[k][:, part]) | same)
            filled = jnp.where(allowed, logits, NEG)
            largest = jnp.max(filled, 0, keepdims=True)
            total = jnp.sum(jnp.where(allowed, jnp.exp(filled - largest), 0.0), 0, keepdims=True) + (1.0 - lives[k][:, part])
            lse[:, at + lo:at + lo + logits.shape[1]] = jnp.broadcast_to(largest + jnp.log(total), (8, logits.shape[1]))
        return at + w

    for k in range(len(plan)):
        if k == len(plan) - 1:
            arrive(k + 1)
            pass_over(bufs[k + 1], k + 1).wait()
        elif k == len(plan) - 2:
            pass_over(bufs[k + 1], k + 1).wait()
        at = chunk_logits(k, at)
    column_group, column_live, column_place = (jnp.concatenate(v, 1) for v in (groups, lives, places))
    diag_b = column_place == lax.broadcasted_iota(jnp.int32, (ex, every), 0) + rank * ex
    diagonal = diag_b.astype(F32)
    image_lse = lse[0:1, :]
    fl = own_rows[...]
    live_own = jnp.sum(diagonal * column_live, -1, keepdims=True)
    group_own = jnp.sum(diagonal * column_group, -1, keepdims=True)
    allowed = (live_own * column_live > 0.0) & ((group_own != column_group) | diag_b)
    probs, text_lse = contrast_rows(fl, allowed, live_own)
    own_diag = fl * diagonal
    terms = live_own * (text_lse - jnp.sum(own_diag, -1, keepdims=True)) + jnp.sum(diagonal * (live_own * image_lse) - live_own * own_diag, -1, keepdims=True)
    loss_ref[...] = jnp.broadcast_to(0.5 * jnp.sum(terms, 0, keepdims=True), loss_ref.shape)
    forward_coef = (0.5 * live_own * (probs - diagonal)).astype(BF16)
    shifted = jnp.where(allowed, jnp.exp(jnp.where(allowed, fl - image_lse, NEG)), 0.0)
    column_coef = (0.5 * column_live * (shifted - diagonal)).astype(BF16)
    coefs = jnp.concatenate([forward_coef, column_coef], 0)
    at, grad = 0, None
    for k, (first, pairs) in enumerate(plan):
        w = nd * 2 * pairs
        part = dot(coefs[:, at:at + w], lows_i[k][...].reshape(w, D))
        grad = part if grad is None else grad + part
        at += w
    grad = LOGIT_SCALE * grad[0:ex] + LOGIT_SCALE * grad[ex:]
    emb = emb_ref[0]
    pooled = emb_ref[1] * (grad - emb * jnp.sum(grad * emb, -1, keepdims=True))
    rows_out = pooled * (1.0 / per_text)
    grow_ref[...] = rows_out
    g_ref[...] = rows_out.astype(BF16)
    settle(nz, ag_ref, ssem.at[1], rsem.at[1])
    for o in outs.values():
        o.wait()


def front(n, text_tokens, image_tokens, counts, group, image_params, text_params, plan):
    ex, per, _ = text_tokens.shape
    real = image_tokens.shape[1]
    M = ex * per
    nz = n // 4
    S = jax.ShapeDtypeStruct
    small_of = lambda p: [p[0], p[1], p[3], p[5], p[7], p[9]]
    weights_of = lambda p: [p[2], p[4], p[6], p[8]]
    kept = [S((M, D), BF16), S((M, 3 * D), BF16), S((M // KW * PAIRS, KW, 2 * KW), F32), S((M, D), BF16), S((M, D), F32), S((M, D), BF16), S((M, FF), BF16)]
    like = lambda a: pltpu.VMEM(a.shape, a.dtype)
    per_i = -(-real // 8) * 8
    big = max(p for _, p in plan) * 2 * per_i
    scratch = [like(a) for a in weights_of(text_params)] + [like(a) for a in kept]
    scratch += [pltpu.VMEM((real, ex, D), BF16), pltpu.VMEM((D // 128, real * ex // 2, 128), F32), pltpu.VMEM((big, D), F32), pltpu.VMEM((big + 16, 3 * D), BF16), pltpu.VMEM((big, D), BF16),
                pltpu.VMEM((KW, 2 * KW), F32), pltpu.VMEM((2 * per_i, 2 * KW), F32), pltpu.VMEM((16, D), F32), pltpu.VMEM((16, D), F32)]
    scratch += [pltpu.VMEM((2, n, ex, D), BF16), pltpu.VMEM((nz, ex, FF // nz), BF16), pltpu.VMEM((2, ex, D), F32), pltpu.VMEM((ex, 2 * n * ex), F32), pltpu.VMEM((8, 2 * n * ex), F32)]
    scratch += [pltpu.VMEM((2, n, 2 * p, D), BF16) for _, p in plan]
    dma = pltpu.SemaphoreType.DMA
    k = len(plan)
    scratch += [dma((8,)), dma((7,)), dma, dma((k + 2,)), dma((k + 2,)), dma((k + 1,)), dma((k + 1,))]
    return pl.pallas_call(
        functools.partial(front_kernel, per, real, plan, n),
        out_shape=[S((ex, D), BF16), S((ex, D), F32), S((8, 128), F32), S((nz, ex, FF // nz), BF16)] + kept,
        in_specs=[VM] * 15 + [ANY] * 9, out_specs=[VM] * 4 + [ANY] * 7, scratch_shapes=scratch,
        compiler_params=pltpu.CompilerParams(collective_id=0, has_side_effects=True, vmem_limit_bytes=63 << 20),
        name="forward_and_loss",
    )(text_tokens.reshape(M, D), counts, group, *small_of(image_params), *small_of(text_params), *weights_of(image_params), *weights_of(text_params), image_tokens.transpose(1, 0, 2))


def norm_back(grad, unit, inv, gain):
    gu = grad * gain
    out = inv * (gu - jnp.mean(gu, -1, keepdims=True) - unit * jnp.mean(gu * unit, -1, keepdims=True))
    return out, jnp.sum(grad * unit, 0, keepdims=True), jnp.sum(grad, 0, keepdims=True)


def back_kernel(per, n, small, g_ref, grow_ref, ag_ref, loss_ref, x_h, n1_h, proj_h, att_h, ctx_h, mid_h, n2_h, gp_h, contract_h, expand_h, output_h, attend_h,
                tg_ref, oe_ref, oa_ref, oo_ref, os_ref, oc_ref,
                xb, n1, proj, att, ctx, mid, n2, gp, contract, expand, output, attend, gctx, gproj, rowsums,
                grads, core_in, in1, in2, red, zin_e, zin_a, fin_e, fin_a, fin_c, s_out, s_in, s_fin, gall,
                load, csem_s, csem_r, sem1_s, sem1_r, sem2_s, sem2_r, zsem_s, zsem_r, fsem_s, fsem_r, gsem, ssem):
    t, d = place()
    dx, dy, dz, nz = lax.rem(d, 2), lax.rem(d // 2, 2), d // 4, n // 4
    xy = lax.rem(d, 4)
    other = (1 - t, d)
    partner = ((t, d + 1 - 2 * dx), (t, d + 2 - 4 * dy))
    greet(n)
    copies = {}
    for k, (name, h, v) in enumerate((("contract", contract_h, contract), ("gp", gp_h, gp), ("n2", n2_h, n2), ("expand", expand_h, expand), ("mid", mid_h, mid), ("ctx", ctx_h, ctx),
                                      ("output", output_h, output), ("proj", proj_h, proj), ("att", att_h, att), ("n1", n1_h, n1), ("attend", attend_h, attend), ("x", x_h, xb))):
        copies[name] = pltpu.make_async_copy(h, v, load.at[k])
        copies[name].start()
    M = xb.shape[0]
    ex = M // per
    rows_e, rows_a, H = FF // n, D // n, D // 2
    B = D // 2
    Q, E8 = B // 4, B // 2

    def remote(src, dst, ss, rs, who):
        return pltpu.make_async_remote_copy(src_ref=src, dst_ref=dst, send_sem=ss, recv_sem=rs, device_id=who, device_id_type=MESH_ID)

    def core_copy(q):
        return remote(grads.at[q, 1 - t], core_in.at[q], csem_s.at[q], csem_r.at[q], other)

    def first_copy(q, b):
        away = pl.multiple_of(b * B + (1 - (dx, dy)[b]) * E8, 16)
        return remote(grads.at[q, t, pl.ds(away, E8)], in1.at[q, b], sem1_s.at[q, b], sem1_r.at[q, b], partner[b])

    def second_copy(q, b):
        away = pl.multiple_of(b * B + (dx, dy)[b] * E8 + (1 - (dy, dx)[b]) * Q, 16)
        return remote(grads.at[q, t, pl.ds(away, Q)], in2.at[q, b], sem2_s.at[q, b], sem2_r.at[q, b], partner[1 - b])

    def step0(q):
        core_copy(q).start()

    def step1(q):
        core_copy(q).wait()
        grads[q, t] = (grads[q, t].astype(F32) + core_in[q].astype(F32)).astype(BF16)
        for b in range(2):
            first_copy(q, b).start()

    def step2(q):
        for b in range(2):
            first_copy(q, b).wait()
            keep = pl.multiple_of(b * B + (dx, dy)[b] * E8, 16)
            grads[q, t, pl.ds(keep, E8)] = (grads[q, t, pl.ds(keep, E8)].astype(F32) + in1[q, b].astype(F32)).astype(BF16)
            second_copy(q, b).start()

    def step3(q):
        for b in range(2):
            second_copy(q, b).wait()
            keep = pl.multiple_of(b * B + (dx, dy)[b] * E8 + (dy, dx)[b] * Q, 16)
            red[q, b * Q:(b + 1) * Q] = (grads[q, t, pl.ds(keep, Q)].astype(F32) + in2[q, b].astype(F32)).astype(BF16)

    def over_z(k):
        to = lax.rem(dz + k, nz)
        return to, (t, to * 4 + lax.rem(d, 4))

    def z_expand(c):
        @pl.when(dz != c)
        def _():
            remote(red.at[c], zin_e.at[dz], zsem_s.at[nz], zsem_r.at[nz], (t, c * 4 + xy)).start()

    def z_attend(a):
        for k in range(1, nz):
            to, who = over_z(k)
            remote(red.at[nz + a, pl.ds(pl.multiple_of(to * rows_a, 16), rows_a)], zin_a.at[a, dz], zsem_s.at[a], zsem_r.at[a], who).start()
        zin_a[a, dz] = red[nz + a, pl.ds(pl.multiple_of(dz * rows_a, 16), rows_a)]

    def all_but_one(ref, count, ss, rs):
        part = ref.at[pl.ds(0, count)]
        pltpu.make_async_copy(part, part, ss).wait()
        pltpu.make_async_copy(part, part, rs).wait()

    def fin_copy(k):
        ref = fin_a.at[k] if k < 4 else (fin_e, fin_c)[k - 4]
        return remote(ref.at[t], ref.at[t], fsem_s.at[k], fsem_r.at[k], other)

    def last_expand():
        all_but_one(zin_e, nz - 1, zsem_s.at[nz], zsem_r.at[nz])
        zin_e[dz] = red[dz]
        fin_e[t] = jnp.sum(zin_e[...].astype(F32), 0).astype(BF16)
        fin_copy(4).start()

    def last_attend(a):
        all_but_one(zin_a.at[a], nz - 1, zsem_s.at[a], zsem_r.at[a])
        fin_a[a, t] = jnp.sum(zin_a[a].astype(F32), 0).astype(BF16)
        fin_copy(a).start()

    def put_shards(q, value):
        for y in range(2):
            for x in range(2):
                at = (2 * y + x) * rows_e
                for h in range(2):
                    grads[q, h, (2 * x + y) * Q:(2 * x + y + 1) * Q, :] = value[at:at + Q, h * H:(h + 1) * H]
                    grads[q, h, B + (2 * y + x) * Q:B + (2 * y + x + 1) * Q, :] = value[at + Q:at + 2 * Q, h * H:(h + 1) * H]

    def put_rows(q, value, lanes):
        for s in range(n):
            z, y, x = s // 4, s // 2 % 2, s % 2
            p = (2 * x + y) * Q + z * rows_a if z < nz // 2 else B + (2 * y + x) * Q + (z - nz // 2) * rows_a
            for h in range(2):
                for src, dst, w in lanes(h):
                    grads[q, h, p:p + rows_a, dst:dst + w] = value[s * rows_a:(s + 1) * rows_a, src:src + w]

    g_low = g_ref[...]
    rowsums[13:14, :] = per * jnp.sum(g_low.astype(F32), 0, keepdims=True)
    step = FF // nz
    gn2 = None
    for c in range(nz):
        cols = slice(c * step, (c + 1) * step)
        if c == 0:
            copies["contract"].wait()
        ga = dot_t(g_low, contract[cols, :])
        if c == 0:
            pl.semaphore_wait(pltpu.get_barrier_semaphore(), 2 * n - 1)
            gall[dz] = g_ref[...]
            for k in range(1, nz):
                remote(g_ref, gall.at[dz], gsem.at[0], gsem.at[1], over_z(k)[1]).start()
            copies["gp"].wait()
            copies["n2"].wait()
        pre = (ga[:, None, :] * gp[:, cols].astype(F32).reshape(ex, per, step)).reshape(M, step).astype(BF16)
        rowsums[8 + c:9 + c, :] = jnp.sum(pre.astype(F32), 0, keepdims=True)
        ge = t_dot(pre, n2[...]).astype(BF16)
        put_shards(c, ge)
        step0(c)
        if c == 0:
            copies["expand"].wait()
        part = dot_t(pre, expand[:, cols])
        gn2 = part if gn2 is None else gn2 + part
        if c >= 1:
            step1(c - 1)
        if c >= 2:
            step2(c - 2)
        if c == 1:
            all_but_one(gall, nz - 1, gsem.at[0], gsem.at[1])
            put_shards(nz + 4, t_dot(ag_ref[...].reshape(nz * ex, FF // nz), gall[...].reshape(nz * ex, D)).astype(BF16))
            step0(nz + 4)
        elif c == 2:
            step1(nz + 4)
        elif c == 3:
            step2(nz + 4)
    copies["mid"].wait()
    unit, inv = unit_rows(mid[...])
    gm, gain_two, shift_two = norm_back(gn2, unit, inv, small[1:2, :].astype(F32))
    rowsums[1:2, :] = gain_two
    rowsums[3:4, :] = shift_two
    gm = (gm.reshape(ex, per, D) + grow_ref[...][:, None, :]).reshape(M, D)
    tg_ref[...] = gm
    gb = gm.astype(BF16)
    rowsums[12:13, :] = jnp.sum(gb.astype(F32), 0, keepdims=True)
    step1(nz - 1)
    copies["ctx"].wait()
    put_rows(nz, t_dot(ctx[...], gb).astype(BF16), lambda h: [(h * H, 0, H)])
    step0(nz)
    step2(nz - 2)
    step3(0)
    z_expand(0)
    copies["output"].wait()
    gctx[...] = dot_t(gb, output[...]).astype(BF16)
    step1(nz)
    step3(1)
    z_expand(1)
    step3(nz + 4)
    fin_c[t] = red[nz + 4]
    fin_copy(5).start()
    even, odd = head_masks()
    lane = lax.broadcasted_iota(jnp.int32, (KW, 2 * HD), 1)
    copies["proj"].wait()
    copies["att"].wait()

    for third in range(3):
        def group(i, _):
            r0 = pl.multiple_of(i * KW, KW)
            for j in (2 * third, 2 * third + 1):
                L = slice(j * 128, (j + 1) * 128)
                gc = gctx[pl.ds(r0, KW), L]
                q = proj[pl.ds(r0, KW), j * 128:(j + 1) * 128]
                kk = split_heads(proj[pl.ds(r0, KW), D + j * 128:D + (j + 1) * 128], even, odd)
                vv = split_heads(proj[pl.ds(r0, KW), 2 * D + j * 128:2 * D + (j + 1) * 128], even, odd)
                a = att[i * PAIRS + j]
                gatt = dot_t(gc, vv)
                prod = gatt * a
                gs = jnp.concatenate([a[:, h * KW:(h + 1) * KW] * (gatt[:, h * KW:(h + 1) * KW] - jnp.sum(prod[:, h * KW:(h + 1) * KW], -1, keepdims=True)) for h in range(2)], axis=1).astype(BF16)
                gv = t_dot(a.astype(BF16), gc)
                gk = t_dot(gs, q) * HD ** -0.5
                gproj[pl.ds(r0, KW), j * 128:(j + 1) * 128] = (dot(gs, kk) * HD ** -0.5).astype(BF16)
                gproj[pl.ds(r0, KW), D + j * 128:D + (j + 1) * 128] = jnp.where(lane < HD, gk[:KW], gk[KW:]).astype(BF16)
                gproj[pl.ds(r0, KW), 2 * D + j * 128:2 * D + (j + 1) * 128] = jnp.where(lane < HD, gv[:KW], gv[KW:]).astype(BF16)
            return 0

        lax.fori_loop(0, M // KW, group, 0)
        if third == 0:
            copies["n1"].wait()
        else:
            step1(nz + third)
        wide3 = jnp.concatenate([gproj[:, part * D + 256 * third:part * D + 256 * (third + 1)] for part in range(3)], axis=1)
        put_rows(nz + 1 + third, t_dot(n1[...], wide3).astype(BF16), lambda h: [(256 * part + 128 * h, 128 * part, 128) for part in range(3)])
        step0(nz + 1 + third)
        if third == 0:
            step2(nz - 1)
            for c in range(2, nz - 1):
                step3(c)
                z_expand(c)
        elif third == 1:
            step2(nz)
            step3(nz - 1)
            z_expand(nz - 1)
        else:
            step3(nz)
            z_attend(0)
            step2(nz + 1)
    rowsums[4:5, :] = jnp.sum(gproj[:, 0:D].astype(F32), 0, keepdims=True)
    rowsums[5:6, :] = rowsums[4:5, :]
    rowsums[6:7, :] = jnp.sum(gproj[:, 2 * D:3 * D].astype(F32), 0, keepdims=True)
    rowsums[7:8, :] = rowsums[6:7, :]
    step1(nz + 3)
    copies["attend"].wait()
    gn1 = dot_t(gproj[...], attend[...])
    step3(nz + 1)
    z_attend(1)
    step2(nz + 2)
    last_expand()
    copies["x"].wait()
    unit, inv = unit_rows(xb[...].astype(F32))
    gx, gain_one, shift_one = norm_back(gn1, unit, inv, small[0:1, :].astype(F32))
    tg_ref[...] += gx
    rowsums[0:1, :] = gain_one
    rowsums[2:3, :] = shift_one
    step2(nz + 3)
    step3(nz + 2)
    z_attend(2)
    sums = rowsums[...]
    parts = [sums[0:8, :]] + [jnp.broadcast_to(sums[8 + r:9 + r, :], (4, D)) for r in range(4)] + [sums[12:13, :], jnp.zeros((3, D), F32), sums[13:14, :], jnp.zeros((128 - 29, D), F32)]
    cols = jnp.transpose(jnp.concatenate(parts, 0))
    at = lax.broadcasted_iota(jnp.int32, (rows_a, 128), 1)
    loss = loss_ref[0:1, :]
    loss_high = loss.astype(BF16)
    loss_mid = (loss - loss_high.astype(F32)).astype(BF16)
    loss_low = (loss - loss_high.astype(F32) - loss_mid.astype(F32)).astype(BF16)
    for s in range(n):
        piece = jnp.where((at < 4) | (at == 24) | (at == 28), cols[s * rows_a:(s + 1) * rows_a, :], 0.0)
        r0, first = 2 * s * rows_a % D, 2 * s * rows_a // D * 2
        for c in range(2):
            piece = jnp.where(at == 4 + first + c, cols[r0 + c * rows_a:r0 + (c + 1) * rows_a, :], piece)
        r0, first = 4 * s * rows_a % D, 4 * s * rows_a // D * 4
        for c in range(4):
            piece = jnp.where(at == 8 + first + c, cols[r0 + c * rows_a:r0 + (c + 1) * rows_a, :], piece)
        for k, v in enumerate((loss_high, loss_mid, loss_low)):
            piece = jnp.where(at == 25 + k, v.astype(F32), piece)
        s_out[s] = piece.astype(BF16)

    def small_send(k, _):
        to = lax.rem(d + k, n)
        remote(s_out.at[to], s_in.at[d], ssem.at[0], ssem.at[1], (t, to)).start()
        return 0

    lax.fori_loop(1, n, small_send, 0)
    s_in[d] = s_out[d]

    last_attend(0)
    step3(nz + 3)
    z_attend(3)
    last_attend(1)
    all_but_one(s_in, n - 1, ssem.at[0], ssem.at[1])
    s_fin[t] = jnp.sum(s_in[...].astype(F32), 0)
    s_copy = remote(s_fin.at[t], s_fin.at[t], fsem_s.at[6], fsem_r.at[6], other)
    s_copy.start()
    last_attend(2)
    fin_copy(4).wait()
    fin_copy(5).wait()
    for h in range(2):
        oc_ref[:, h * H:(h + 1) * H] = fin_c[h].astype(F32)
        oe_ref[:, h * H:(h + 1) * H] = fin_e[h].astype(F32)
    s_copy.wait()
    os_ref[...] = s_fin[0] + s_fin[1]
    last_attend(3)
    fin_copy(0).wait()
    for h in range(2):
        oo_ref[:, h * H:(h + 1) * H] = fin_a[0, h].astype(F32)
    for third in range(3):
        fin_copy(1 + third).wait()
        for h in range(2):
            for part in range(3):
                lo = part * D + 256 * third + 128 * h
                oa_ref[:, lo:lo + 128] = fin_a[1 + third, h, :, 128 * part:128 * (part + 1)].astype(F32)


def text_backward(per, n, x, small, g, grow, ag, loss, saved, attend, output, expand, contract):
    n1, proj, att, ctx, mid, n2, gp = saved
    M = x.shape[0]
    ex, nz = g.shape[0], n // 4
    rows_e, rows_a, H = FF // n, D // n, D // 2
    S = jax.ShapeDtypeStruct
    V = lambda *shape: pltpu.VMEM(shape, BF16)
    like = lambda a: pltpu.VMEM(a.shape, a.dtype)
    outs = [S((M, D), F32), S((rows_e, D), F32), S((rows_a, 3 * D), F32), S((rows_a, D), F32), S((rows_a, 128), F32), S((rows_e, D), F32)]
    q = nz + 5
    dma = pltpu.SemaphoreType.DMA
    held = (x, n1, proj, att, ctx, mid, n2, gp, contract, expand, output, attend)
    scratch = [like(a) for a in held] + [V(M, D), V(M, 3 * D), pltpu.VMEM((16, D), F32)]
    scratch += [V(q, 2, D, H), V(q, D, H), V(q, 2, D // 4, H), V(q, 2, D // 8, H), V(q, D // 4, H), V(nz, D // 4, H), V(4, nz, rows_a, H), V(2, D // 4, H), V(4, 2, rows_a, H), V(2, D // 4, H),
                V(n, rows_a, 128), V(n, rows_a, 128), pltpu.VMEM((2, rows_a, 128), F32), V(nz, ex, D)]
    scratch += [dma((12,)), dma((q,)), dma((q,)), dma((q, 2)), dma((q, 2)), dma((q, 2)), dma((q, 2)), dma((nz + 4,)), dma((nz + 4,)), dma((7,)), dma((7,)), dma((2,)), dma((2,))]
    return pl.pallas_call(
        functools.partial(back_kernel, per, n), out_shape=outs, in_specs=[VM] * 5 + [ANY] * 12, out_specs=[VM] * 6, scratch_shapes=scratch,
        compiler_params=pltpu.CompilerParams(collective_id=1, has_side_effects=True, vmem_limit_bytes=63 << 20),
        name="text_backward",
    )(small, g, grow, ag, loss, x, n1, proj, att, ctx, mid, n2, gp, contract, expand, output, attend)


def finish_kernel(n, per, counts_ref, tg, oe, oa, oo, os, oc, loss_ref, tg_out, gains, shifts, attend, attend_bias, output, output_bias, expand_t, expand_bias, contract, contract_bias):
    rows_a = D // n
    loss_ref[...] = (os[0:1, 25:26] + os[0:1, 26:27] + os[0:1, 27:28]) / jnp.sum(counts_ref[...].astype(F32).reshape(1, -1), -1, keepdims=True)
    tg_out[...] = tg[...]
    attend[...] = oa[...]
    output[...] = oo[...]
    expand_t[...] = oe[...]
    contract[...] = oc[...]
    rows = jnp.transpose(jnp.concatenate([os[...], jnp.zeros((128 - rows_a, 128), F32)], 0))
    gains[...] = rows[0:2, 0:rows_a]
    shifts[...] = rows[2:4, 0:rows_a]

    def joined(pieces):
        total = None
        for c, piece in enumerate(pieces):
            line = jnp.concatenate([jnp.broadcast_to(piece, (8, 128)), jnp.zeros((8, 128), F32)], 1)
            line = pltpu.roll(line, c * rows_a, 1) if c else line
            total = line if total is None else total + line
        return total[0:1, 0:len(pieces) * rows_a].reshape(len(pieces) * rows_a)

    attend_bias[...] = joined([rows[4 + c:5 + c] + rows[6 + c:7 + c] for c in range(2)])
    expand_bias[...] = joined([rows[8 + c:9 + c] + rows[12 + c:13 + c] + rows[16 + c:17 + c] + rows[20 + c:21 + c] for c in range(4)])
    output_bias[...] = joined([rows[24:25]])
    contract_bias[...] = joined([rows[28:29]])


def finish(n, per, counts, *parts):
    tg, oe, oa, oo = parts[:4]
    S = jax.ShapeDtypeStruct
    rows_e, rows_a = FF // n, D // n
    f = lambda *shape: S(shape, F32)
    outs = [f(1, 1), f(*tg.shape), f(2, rows_a), f(2, rows_a), f(*oa.shape), f(2 * rows_a), f(*oo.shape), f(rows_a), f(*oe.shape), f(4 * rows_a), f(rows_e, D), f(rows_a)]
    return pl.pallas_call(functools.partial(finish_kernel, n, per), out_shape=outs, in_specs=[VM] * 7, out_specs=[VM] * 12,
                          compiler_params=pltpu.CompilerParams(vmem_limit_bytes=60 << 20), name="finish")(counts, *parts)


def on_device(n, text_tokens, image_tokens, counts, caption_group, *params):
    per_dev = text_tokens.shape[0]
    plan = ((0, per_dev // 4), (per_dev // 2, per_dev // 8), (per_dev * 3 // 4, per_dev // 8))
    image_params, text_params = params[:10], params[10:]
    ex, per, _ = text_tokens.shape
    g, grow, loss, ag, *saved = front(n, text_tokens, image_tokens, counts, caption_group, image_params, text_params, plan)
    parts = text_backward(per, n, text_tokens.reshape(ex * per, D), text_params[0], g, grow, ag, loss, saved, *(text_params[k] for k in (2, 4, 6, 8)))
    out = list(finish(n, per, counts, *parts))
    out[0] = out[0].reshape(())
    out[1] = out[1].reshape(ex, per, D)
    out[8] = out[8].T
    return tuple(out)


HEADS = 12
HEAD_DIM = 64


def multiply(left, right):
    return jnp.dot(left, right, preferred_element_type=jnp.float32)


def left_inner(left, right):
    return lax.dot_general(
        left, right, (((0,), (0,)), ((), ())), preferred_element_type=jnp.float32
    )


def right_inner(left, right):
    return lax.dot_general(
        left, right, (((1,), (1,)), ((), ())), preferred_element_type=jnp.float32
    )


def normalize(rows_in, gain, shift):
    centre = rows_in - jnp.mean(rows_in, -1, keepdims=True)
    inverse_std = lax.rsqrt(jnp.mean(centre * centre, -1, keepdims=True) + NORM_EPS)
    unit_rows = centre * inverse_std
    return (unit_rows * gain + shift, unit_rows, inverse_std)


def normalize_back(grad_rows, unit_rows, inverse_std, gain):
    grad_unit = grad_rows * gain
    grad_in = inverse_std * (
        grad_unit
        - jnp.mean(grad_unit, -1, keepdims=True)
        - unit_rows * jnp.mean(grad_unit * unit_rows, -1, keepdims=True)
    )
    return (grad_in, jnp.sum(grad_rows * unit_rows, 0), jnp.sum(grad_rows, 0))


def plain_forward(tokens, params):
    (
        gains,
        shifts,
        attend,
        attend_bias,
        output,
        output_bias,
        expand,
        expand_bias,
        contract,
        contract_bias,
    ) = params
    examples, row_count, features = tokens.shape
    inputs = tokens.astype(jnp.float32).reshape(examples * row_count, features)
    normed, unit_one, inverse_one = normalize(
        inputs, gains[0].astype(jnp.float32), shifts[0].astype(jnp.float32)
    )
    normed_one = normed.astype(jnp.bfloat16)
    full_bias = jnp.concatenate(
        [attend_bias[:features], jnp.zeros_like(output_bias), attend_bias[features:]]
    ).astype(jnp.float32)
    projected = (multiply(normed_one, attend) + full_bias).astype(jnp.bfloat16)
    projected = projected.reshape(examples, row_count, 3, HEADS, HEAD_DIM)
    queries = projected[:, :, 0]
    keys = projected[:, :, 1]
    values = projected[:, :, 2]
    scores = jnp.einsum(
        "erhd,eshd->ehrs", queries, keys, preferred_element_type=jnp.float32
    ) * HEAD_DIM ** (-0.5)
    attention = jax.nn.softmax(scores, axis=-1)
    attention_low = attention.astype(jnp.bfloat16)
    context = jnp.einsum(
        "ehrs,eshd->erhd", attention_low, values, preferred_element_type=jnp.float32
    )
    context = context.astype(jnp.bfloat16).reshape(examples * row_count, features)
    middle = inputs + (multiply(context, output) + output_bias.astype(jnp.float32))
    normed, unit_two, inverse_two = normalize(
        middle, gains[1].astype(jnp.float32), shifts[1].astype(jnp.float32)
    )
    normed_two = normed.astype(jnp.bfloat16)
    pre_gelu = multiply(normed_two, expand) + expand_bias.astype(jnp.float32)
    activated = jax.nn.gelu(pre_gelu).astype(jnp.bfloat16)
    block_out = middle + (multiply(activated, contract) + contract_bias.astype(jnp.float32))
    pooled = jnp.mean(block_out.reshape(examples, row_count, features), axis=1)
    inverse_norm = lax.rsqrt(jnp.sum(pooled * pooled, -1, keepdims=True) + EMBED_EPS)
    embedding = pooled * inverse_norm
    saved = (
        normed_one,
        unit_one,
        inverse_one,
        queries,
        keys,
        values,
        attention,
        attention_low,
        context,
        unit_two,
        inverse_two,
        normed_two,
        pre_gelu,
        activated,
        embedding,
        inverse_norm,
    )
    return (embedding, saved)


def backward(params, saved, grad_embedding, row_count):
    (
        gains,
        shifts,
        attend,
        attend_bias,
        output,
        output_bias,
        expand,
        expand_bias,
        contract,
        contract_bias,
    ) = params
    (
        normed_one,
        unit_one,
        inverse_one,
        queries,
        keys,
        values,
        attention,
        attention_low,
        context,
        unit_two,
        inverse_two,
        normed_two,
        pre_gelu,
        activated,
        embedding,
        inverse_norm,
    ) = saved
    examples, features = embedding.shape
    grad_pooled = inverse_norm * (
        grad_embedding - embedding * jnp.sum(grad_embedding * embedding, -1, keepdims=True)
    )
    grad_rows = jnp.broadcast_to(
        (grad_pooled / row_count)[:, None, :], (examples, row_count, features)
    ).reshape(examples * row_count, features)
    grad_mlp = grad_rows.astype(jnp.bfloat16)
    grad_contract = left_inner(activated, grad_mlp)
    grad_contract_bias = jnp.sum(grad_mlp.astype(jnp.float32), 0)
    grad_activated = right_inner(grad_mlp, contract)
    gelu_back = jax.vjp(jax.nn.gelu, pre_gelu)[1]
    grad_pre = gelu_back(grad_activated)[0].astype(jnp.bfloat16)
    grad_expand = left_inner(normed_two, grad_pre)
    grad_expand_bias = jnp.sum(grad_pre.astype(jnp.float32), 0)
    grad_normed_two = right_inner(grad_pre, expand)
    grad_middle, gain_two, shift_two = normalize_back(
        grad_normed_two, unit_two, inverse_two, gains[1].astype(jnp.float32)
    )
    grad_middle = grad_middle + grad_rows
    grad_branch = grad_middle.astype(jnp.bfloat16)
    grad_output = left_inner(context, grad_branch)
    grad_output_bias = jnp.sum(grad_branch.astype(jnp.float32), 0)
    grad_context = (
        right_inner(grad_branch, output)
        .astype(jnp.bfloat16)
        .reshape(examples, row_count, HEADS, HEAD_DIM)
    )
    grad_attention = jnp.einsum(
        "erhd,eshd->ehrs", grad_context, values, preferred_element_type=jnp.float32
    )
    grad_values = jnp.einsum(
        "ehrs,erhd->eshd", attention_low, grad_context, preferred_element_type=jnp.float32
    )
    grad_scores = (
        attention * (grad_attention - jnp.sum(grad_attention * attention, -1, keepdims=True))
    ).astype(jnp.bfloat16)
    grad_queries = jnp.einsum(
        "ehrs,eshd->erhd", grad_scores, keys, preferred_element_type=jnp.float32
    ) * HEAD_DIM ** (-0.5)
    grad_keys = jnp.einsum(
        "ehrs,erhd->eshd", grad_scores, queries, preferred_element_type=jnp.float32
    ) * HEAD_DIM ** (-0.5)
    grad_projected = (
        jnp.stack([grad_queries, grad_keys, grad_values], 2)
        .astype(jnp.bfloat16)
        .reshape(examples * row_count, 3 * features)
    )
    grad_attend = left_inner(normed_one, grad_projected)
    column_sums = jnp.sum(grad_projected.astype(jnp.float32), 0)
    grad_attend_bias = jnp.concatenate([column_sums[:features], column_sums[2 * features :]])
    grad_normed_one = right_inner(grad_projected, attend)
    grad_inputs, gain_one, shift_one = normalize_back(
        grad_normed_one, unit_one, inverse_one, gains[0].astype(jnp.float32)
    )
    grad_inputs = grad_inputs + grad_middle
    grads = (
        jnp.stack([gain_one, gain_two]),
        jnp.stack([shift_one, shift_two]),
        grad_attend,
        grad_attend_bias,
        grad_output,
        grad_output_bias,
        grad_expand,
        grad_expand_bias,
        grad_contract,
        grad_contract_bias,
    )
    return (grad_inputs.reshape(examples, row_count, features), grads)


def masked_softmax(logits, allowed, live_rows):
    filled = jnp.where(allowed, logits, -1e30)
    largest = jnp.max(filled, -1, keepdims=True)
    weights = jnp.exp(filled - largest) * allowed.astype(jnp.float32)
    safe_total = jnp.sum(weights, -1, keepdims=True) + (1.0 - live_rows)[:, None]
    return (weights / safe_total, largest[:, 0] + jnp.log(safe_total[:, 0]))


def plain_on_device(
    text_tokens,
    image_tokens,
    counts,
    caption_group,
    image_gains,
    image_shifts,
    image_attend,
    image_attend_bias,
    image_output,
    image_output_bias,
    image_expand,
    image_expand_bias,
    image_contract,
    image_contract_bias,
    text_gains,
    text_shifts,
    text_attend,
    text_attend_bias,
    text_output,
    text_output_bias,
    text_expand,
    text_expand_bias,
    text_contract,
    text_contract_bias,
):
    image_params = (
        image_gains,
        image_shifts,
        image_attend,
        image_attend_bias,
        image_output,
        image_output_bias,
        image_expand,
        image_expand_bias,
        image_contract,
        image_contract_bias,
    )
    text_params = (
        text_gains,
        text_shifts,
        text_attend,
        text_attend_bias,
        text_output,
        text_output_bias,
        text_expand,
        text_expand_bias,
        text_contract,
        text_contract_bias,
    )
    image_embedding, image_saved = plain_forward(image_tokens, image_params)
    text_embedding, text_saved = plain_forward(text_tokens, text_params)
    image_low = image_embedding.astype(jnp.bfloat16)
    text_low = text_embedding.astype(jnp.bfloat16)
    all_images, all_texts = (
        lax.all_gather(image_low, ("tower", "dp"), axis=0, tiled=True),
        lax.all_gather(text_low, ("tower", "dp"), axis=0, tiled=True),
    )
    per_device = image_low.shape[0]
    everyone = all_images.shape[0]
    device_rank = lax.axis_index(("tower", "dp"))
    positions = jnp.arange(everyone, dtype=jnp.int32)
    owned = device_rank * per_device + jnp.arange(per_device, dtype=jnp.int32)
    live_all = positions % per_device < jnp.repeat(counts, per_device, total_repeat_length=everyone)
    live_own = lax.dynamic_slice_in_dim(live_all, device_rank * per_device, per_device)
    group_own = lax.dynamic_slice_in_dim(caption_group, device_rank * per_device, per_device)
    diagonal = owned[:, None] == positions[None, :]
    allowed = (
        live_own[:, None]
        & live_all[None, :]
        & ((group_own[:, None] != caption_group[None, :]) | diagonal)
    )
    live_rows = live_own.astype(jnp.float32)
    diagonal_float = diagonal.astype(jnp.float32)
    forward_logits = right_inner(text_low, all_images) * LOGIT_SCALE
    backward_logits = right_inner(image_low, all_texts) * LOGIT_SCALE
    forward_probs, forward_lse = masked_softmax(forward_logits, allowed, live_rows)
    backward_probs, backward_lse = masked_softmax(backward_logits, allowed, live_rows)
    forward_terms = forward_lse - jnp.sum(forward_logits * diagonal_float, -1)
    backward_terms = backward_lse - jnp.sum(backward_logits * diagonal_float, -1)
    local_sum = 0.5 * (jnp.sum(live_rows * forward_terms) + jnp.sum(live_rows * backward_terms))
    loss_sum = lax.psum(local_sum, ("tower", "dp"))
    loss_value = loss_sum / jnp.sum(counts).astype(jnp.float32)
    forward_coef = (0.5 * live_rows[:, None] * (forward_probs - diagonal_float)).astype(
        jnp.bfloat16
    )
    grad_embedding = LOGIT_SCALE * multiply(forward_coef, all_images)
    lse_everyone = lax.all_gather(backward_lse, ("tower", "dp"), axis=0, tiled=True)
    shifted = jnp.where(allowed, forward_logits - lse_everyone[None, :], -1e30)
    live_columns = live_all.astype(jnp.float32)
    column_coef = (0.5 * live_columns[None, :] * (jnp.exp(shifted) - diagonal_float)).astype(
        jnp.bfloat16
    )
    grad_embedding = grad_embedding + LOGIT_SCALE * multiply(column_coef, all_images)
    text_grad, grads = backward(text_params, text_saved, grad_embedding, text_tokens.shape[1])
    shards = (
        lax.psum_scatter(grads[0], "dp", scatter_dimension=1, tiled=True),
        lax.psum_scatter(grads[1], "dp", scatter_dimension=1, tiled=True),
        lax.psum_scatter(grads[2], "dp", scatter_dimension=0, tiled=True),
        lax.psum_scatter(grads[3], "dp", scatter_dimension=0, tiled=True),
        lax.psum_scatter(grads[4], "dp", scatter_dimension=0, tiled=True),
        lax.psum_scatter(grads[5], "dp", scatter_dimension=0, tiled=True),
        lax.psum_scatter(grads[6], "dp", scatter_dimension=1, tiled=True),
        lax.psum_scatter(grads[7], "dp", scatter_dimension=0, tiled=True),
        lax.psum_scatter(grads[8], "dp", scatter_dimension=0, tiled=True),
        lax.psum_scatter(grads[9], "dp", scatter_dimension=0, tiled=True),
    )
    totals = (
        lax.psum(shards[0].astype(jnp.bfloat16), "tower").astype(jnp.float32),
        lax.psum(shards[1].astype(jnp.bfloat16), "tower").astype(jnp.float32),
        lax.psum(shards[2].astype(jnp.bfloat16), "tower").astype(jnp.float32),
        lax.psum(shards[3].astype(jnp.bfloat16), "tower").astype(jnp.float32),
        lax.psum(shards[4].astype(jnp.bfloat16), "tower").astype(jnp.float32),
        lax.psum(shards[5].astype(jnp.bfloat16), "tower").astype(jnp.float32),
        lax.psum(shards[6].astype(jnp.bfloat16), "tower").astype(jnp.float32),
        lax.psum(shards[7].astype(jnp.bfloat16), "tower").astype(jnp.float32),
        lax.psum(shards[8].astype(jnp.bfloat16), "tower").astype(jnp.float32),
        lax.psum(shards[9].astype(jnp.bfloat16), "tower").astype(jnp.float32),
    )
    return (
        loss_value,
        text_grad,
        totals[0],
        totals[1],
        totals[2],
        totals[3],
        totals[4],
        totals[5],
        totals[6],
        totals[7],
        totals[8],
        totals[9],
    )


def solution(mesh):
    n = mesh.shape["dp"]
    whole, both = P(), P(("tower", "dp"), None, None)
    fits = FF // n * 4 == D and n % 8 == 0
    body = functools.partial(on_device, n) if fits else plain_on_device
    out_specs = (P(), both, P(None, "dp"), P(None, "dp"), P("dp", None), P("dp"), P("dp", None), P("dp"), P(None, "dp"), P("dp"), P("dp", None), P("dp"))
    return jax.shard_map(body, mesh=mesh, in_specs=(both, both) + (whole,) * 22, out_specs=out_specs, check_vma=False)
```

```python
import functools
import jax
import jax.numpy as jnp
import numpy as np
from jax import lax
from jax.experimental import pallas as pl
from jax.experimental.pallas import tpu as pltpu
from jax.sharding import PartitionSpec as P

F32, BF16 = jnp.float32, jnp.bfloat16
D, HD, FF = 768, 64, 3072
PAIRS = D // (2 * HD)
KW = 128
NORM_EPS, EMBED_EPS, LOGIT_SCALE = 1e-5, 1e-6, 64.0
NEG = -1e30
ANY = pl.BlockSpec(memory_space=pl.ANY)
VM = pl.BlockSpec(memory_space=pltpu.VMEM)
GELU_C, GELU_A = float(np.sqrt(2 / np.pi)), 0.044715


def dot(a, b):
    return jnp.dot(a, b, preferred_element_type=F32)


def dot_t(a, b):
    return lax.dot_general(a, b, (((1,), (1,)), ((), ())), preferred_element_type=F32)


def t_dot(a, b):
    return lax.dot_general(a, b, (((0,), (0,)), ((), ())), preferred_element_type=F32)


def unit_rows(v):
    centre = v - jnp.mean(v, -1, keepdims=True)
    inv = lax.rsqrt(jnp.mean(centre * centre, -1, keepdims=True) + NORM_EPS)
    return centre * inv, inv


def head_masks():
    lane = lax.broadcasted_iota(jnp.int32, (1, 2 * HD), 1)
    even = (lane < HD).astype(F32)
    return even.astype(BF16), (1.0 - even).astype(BF16)


def pair_mask(rows, per, real):
    r = lax.broadcasted_iota(jnp.int32, (rows, 2 * KW), 0)
    c = lax.broadcasted_iota(jnp.int32, (rows, 2 * KW), 1) % KW
    ok = (r // per == c // per) & (c % per < real) & (c < rows)
    return jnp.where(ok, 0.0, NEG).astype(F32)


def split_heads(a, even, odd):
    return jnp.concatenate([a * even, a * odd], axis=0)


def softmax_half(s):
    m = jnp.max(s, -1, keepdims=True)
    p = jnp.exp(s - m)
    return p / jnp.sum(p, -1, keepdims=True)


def exp_half(s):
    return jnp.exp(s - jnp.max(s, -1, keepdims=True)).astype(BF16)


def block_forward(x, rows, groups, small, W, wait, done, proj, ctx, mask, att_out, keep):
    attend, output, expand, contract = W
    unit, _ = unit_rows(x)
    n1 = (unit * small[0:1, :] + small[2:3, :]).astype(BF16)
    keep("n1", n1)
    wait("attend")
    M = rows * groups
    step = 256
    for c in range(3 * D // step):
        y = dot(n1, attend[:, c * step:(c + 1) * step])
        if c * step < D:
            y = y + small[4:5, c * step:(c + 1) * step]
        elif c * step >= 2 * D:
            y = y + small[5:6, c * step - 2 * D:(c + 1) * step - 2 * D]
        proj[0:M, c * step:(c + 1) * step] = y.astype(BF16)
    done("attend")
    keep("proj", None)
    even, odd = head_masks()
    ones = split_heads(jnp.ones((KW, 2 * HD), BF16), even, odd)

    def group(g, _):
        r0 = pl.multiple_of(g * rows, 16)
        for j in range(PAIRS):
            lanes = slice(j * 2 * HD, (j + 1) * 2 * HD)
            q = proj[pl.ds(r0, rows), j * 128:(j + 1) * 128]
            kk = split_heads(proj[pl.ds(r0, KW), D + j * 128:D + (j + 1) * 128], even, odd)
            vv = split_heads(proj[pl.ds(r0, KW), 2 * D + j * 128:2 * D + (j + 1) * 128], even, odd)
            s = dot_t(q, kk) * HD ** -0.5 + mask[...]
            if att_out is None:
                p = jnp.concatenate([exp_half(s[:, :KW]), exp_half(s[:, KW:])], axis=1)
                both = dot(p, jnp.concatenate([vv, ones], axis=1))
                ctx[pl.ds(r0, rows), lanes] = (both[:, :128] / both[:, 128:]).astype(BF16)
            else:
                a = jnp.concatenate([softmax_half(s[:, :KW]), softmax_half(s[:, KW:])], axis=1)
                att_out[g * PAIRS + j] = a
                ctx[pl.ds(r0, rows), lanes] = dot(a.astype(BF16), vv).astype(BF16)
        return 0

    lax.fori_loop(0, groups, group, 0)
    wait("output")
    middle = x + (dot(ctx[0:M, :], output[...]) + small[6:7, :])
    done("output")
    keep("middle", middle)
    unit, _ = unit_rows(middle)
    n2 = (unit * small[1:2, :] + small[3:4, :]).astype(BF16)
    keep("n2", n2)
    wait("expand")
    acc = middle + small[11:12, :]
    step = 768
    for c in range(FF // step):
        pre = dot(n2, expand[:, c * step:(c + 1) * step]) + small[7 + c:8 + c, :]
        sq = pre * pre
        th = jnp.tanh(pre * (GELU_C + GELU_C * GELU_A * sq))
        cdf = 0.5 + 0.5 * th
        act = (pre * cdf).astype(BF16)
        keep("act", act, c, pre, sq, th, cdf)
        if c == 0:
            wait("contract")
        acc = acc + dot(act, contract[c * step:(c + 1) * step, :])
    done("expand")
    done("contract")
    return acc


def embed_rows(pooled):
    inv = lax.rsqrt(jnp.sum(pooled * pooled, -1, keepdims=True) + EMBED_EPS)
    return pooled * inv, inv


MESH_ID = pl.DeviceIdType.MESH


def place():
    return lax.axis_index("tower"), lax.axis_index("dp")


def greet(n):
    t, d = place()
    barrier = pltpu.get_barrier_semaphore()

    def one(k, _):
        who = (lax.rem(t + k // n, 2), lax.rem(d + lax.rem(k, n), n))
        pl.semaphore_signal(barrier, inc=1, device_id=who, device_id_type=MESH_ID)
        return 0

    lax.fori_loop(1, 2 * n, one, 0)


def spread(n, src, dst, send, recv):
    t, d = place()

    def one(k, _):
        pltpu.make_async_remote_copy(src_ref=src, dst_ref=dst.at[d], send_sem=send, recv_sem=recv,
                                     device_id=(t, lax.rem(d + k, n)), device_id_type=MESH_ID).start()
        return 0

    lax.fori_loop(1, n, one, 0)


def settle(n, dst, send, recv):
    part = dst.at[pl.ds(0, n - 1)]
    pltpu.make_async_copy(part, part, send).wait()
    pltpu.make_async_copy(part, part, recv).wait()


def contrast_rows(fl, allowed, live_rows):
    filled = jnp.where(allowed, fl, NEG)
    largest = jnp.max(filled, -1, keepdims=True)
    weights = jnp.where(allowed, jnp.exp(filled - largest), 0.0)
    total = jnp.sum(weights, -1, keepdims=True) + (1.0 - live_rows)
    return weights / total, largest + jnp.log(total)


def contrast_rows(fl, allowed, live_rows):
    filled = jnp.where(allowed, fl, NEG)
    largest = jnp.max(filled, -1, keepdims=True)
    weights = jnp.where(allowed, jnp.exp(filled - largest), 0.0)
    total = jnp.sum(weights, -1, keepdims=True) + (1.0 - live_rows)
    return weights / total, largest + jnp.log(total)


def fill_small(small, refs):
    gains, shifts, attend_bias, output_bias, expand_bias, contract_bias = refs
    small[0:2, :] = gains[...].astype(F32)
    small[2:4, :] = shifts[...].astype(F32)
    row = 4
    for ref in (attend_bias, output_bias, expand_bias, contract_bias):
        for k in range(ref.shape[0] // D):
            small[row:row + 1, :] = ref[pl.ds(k * D, D)].astype(F32).reshape(1, D)
            row += 1


def front_kernel(per_text, real, plan, n, *refs):
    it = iter(refs)
    take = lambda k: [next(it) for _ in range(k)]
    x_ref, counts_ref, group_ref = take(3)
    image_small, text_small = take(6), take(6)
    image_w, text_w = take(4), take(4)
    tokens_h, = take(1)
    g_ref, grow_ref, loss_ref, ag_ref = take(4)
    saved_h = take(7)
    weights = take(4)
    saved = take(7)
    tokens, by_place, xs, proj_i, ctx_i, mask_t, mask_i, small_t, small_i = take(9)
    lows_t, asum, emb_ref, own_rows, lse, = take(5)
    lows_i = take(len(plan))
    load, out_sem, tok_sem, ssem, rsem, osem_s, osem_r = take(7)
    t, d = place()
    greet(n)
    names = ("attend", "output", "expand", "contract")
    copies = {}
    for k, name in enumerate(names):
        copies["text", name] = pltpu.make_async_copy(text_w[k], weights[k], load.at[k])
        if k < 2:
            copies["text", name].start()
        copies["image", name] = pltpu.make_async_copy(image_w[k], weights[k], load.at[4 + k])
    token_copy = pltpu.make_async_copy(tokens_h, tokens, tok_sem)

    def text_wait(name):
        copies["text", name].wait()
        if name == "attend":
            copies["text", "expand"].start()
            copies["text", "contract"].start()
            token_copy.start()

    n1, proj, att, ctx, mid, n2, gp = saved
    outs = dict(zip(("n1", "proj", "att", "ctx", "mid", "n2", "gp"), [pltpu.make_async_copy(v, h, out_sem.at[k]) for k, (v, h) in enumerate(zip(saved, saved_h))]))
    fill_small(small_t, text_small)
    fill_small(small_i, image_small)
    M = x_ref.shape[0]
    ex = M // per_text
    mask_t[...] = pair_mask(KW, per_text, per_text)

    def keep(name, value, *extra):
        if name == "n1":
            n1[...] = value
            outs["n1"].start()
        elif name == "proj":
            outs["proj"].start()
        elif name == "middle":
            mid[...] = value
            for o in ("att", "ctx", "mid"):
                outs[o].start()
        elif name == "n2":
            n2[...] = value
            outs["n2"].start()
        else:
            c, pre, sq, th, cdf = extra
            w = value.shape[1]
            asum[c] = jnp.sum(value.astype(F32).reshape(ex, per_text, w), 1).astype(BF16)
            gp[:, c * w:(c + 1) * w] = (cdf + (0.5 * GELU_C) * pre * (1.0 - th * th) * (1.0 + (3 * GELU_A) * sq)).astype(BF16)

    out = block_forward(x_ref[...].astype(F32), KW, M // KW, small_t, weights, text_wait, lambda name: copies["image", name].start(),
                        proj, ctx, mask_t, att, keep)
    outs["gp"].start()
    emb, inv = embed_rows(jnp.sum(out.reshape(ex, per_text, D), 1) * (1.0 / per_text))
    emb_ref[0] = emb
    emb_ref[1] = jnp.broadcast_to(inv, emb.shape)
    lows_t[t, d] = emb.astype(BF16)

    def send(src, dst, s, r, who):
        return pltpu.make_async_remote_copy(src_ref=src, dst_ref=dst, send_sem=s, recv_sem=r, device_id=who, device_id_type=MESH_ID)

    pl.semaphore_wait(pltpu.get_barrier_semaphore(), 2 * n - 1)
    spread(n, lows_t.at[t, d], lows_t.at[t], ssem.at[0], rsem.at[0])
    nz, dz, xy = n // 4, d // 4, lax.rem(d, 4)
    for k in range(1, nz):
        to = lax.rem(dz + k, nz)
        send(asum.at[to], ag_ref.at[dz], ssem.at[1], rsem.at[1], (t, to * 4 + xy)).start()
    ag_ref[dz] = asum[dz]

    def pass_over(buf, k):
        return send(buf.at[t], buf.at[t], osem_s.at[k], osem_r.at[k], (1 - t, d))

    per = -(-real // 8) * 8
    rows = 2 * per
    xs[...] = jnp.zeros_like(xs)
    proj_i[proj_i.shape[0] - 16:, :] = jnp.zeros((16, 3 * D), BF16)
    mask_i[...] = pair_mask(rows, per, real)
    bufs = [lows_t] + lows_i
    slots = [0] + [2 + k for k in range(len(plan))]

    def arrive(k):
        settle(n, bufs[k].at[t], ssem.at[slots[k]], rsem.at[slots[k]])
        pass_over(bufs[k], k).start()

    for k, (first, pairs) in enumerate(plan):
        def wait(name):
            if k == 0:
                copies["image", name].wait()
        if k == 0:
            token_copy.wait()
        rows_k, ex_k = rows * pairs, 2 * pairs
        held = ex // 2
        if first % held == 0:
            for v in range(D // 128):
                by_place[v] = tokens[:, first:first + held, v * 128:(v + 1) * 128].astype(F32).reshape(real * held, 128)
        for e in range(ex_k):
            for lo in range(0, real, 8):
                count = min(8, real - lo)
                for v in range(D // 128):
                    xs[e * per + lo:e * per + lo + count, v * 128:(v + 1) * 128] = by_place[v, pl.ds(first % held + e + lo * held, count, stride=held), :]
        out = block_forward(xs[0:rows_k, :], rows, pairs, small_i, weights, wait, lambda name: None, proj_i, ctx_i, mask_i, None, lambda *a: None)
        out = out.reshape(ex_k, per, D)
        ok = lax.broadcasted_iota(jnp.int32, (ex_k, per, D), 1) < real
        emb, _ = embed_rows(jnp.sum(jnp.where(ok, out, 0.0), 1) * (1.0 / real))
        lows_i[k][t, d] = emb.astype(BF16)
        spread(n, lows_i[k].at[t, d], lows_i[k].at[t], ssem.at[slots[k + 1]], rsem.at[slots[k + 1]])
        arrive(k)
        if k > 0:
            pass_over(bufs[k - 1], k - 1).wait()

    every, nd = 2 * n * ex, 2 * n
    rank = t * n + d
    counts_row = jnp.broadcast_to(counts_ref[...].astype(F32).reshape(1, nd), (8, nd)).astype(BF16)

    def live_of(device, row):
        hot = (lax.broadcasted_iota(jnp.int32, (nd, device.shape[1]), 0) == device).astype(F32).astype(BF16)
        return (row.astype(F32) < dot(counts_row, hot)[0:1, :]).astype(F32), hot

    natural = lax.broadcasted_iota(jnp.int32, (1, every), 1)
    group_row = group_ref[...].astype(F32).reshape(1, every)
    live_row, _ = live_of(natural // ex, natural % ex)
    text_group = jnp.transpose(jnp.broadcast_to(group_row, (128, every)))[:, 0:1]
    text_live = jnp.transpose(jnp.broadcast_to(live_row, (128, every)))[:, 0:1]
    own_text = lows_t[t, d]
    groups, lives, places = [], [], []
    at = 0
    for k, (first, pairs) in enumerate(plan):
        ek = 2 * pairs
        w = nd * ek
        col = lax.broadcasted_iota(jnp.int32, (1, w), 1)
        device, row = col // ek, first + col % ek
        live, hot = live_of(device, row)
        pick = (lax.broadcasted_iota(jnp.int32, (every, w), 0) == device * ex + row).astype(F32).astype(BF16)
        groups.append(dot(jnp.broadcast_to(group_row, (8, every)).astype(BF16), pick)[0:1, :])
        lives.append(live)
        places.append(device * ex + row)
    texts = lows_t[...].reshape(every, D)

    def chunk_logits(k, at):
        w = nd * 2 * plan[k][1]
        images = lows_i[k][...].reshape(w, D)
        own_rows[:, at:at + w] = dot_t(own_text, images) * LOGIT_SCALE
        for lo in range(0, w, 256):
            part = slice(lo, min(lo + 256, w))
            logits = dot_t(texts, images[part]) * LOGIT_SCALE
            same = lax.broadcasted_iota(jnp.int32, logits.shape, 0) == places[k][:, part]
            allowed = (text_live * lives[k][:, part] > 0.0) & ((text_group != groups[k][:, part]) | same)
            filled = jnp.where(allowed, logits, NEG)
            largest = jnp.max(filled, 0, keepdims=True)
            total = jnp.sum(jnp.where(allowed, jnp.exp(filled - largest), 0.0), 0, keepdims=True) + (1.0 - lives[k][:, part])
            lse[:, at + lo:at + lo + logits.shape[1]] = jnp.broadcast_to(largest + jnp.log(total), (8, logits.shape[1]))
        return at + w

    for k in range(len(plan)):
        if k == len(plan) - 1:
            arrive(k + 1)
            pass_over(bufs[k + 1], k + 1).wait()
        elif k == len(plan) - 2:
            pass_over(bufs[k + 1], k + 1).wait()
        at = chunk_logits(k, at)
    column_group, column_live, column_place = (jnp.concatenate(v, 1) for v in (groups, lives, places))
    diag_b = column_place == lax.broadcasted_iota(jnp.int32, (ex, every), 0) + rank * ex
    diagonal = diag_b.astype(F32)
    image_lse = lse[0:1, :]
    fl = own_rows[...]
    live_own = jnp.sum(diagonal * column_live, -1, keepdims=True)
    group_own = jnp.sum(diagonal * column_group, -1, keepdims=True)
    allowed = (live_own * column_live > 0.0) & ((group_own != column_group) | diag_b)
    probs, text_lse = contrast_rows(fl, allowed, live_own)
    own_diag = fl * diagonal
    terms = live_own * (text_lse - jnp.sum(own_diag, -1, keepdims=True)) + jnp.sum(diagonal * (live_own * image_lse) - live_own * own_diag, -1, keepdims=True)
    loss_ref[...] = jnp.broadcast_to(0.5 * jnp.sum(terms, 0, keepdims=True), loss_ref.shape)
    forward_coef = (0.5 * live_own * (probs - diagonal)).astype(BF16)
    shifted = jnp.where(allowed, jnp.exp(jnp.where(allowed, fl - image_lse, NEG)), 0.0)
    column_coef = (0.5 * column_live * (shifted - diagonal)).astype(BF16)
    coefs = jnp.concatenate([forward_coef, column_coef], 0)
    at, grad = 0, None
    for k, (first, pairs) in enumerate(plan):
        w = nd * 2 * pairs
        part = dot(coefs[:, at:at + w], lows_i[k][...].reshape(w, D))
        grad = part if grad is None else grad + part
        at += w
    grad = LOGIT_SCALE * grad[0:ex] + LOGIT_SCALE * grad[ex:]
    emb = emb_ref[0]
    pooled = emb_ref[1] * (grad - emb * jnp.sum(grad * emb, -1, keepdims=True))
    rows_out = pooled * (1.0 / per_text)
    grow_ref[...] = rows_out
    g_ref[...] = rows_out.astype(BF16)
    settle(nz, ag_ref, ssem.at[1], rsem.at[1])
    for o in outs.values():
        o.wait()


def front(n, text_tokens, image_tokens, counts, group, image_params, text_params, plan):
    ex, per, _ = text_tokens.shape
    real = image_tokens.shape[1]
    M = ex * per
    nz = n // 4
    S = jax.ShapeDtypeStruct
    small_of = lambda p: [p[0], p[1], p[3], p[5], p[7], p[9]]
    weights_of = lambda p: [p[2], p[4], p[6], p[8]]
    kept = [S((M, D), BF16), S((M, 3 * D), BF16), S((M // KW * PAIRS, KW, 2 * KW), F32), S((M, D), BF16), S((M, D), F32), S((M, D), BF16), S((M, FF), BF16)]
    like = lambda a: pltpu.VMEM(a.shape, a.dtype)
    per_i = -(-real // 8) * 8
    big = max(p for _, p in plan) * 2 * per_i
    scratch = [like(a) for a in weights_of(text_params)] + [like(a) for a in kept]
    scratch += [pltpu.VMEM((real, ex, D), BF16), pltpu.VMEM((D // 128, real * ex // 2, 128), F32), pltpu.VMEM((big, D), F32), pltpu.VMEM((big + 16, 3 * D), BF16), pltpu.VMEM((big, D), BF16),
                pltpu.VMEM((KW, 2 * KW), F32), pltpu.VMEM((2 * per_i, 2 * KW), F32), pltpu.VMEM((16, D), F32), pltpu.VMEM((16, D), F32)]
    scratch += [pltpu.VMEM((2, n, ex, D), BF16), pltpu.VMEM((nz, ex, FF // nz), BF16), pltpu.VMEM((2, ex, D), F32), pltpu.VMEM((ex, 2 * n * ex), F32), pltpu.VMEM((8, 2 * n * ex), F32)]
    scratch += [pltpu.VMEM((2, n, 2 * p, D), BF16) for _, p in plan]
    dma = pltpu.SemaphoreType.DMA
    k = len(plan)
    scratch += [dma((8,)), dma((7,)), dma, dma((k + 2,)), dma((k + 2,)), dma((k + 1,)), dma((k + 1,))]
    return pl.pallas_call(
        functools.partial(front_kernel, per, real, plan, n),
        out_shape=[S((ex, D), BF16), S((ex, D), F32), S((8, 128), F32), S((nz, ex, FF // nz), BF16)] + kept,
        in_specs=[VM] * 15 + [ANY] * 9, out_specs=[VM] * 4 + [ANY] * 7, scratch_shapes=scratch,
        compiler_params=pltpu.CompilerParams(collective_id=0, has_side_effects=True, vmem_limit_bytes=63 << 20),
        name="forward_and_loss",
    )(text_tokens.reshape(M, D), counts, group, *small_of(image_params), *small_of(text_params), *weights_of(image_params), *weights_of(text_params), image_tokens.transpose(1, 0, 2))


def norm_back(grad, unit, inv, gain):
    gu = grad * gain
    out = inv * (gu - jnp.mean(gu, -1, keepdims=True) - unit * jnp.mean(gu * unit, -1, keepdims=True))
    return out, jnp.sum(grad * unit, 0, keepdims=True), jnp.sum(grad, 0, keepdims=True)


def back_kernel(per, n, small, g_ref, grow_ref, ag_ref, loss_ref, x_h, n1_h, proj_h, att_h, ctx_h, mid_h, n2_h, gp_h, contract_h, expand_h, output_h, attend_h,
                tg_ref, oe_ref, oa_ref, oo_ref, os_ref, oc_ref,
                xb, n1, proj, att, ctx, mid, n2, gp, contract, expand, output, attend, gctx, gproj, rowsums,
                grads, core_in, in1, in2, red, zin_e, zin_a, fin_e, fin_a, fin_c, s_out, s_in, s_fin, gall,
                load, csem_s, csem_r, sem1_s, sem1_r, sem2_s, sem2_r, zsem_s, zsem_r, fsem_s, fsem_r, gsem, ssem):
    t, d = place()
    dx, dy, dz, nz = lax.rem(d, 2), lax.rem(d // 2, 2), d // 4, n // 4
    xy = lax.rem(d, 4)
    other = (1 - t, d)
    partner = ((t, d + 1 - 2 * dx), (t, d + 2 - 4 * dy))
    greet(n)
    copies = {}
    for k, (name, h, v) in enumerate((("contract", contract_h, contract), ("gp", gp_h, gp), ("n2", n2_h, n2), ("expand", expand_h, expand), ("mid", mid_h, mid), ("ctx", ctx_h, ctx),
                                      ("output", output_h, output), ("proj", proj_h, proj), ("att", att_h, att), ("n1", n1_h, n1), ("attend", attend_h, attend), ("x", x_h, xb))):
        copies[name] = pltpu.make_async_copy(h, v, load.at[k])
        if k < 3:
            copies[name].start()
    M = xb.shape[0]
    ex = M // per
    rows_e, rows_a, H = FF // n, D // n, D // 2
    B = D // 2
    Q, E8 = B // 4, B // 2

    def remote(src, dst, ss, rs, who):
        return pltpu.make_async_remote_copy(src_ref=src, dst_ref=dst, send_sem=ss, recv_sem=rs, device_id=who, device_id_type=MESH_ID)

    def core_copy(q):
        return remote(grads.at[q, 1 - t], core_in.at[q], csem_s.at[q], csem_r.at[q], other)

    def first_copy(q, b):
        away = pl.multiple_of(b * B + (1 - (dx, dy)[b]) * E8, 16)
        return remote(grads.at[q, t, pl.ds(away, E8)], in1.at[q, b], sem1_s.at[q, b], sem1_r.at[q, b], partner[b])

    def second_copy(q, b):
        away = pl.multiple_of(b * B + (dx, dy)[b] * E8 + (1 - (dy, dx)[b]) * Q, 16)
        return remote(grads.at[q, t, pl.ds(away, Q)], in2.at[q, b], sem2_s.at[q, b], sem2_r.at[q, b], partner[1 - b])

    def step0(q):
        core_copy(q).start()

    def step1(q):
        core_copy(q).wait()
        grads[q, t] = (grads[q, t].astype(F32) + core_in[q].astype(F32)).astype(BF16)
        for b in range(2):
            first_copy(q, b).start()

    def step2(q):
        for b in range(2):
            first_copy(q, b).wait()
            keep = pl.multiple_of(b * B + (dx, dy)[b] * E8, 16)
            grads[q, t, pl.ds(keep, E8)] = (grads[q, t, pl.ds(keep, E8)].astype(F32) + in1[q, b].astype(F32)).astype(BF16)
            second_copy(q, b).start()

    def step3(q):
        for b in range(2):
            second_copy(q, b).wait()
            keep = pl.multiple_of(b * B + (dx, dy)[b] * E8 + (dy, dx)[b] * Q, 16)
            red[q, b * Q:(b + 1) * Q] = (grads[q, t, pl.ds(keep, Q)].astype(F32) + in2[q, b].astype(F32)).astype(BF16)

    def over_z(k):
        to = lax.rem(dz + k, nz)
        return to, (t, to * 4 + lax.rem(d, 4))

    def z_expand(c):
        @pl.when(dz != c)
        def _():
            remote(red.at[c], zin_e.at[dz], zsem_s.at[nz], zsem_r.at[nz], (t, c * 4 + xy)).start()

    def z_attend(a):
        for k in range(1, nz):
            to, who = over_z(k)
            remote(red.at[nz + a, pl.ds(pl.multiple_of(to * rows_a, 16), rows_a)], zin_a.at[a, dz], zsem_s.at[a], zsem_r.at[a], who).start()
        zin_a[a, dz] = red[nz + a, pl.ds(pl.multiple_of(dz * rows_a, 16), rows_a)]

    def all_but_one(ref, count, ss, rs):
        part = ref.at[pl.ds(0, count)]
        pltpu.make_async_copy(part, part, ss).wait()
        pltpu.make_async_copy(part, part, rs).wait()

    def fin_copy(k):
        ref = fin_a.at[k] if k < 4 else (fin_e, fin_c)[k - 4]
        return remote(ref.at[t], ref.at[t], fsem_s.at[k], fsem_r.at[k], other)

    def last_expand():
        all_but_one(zin_e, nz - 1, zsem_s.at[nz], zsem_r.at[nz])
        zin_e[dz] = red[dz]
        fin_e[t] = jnp.sum(zin_e[...].astype(F32), 0).astype(BF16)
        fin_copy(4).start()

    def last_attend(a):
        all_but_one(zin_a.at[a], nz - 1, zsem_s.at[a], zsem_r.at[a])
        fin_a[a, t] = jnp.sum(zin_a[a].astype(F32), 0).astype(BF16)
        fin_copy(a).start()

    def put_shards(q, value):
        for y in range(2):
            for x in range(2):
                at = (2 * y + x) * rows_e
                for h in range(2):
                    grads[q, h, (2 * x + y) * Q:(2 * x + y + 1) * Q, :] = value[at:at + Q, h * H:(h + 1) * H]
                    grads[q, h, B + (2 * y + x) * Q:B + (2 * y + x + 1) * Q, :] = value[at + Q:at + 2 * Q, h * H:(h + 1) * H]

    def put_rows(q, value, lanes):
        for s in range(n):
            z, y, x = s // 4, s // 2 % 2, s % 2
            p = (2 * x + y) * Q + z * rows_a if z < nz // 2 else B + (2 * y + x) * Q + (z - nz // 2) * rows_a
            for h in range(2):
                for src, dst, w in lanes(h):
                    grads[q, h, p:p + rows_a, dst:dst + w] = value[s * rows_a:(s + 1) * rows_a, src:src + w]

    g_low = g_ref[...]
    rowsums[13:14, :] = per * jnp.sum(g_low.astype(F32), 0, keepdims=True)
    step = FF // nz
    gn2 = None
    for c in range(nz):
        cols = slice(c * step, (c + 1) * step)
        if c == 0:
            copies["contract"].wait()
        ga = dot_t(g_low, contract[cols, :])
        if c == 0:
            pl.semaphore_wait(pltpu.get_barrier_semaphore(), 2 * n - 1)
            gall[dz] = g_ref[...]
            for k in range(1, nz):
                remote(g_ref, gall.at[dz], gsem.at[0], gsem.at[1], over_z(k)[1]).start()
            copies["gp"].wait()
            copies["n2"].wait()
            for name in ("expand", "mid", "ctx", "output"):
                copies[name].start()
        pre = (ga[:, None, :] * gp[:, cols].astype(F32).reshape(ex, per, step)).reshape(M, step).astype(BF16)
        rowsums[8 + c:9 + c, :] = jnp.sum(pre.astype(F32), 0, keepdims=True)
        ge = t_dot(pre, n2[...]).astype(BF16)
        put_shards(c, ge)
        step0(c)
        if c == 0:
            copies["expand"].wait()
        part = dot_t(pre, expand[:, cols])
        gn2 = part if gn2 is None else gn2 + part
        if c >= 1:
            step1(c - 1)
        if c >= 2:
            step2(c - 2)
        if c == 1:
            all_but_one(gall, nz - 1, gsem.at[0], gsem.at[1])
            put_shards(nz + 4, t_dot(ag_ref[...].reshape(nz * ex, FF // nz), gall[...].reshape(nz * ex, D)).astype(BF16))
            step0(nz + 4)
        elif c == 2:
            for name in ("proj", "att", "n1", "attend", "x"):
                copies[name].start()
            step1(nz + 4)
        elif c == 3:
            step2(nz + 4)
    copies["mid"].wait()
    unit, inv = unit_rows(mid[...])
    gm, gain_two, shift_two = norm_back(gn2, unit, inv, small[1:2, :].astype(F32))
    rowsums[1:2, :] = gain_two
    rowsums[3:4, :] = shift_two
    gm = (gm.reshape(ex, per, D) + grow_ref[...][:, None, :]).reshape(M, D)
    tg_ref[...] = gm
    gb = gm.astype(BF16)
    rowsums[12:13, :] = jnp.sum(gb.astype(F32), 0, keepdims=True)
    step1(nz - 1)
    copies["ctx"].wait()
    put_rows(nz, t_dot(ctx[...], gb).astype(BF16), lambda h: [(h * H, 0, H)])
    step0(nz)
    step2(nz - 2)
    step3(0)
    z_expand(0)
    copies["output"].wait()
    gctx[...] = dot_t(gb, output[...]).astype(BF16)
    step1(nz)
    step3(1)
    z_expand(1)
    step3(nz + 4)
    fin_c[t] = red[nz + 4]
    fin_copy(5).start()
    even, odd = head_masks()
    lane = lax.broadcasted_iota(jnp.int32, (KW, 2 * HD), 1)
    copies["proj"].wait()
    copies["att"].wait()

    for third in range(3):
        def group(i, _):
            r0 = pl.multiple_of(i * KW, KW)
            for j in (2 * third, 2 * third + 1):
                L = slice(j * 128, (j + 1) * 128)
                gc = gctx[pl.ds(r0, KW), L]
                q = proj[pl.ds(r0, KW), j * 128:(j + 1) * 128]
                kk = split_heads(proj[pl.ds(r0, KW), D + j * 128:D + (j + 1) * 128], even, odd)
                vv = split_heads(proj[pl.ds(r0, KW), 2 * D + j * 128:2 * D + (j + 1) * 128], even, odd)
                a = att[i * PAIRS + j]
                gatt = dot_t(gc, vv)
                prod = gatt * a
                gs = jnp.concatenate([a[:, h * KW:(h + 1) * KW] * (gatt[:, h * KW:(h + 1) * KW] - jnp.sum(prod[:, h * KW:(h + 1) * KW], -1, keepdims=True)) for h in range(2)], axis=1).astype(BF16)
                gv = t_dot(a.astype(BF16), gc)
                gk = t_dot(gs, q) * HD ** -0.5
                gproj[pl.ds(r0, KW), j * 128:(j + 1) * 128] = (dot(gs, kk) * HD ** -0.5).astype(BF16)
                gproj[pl.ds(r0, KW), D + j * 128:D + (j + 1) * 128] = jnp.where(lane < HD, gk[:KW], gk[KW:]).astype(BF16)
                gproj[pl.ds(r0, KW), 2 * D + j * 128:2 * D + (j + 1) * 128] = jnp.where(lane < HD, gv[:KW], gv[KW:]).astype(BF16)
            return 0

        lax.fori_loop(0, M // KW, group, 0)
        if third == 0:
            copies["n1"].wait()
        else:
            step1(nz + third)
        wide3 = jnp.concatenate([gproj[:, part * D + 256 * third:part * D + 256 * (third + 1)] for part in range(3)], axis=1)
        put_rows(nz + 1 + third, t_dot(n1[...], wide3).astype(BF16), lambda h: [(256 * part + 128 * h, 128 * part, 128) for part in range(3)])
        step0(nz + 1 + third)
        if third == 0:
            step2(nz - 1)
            for c in range(2, nz - 1):
                step3(c)
                z_expand(c)
        elif third == 1:
            step2(nz)
            step3(nz - 1)
            z_expand(nz - 1)
        else:
            step3(nz)
            z_attend(0)
            step2(nz + 1)
    rowsums[4:5, :] = jnp.sum(gproj[:, 0:D].astype(F32), 0, keepdims=True)
    rowsums[5:6, :] = rowsums[4:5, :]
    rowsums[6:7, :] = jnp.sum(gproj[:, 2 * D:3 * D].astype(F32), 0, keepdims=True)
    rowsums[7:8, :] = rowsums[6:7, :]
    step1(nz + 3)
    copies["attend"].wait()
    gn1 = dot_t(gproj[...], attend[...])
    step3(nz + 1)
    z_attend(1)
    step2(nz + 2)
    last_expand()
    copies["x"].wait()
    unit, inv = unit_rows(xb[...].astype(F32))
    gx, gain_one, shift_one = norm_back(gn1, unit, inv, small[0:1, :].astype(F32))
    tg_ref[...] += gx
    rowsums[0:1, :] = gain_one
    rowsums[2:3, :] = shift_one
    step2(nz + 3)
    step3(nz + 2)
    z_attend(2)
    sums = rowsums[...]
    parts = [sums[0:8, :]] + [jnp.broadcast_to(sums[8 + r:9 + r, :], (4, D)) for r in range(4)] + [sums[12:13, :], jnp.zeros((3, D), F32), sums[13:14, :], jnp.zeros((128 - 29, D), F32)]
    cols = jnp.transpose(jnp.concatenate(parts, 0))
    at = lax.broadcasted_iota(jnp.int32, (rows_a, 128), 1)
    loss = loss_ref[0:1, :]
    loss_high = loss.astype(BF16)
    loss_mid = (loss - loss_high.astype(F32)).astype(BF16)
    loss_low = (loss - loss_high.astype(F32) - loss_mid.astype(F32)).astype(BF16)
    for s in range(n):
        piece = jnp.where((at < 4) | (at == 24) | (at == 28), cols[s * rows_a:(s + 1) * rows_a, :], 0.0)
        r0, first = 2 * s * rows_a % D, 2 * s * rows_a // D * 2
        for c in range(2):
            piece = jnp.where(at == 4 + first + c, cols[r0 + c * rows_a:r0 + (c + 1) * rows_a, :], piece)
        r0, first = 4 * s * rows_a % D, 4 * s * rows_a // D * 4
        for c in range(4):
            piece = jnp.where(at == 8 + first + c, cols[r0 + c * rows_a:r0 + (c + 1) * rows_a, :], piece)
        for k, v in enumerate((loss_high, loss_mid, loss_low)):
            piece = jnp.where(at == 25 + k, v.astype(F32), piece)
        s_out[s] = piece.astype(BF16)

    def small_send(k, _):
        to = lax.rem(d + k, n)
        remote(s_out.at[to], s_in.at[d], ssem.at[0], ssem.at[1], (t, to)).start()
        return 0

    lax.fori_loop(1, n, small_send, 0)
    s_in[d] = s_out[d]

    last_attend(0)
    step3(nz + 3)
    z_attend(3)
    last_attend(1)
    all_but_one(s_in, n - 1, ssem.at[0], ssem.at[1])
    s_fin[t] = jnp.sum(s_in[...].astype(F32), 0)
    s_copy = remote(s_fin.at[t], s_fin.at[t], fsem_s.at[6], fsem_r.at[6], other)
    s_copy.start()
    last_attend(2)
    fin_copy(4).wait()
    fin_copy(5).wait()
    for h in range(2):
        oc_ref[:, h * H:(h + 1) * H] = fin_c[h].astype(F32)
        oe_ref[:, h * H:(h + 1) * H] = fin_e[h].astype(F32)
    s_copy.wait()
    os_ref[...] = s_fin[0] + s_fin[1]
    last_attend(3)
    fin_copy(0).wait()
    for h in range(2):
        oo_ref[:, h * H:(h + 1) * H] = fin_a[0, h].astype(F32)
    for third in range(3):
        fin_copy(1 + third).wait()
        for h in range(2):
            for part in range(3):
                lo = part * D + 256 * third + 128 * h
                oa_ref[:, lo:lo + 128] = fin_a[1 + third, h, :, 128 * part:128 * (part + 1)].astype(F32)


def text_backward(per, n, x, small, g, grow, ag, loss, saved, attend, output, expand, contract):
    n1, proj, att, ctx, mid, n2, gp = saved
    M = x.shape[0]
    ex, nz = g.shape[0], n // 4
    rows_e, rows_a, H = FF // n, D // n, D // 2
    S = jax.ShapeDtypeStruct
    V = lambda *shape: pltpu.VMEM(shape, BF16)
    like = lambda a: pltpu.VMEM(a.shape, a.dtype)
    outs = [S((M, D), F32), S((rows_e, D), F32), S((rows_a, 3 * D), F32), S((rows_a, D), F32), S((rows_a, 128), F32), S((rows_e, D), F32)]
    q = nz + 5
    dma = pltpu.SemaphoreType.DMA
    held = (x, n1, proj, att, ctx, mid, n2, gp, contract, expand, output, attend)
    scratch = [like(a) for a in held] + [V(M, D), V(M, 3 * D), pltpu.VMEM((16, D), F32)]
    scratch += [V(q, 2, D, H), V(q, D, H), V(q, 2, D // 4, H), V(q, 2, D // 8, H), V(q, D // 4, H), V(nz, D // 4, H), V(4, nz, rows_a, H), V(2, D // 4, H), V(4, 2, rows_a, H), V(2, D // 4, H),
                V(n, rows_a, 128), V(n, rows_a, 128), pltpu.VMEM((2, rows_a, 128), F32), V(nz, ex, D)]
    scratch += [dma((12,)), dma((q,)), dma((q,)), dma((q, 2)), dma((q, 2)), dma((q, 2)), dma((q, 2)), dma((nz + 4,)), dma((nz + 4,)), dma((7,)), dma((7,)), dma((2,)), dma((2,))]
    return pl.pallas_call(
        functools.partial(back_kernel, per, n), out_shape=outs, in_specs=[VM] * 5 + [ANY] * 12, out_specs=[VM] * 6, scratch_shapes=scratch,
        compiler_params=pltpu.CompilerParams(collective_id=1, has_side_effects=True, vmem_limit_bytes=63 << 20),
        name="text_backward",
    )(small, g, grow, ag, loss, x, n1, proj, att, ctx, mid, n2, gp, contract, expand, output, attend)


def finish_kernel(n, per, counts_ref, tg, oe, oa, oo, os, oc, loss_ref, tg_out, gains, shifts, attend, attend_bias, output, output_bias, expand_t, expand_bias, contract, contract_bias):
    rows_a = D // n
    loss_ref[...] = (os[0:1, 25:26] + os[0:1, 26:27] + os[0:1, 27:28]) / jnp.sum(counts_ref[...].astype(F32).reshape(1, -1), -1, keepdims=True)
    tg_out[...] = tg[...]
    attend[...] = oa[...]
    output[...] = oo[...]
    expand_t[...] = oe[...]
    contract[...] = oc[...]
    rows = jnp.transpose(jnp.concatenate([os[...], jnp.zeros((128 - rows_a, 128), F32)], 0))
    gains[...] = rows[0:2, 0:rows_a]
    shifts[...] = rows[2:4, 0:rows_a]

    def joined(pieces):
        total = None
        for c, piece in enumerate(pieces):
            line = jnp.concatenate([jnp.broadcast_to(piece, (8, 128)), jnp.zeros((8, 128), F32)], 1)
            line = pltpu.roll(line, c * rows_a, 1) if c else line
            total = line if total is None else total + line
        return total[0:1, 0:len(pieces) * rows_a].reshape(len(pieces) * rows_a)

    attend_bias[...] = joined([rows[4 + c:5 + c] + rows[6 + c:7 + c] for c in range(2)])
    expand_bias[...] = joined([rows[8 + c:9 + c] + rows[12 + c:13 + c] + rows[16 + c:17 + c] + rows[20 + c:21 + c] for c in range(4)])
    output_bias[...] = joined([rows[24:25]])
    contract_bias[...] = joined([rows[28:29]])


def finish(n, per, counts, *parts):
    tg, oe, oa, oo = parts[:4]
    S = jax.ShapeDtypeStruct
    rows_e, rows_a = FF // n, D // n
    f = lambda *shape: S(shape, F32)
    outs = [f(1, 1), f(*tg.shape), f(2, rows_a), f(2, rows_a), f(*oa.shape), f(2 * rows_a), f(*oo.shape), f(rows_a), f(*oe.shape), f(4 * rows_a), f(rows_e, D), f(rows_a)]
    return pl.pallas_call(functools.partial(finish_kernel, n, per), out_shape=outs, in_specs=[VM] * 7, out_specs=[VM] * 12,
                          compiler_params=pltpu.CompilerParams(vmem_limit_bytes=60 << 20), name="finish")(counts, *parts)


def on_device(n, text_tokens, image_tokens, counts, caption_group, *params):
    per_dev = text_tokens.shape[0]
    plan = ((0, per_dev // 4), (per_dev // 2, per_dev // 8), (per_dev * 3 // 4, per_dev // 8))
    image_params, text_params = params[:10], params[10:]
    ex, per, _ = text_tokens.shape
    g, grow, loss, ag, *saved = front(n, text_tokens, image_tokens, counts, caption_group, image_params, text_params, plan)
    parts = text_backward(per, n, text_tokens.reshape(ex * per, D), text_params[0], g, grow, ag, loss, saved, *(text_params[k] for k in (2, 4, 6, 8)))
    out = list(finish(n, per, counts, *parts))
    out[0] = out[0].reshape(())
    out[1] = out[1].reshape(ex, per, D)
    out[8] = out[8].T
    return tuple(out)


HEADS = 12
HEAD_DIM = 64


def multiply(left, right):
    return jnp.dot(left, right, preferred_element_type=jnp.float32)


def left_inner(left, right):
    return lax.dot_general(
        left, right, (((0,), (0,)), ((), ())), preferred_element_type=jnp.float32
    )


def right_inner(left, right):
    return lax.dot_general(
        left, right, (((1,), (1,)), ((), ())), preferred_element_type=jnp.float32
    )


def normalize(rows_in, gain, shift):
    centre = rows_in - jnp.mean(rows_in, -1, keepdims=True)
    inverse_std = lax.rsqrt(jnp.mean(centre * centre, -1, keepdims=True) + NORM_EPS)
    unit_rows = centre * inverse_std
    return (unit_rows * gain + shift, unit_rows, inverse_std)


def normalize_back(grad_rows, unit_rows, inverse_std, gain):
    grad_unit = grad_rows * gain
    grad_in = inverse_std * (
        grad_unit
        - jnp.mean(grad_unit, -1, keepdims=True)
        - unit_rows * jnp.mean(grad_unit * unit_rows, -1, keepdims=True)
    )
    return (grad_in, jnp.sum(grad_rows * unit_rows, 0), jnp.sum(grad_rows, 0))


def plain_forward(tokens, params):
    (
        gains,
        shifts,
        attend,
        attend_bias,
        output,
        output_bias,
        expand,
        expand_bias,
        contract,
        contract_bias,
    ) = params
    examples, row_count, features = tokens.shape
    inputs = tokens.astype(jnp.float32).reshape(examples * row_count, features)
    normed, unit_one, inverse_one = normalize(
        inputs, gains[0].astype(jnp.float32), shifts[0].astype(jnp.float32)
    )
    normed_one = normed.astype(jnp.bfloat16)
    full_bias = jnp.concatenate(
        [attend_bias[:features], jnp.zeros_like(output_bias), attend_bias[features:]]
    ).astype(jnp.float32)
    projected = (multiply(normed_one, attend) + full_bias).astype(jnp.bfloat16)
    projected = projected.reshape(examples, row_count, 3, HEADS, HEAD_DIM)
    queries = projected[:, :, 0]
    keys = projected[:, :, 1]
    values = projected[:, :, 2]
    scores = jnp.einsum(
        "erhd,eshd->ehrs", queries, keys, preferred_element_type=jnp.float32
    ) * HEAD_DIM ** (-0.5)
    attention = jax.nn.softmax(scores, axis=-1)
    attention_low = attention.astype(jnp.bfloat16)
    context = jnp.einsum(
        "ehrs,eshd->erhd", attention_low, values, preferred_element_type=jnp.float32
    )
    context = context.astype(jnp.bfloat16).reshape(examples * row_count, features)
    middle = inputs + (multiply(context, output) + output_bias.astype(jnp.float32))
    normed, unit_two, inverse_two = normalize(
        middle, gains[1].astype(jnp.float32), shifts[1].astype(jnp.float32)
    )
    normed_two = normed.astype(jnp.bfloat16)
    pre_gelu = multiply(normed_two, expand) + expand_bias.astype(jnp.float32)
    activated = jax.nn.gelu(pre_gelu).astype(jnp.bfloat16)
    block_out = middle + (multiply(activated, contract) + contract_bias.astype(jnp.float32))
    pooled = jnp.mean(block_out.reshape(examples, row_count, features), axis=1)
    inverse_norm = lax.rsqrt(jnp.sum(pooled * pooled, -1, keepdims=True) + EMBED_EPS)
    embedding = pooled * inverse_norm
    saved = (
        normed_one,
        unit_one,
        inverse_one,
        queries,
        keys,
        values,
        attention,
        attention_low,
        context,
        unit_two,
        inverse_two,
        normed_two,
        pre_gelu,
        activated,
        embedding,
        inverse_norm,
    )
    return (embedding, saved)


def backward(params, saved, grad_embedding, row_count):
    (
        gains,
        shifts,
        attend,
        attend_bias,
        output,
        output_bias,
        expand,
        expand_bias,
        contract,
        contract_bias,
    ) = params
    (
        normed_one,
        unit_one,
        inverse_one,
        queries,
        keys,
        values,
        attention,
        attention_low,
        context,
        unit_two,
        inverse_two,
        normed_two,
        pre_gelu,
        activated,
        embedding,
        inverse_norm,
    ) = saved
    examples, features = embedding.shape
    grad_pooled = inverse_norm * (
        grad_embedding - embedding * jnp.sum(grad_embedding * embedding, -1, keepdims=True)
    )
    grad_rows = jnp.broadcast_to(
        (grad_pooled / row_count)[:, None, :], (examples, row_count, features)
    ).reshape(examples * row_count, features)
    grad_mlp = grad_rows.astype(jnp.bfloat16)
    grad_contract = left_inner(activated, grad_mlp)
    grad_contract_bias = jnp.sum(grad_mlp.astype(jnp.float32), 0)
    grad_activated = right_inner(grad_mlp, contract)
    gelu_back = jax.vjp(jax.nn.gelu, pre_gelu)[1]
    grad_pre = gelu_back(grad_activated)[0].astype(jnp.bfloat16)
    grad_expand = left_inner(normed_two, grad_pre)
    grad_expand_bias = jnp.sum(grad_pre.astype(jnp.float32), 0)
    grad_normed_two = right_inner(grad_pre, expand)
    grad_middle, gain_two, shift_two = normalize_back(
        grad_normed_two, unit_two, inverse_two, gains[1].astype(jnp.float32)
    )
    grad_middle = grad_middle + grad_rows
    grad_branch = grad_middle.astype(jnp.bfloat16)
    grad_output = left_inner(context, grad_branch)
    grad_output_bias = jnp.sum(grad_branch.astype(jnp.float32), 0)
    grad_context = (
        right_inner(grad_branch, output)
        .astype(jnp.bfloat16)
        .reshape(examples, row_count, HEADS, HEAD_DIM)
    )
    grad_attention = jnp.einsum(
        "erhd,eshd->ehrs", grad_context, values, preferred_element_type=jnp.float32
    )
    grad_values = jnp.einsum(
        "ehrs,erhd->eshd", attention_low, grad_context, preferred_element_type=jnp.float32
    )
    grad_scores = (
        attention * (grad_attention - jnp.sum(grad_attention * attention, -1, keepdims=True))
    ).astype(jnp.bfloat16)
    grad_queries = jnp.einsum(
        "ehrs,eshd->erhd", grad_scores, keys, preferred_element_type=jnp.float32
    ) * HEAD_DIM ** (-0.5)
    grad_keys = jnp.einsum(
        "ehrs,erhd->eshd", grad_scores, queries, preferred_element_type=jnp.float32
    ) * HEAD_DIM ** (-0.5)
    grad_projected = (
        jnp.stack([grad_queries, grad_keys, grad_values], 2)
        .astype(jnp.bfloat16)
        .reshape(examples * row_count, 3 * features)
    )
    grad_attend = left_inner(normed_one, grad_projected)
    column_sums = jnp.sum(grad_projected.astype(jnp.float32), 0)
    grad_attend_bias = jnp.concatenate([column_sums[:features], column_sums[2 * features :]])
    grad_normed_one = right_inner(grad_projected, attend)
    grad_inputs, gain_one, shift_one = normalize_back(
        grad_normed_one, unit_one, inverse_one, gains[0].astype(jnp.float32)
    )
    grad_inputs = grad_inputs + grad_middle
    grads = (
        jnp.stack([gain_one, gain_two]),
        jnp.stack([shift_one, shift_two]),
        grad_attend,
        grad_attend_bias,
        grad_output,
        grad_output_bias,
        grad_expand,
        grad_expand_bias,
        grad_contract,
        grad_contract_bias,
    )
    return (grad_inputs.reshape(examples, row_count, features), grads)


def masked_softmax(logits, allowed, live_rows):
    filled = jnp.where(allowed, logits, -1e30)
    largest = jnp.max(filled, -1, keepdims=True)
    weights = jnp.exp(filled - largest) * allowed.astype(jnp.float32)
    safe_total = jnp.sum(weights, -1, keepdims=True) + (1.0 - live_rows)[:, None]
    return (weights / safe_total, largest[:, 0] + jnp.log(safe_total[:, 0]))


def plain_on_device(
    text_tokens,
    image_tokens,
    counts,
    caption_group,
    image_gains,
    image_shifts,
    image_attend,
    image_attend_bias,
    image_output,
    image_output_bias,
    image_expand,
    image_expand_bias,
    image_contract,
    image_contract_bias,
    text_gains,
    text_shifts,
    text_attend,
    text_attend_bias,
    text_output,
    text_output_bias,
    text_expand,
    text_expand_bias,
    text_contract,
    text_contract_bias,
):
    image_params = (
        image_gains,
        image_shifts,
        image_attend,
        image_attend_bias,
        image_output,
        image_output_bias,
        image_expand,
        image_expand_bias,
        image_contract,
        image_contract_bias,
    )
    text_params = (
        text_gains,
        text_shifts,
        text_attend,
        text_attend_bias,
        text_output,
        text_output_bias,
        text_expand,
        text_expand_bias,
        text_contract,
        text_contract_bias,
    )
    image_embedding, image_saved = plain_forward(image_tokens, image_params)
    text_embedding, text_saved = plain_forward(text_tokens, text_params)
    image_low = image_embedding.astype(jnp.bfloat16)
    text_low = text_embedding.astype(jnp.bfloat16)
    all_images, all_texts = (
        lax.all_gather(image_low, ("tower", "dp"), axis=0, tiled=True),
        lax.all_gather(text_low, ("tower", "dp"), axis=0, tiled=True),
    )
    per_device = image_low.shape[0]
    everyone = all_images.shape[0]
    device_rank = lax.axis_index(("tower", "dp"))
    positions = jnp.arange(everyone, dtype=jnp.int32)
    owned = device_rank * per_device + jnp.arange(per_device, dtype=jnp.int32)
    live_all = positions % per_device < jnp.repeat(counts, per_device, total_repeat_length=everyone)
    live_own = lax.dynamic_slice_in_dim(live_all, device_rank * per_device, per_device)
    group_own = lax.dynamic_slice_in_dim(caption_group, device_rank * per_device, per_device)
    diagonal = owned[:, None] == positions[None, :]
    allowed = (
        live_own[:, None]
        & live_all[None, :]
        & ((group_own[:, None] != caption_group[None, :]) | diagonal)
    )
    live_rows = live_own.astype(jnp.float32)
    diagonal_float = diagonal.astype(jnp.float32)
    forward_logits = right_inner(text_low, all_images) * LOGIT_SCALE
    backward_logits = right_inner(image_low, all_texts) * LOGIT_SCALE
    forward_probs, forward_lse = masked_softmax(forward_logits, allowed, live_rows)
    backward_probs, backward_lse = masked_softmax(backward_logits, allowed, live_rows)
    forward_terms = forward_lse - jnp.sum(forward_logits * diagonal_float, -1)
    backward_terms = backward_lse - jnp.sum(backward_logits * diagonal_float, -1)
    local_sum = 0.5 * (jnp.sum(live_rows * forward_terms) + jnp.sum(live_rows * backward_terms))
    loss_sum = lax.psum(local_sum, ("tower", "dp"))
    loss_value = loss_sum / jnp.sum(counts).astype(jnp.float32)
    forward_coef = (0.5 * live_rows[:, None] * (forward_probs - diagonal_float)).astype(
        jnp.bfloat16
    )
    grad_embedding = LOGIT_SCALE * multiply(forward_coef, all_images)
    lse_everyone = lax.all_gather(backward_lse, ("tower", "dp"), axis=0, tiled=True)
    shifted = jnp.where(allowed, forward_logits - lse_everyone[None, :], -1e30)
    live_columns = live_all.astype(jnp.float32)
    column_coef = (0.5 * live_columns[None, :] * (jnp.exp(shifted) - diagonal_float)).astype(
        jnp.bfloat16
    )
    grad_embedding = grad_embedding + LOGIT_SCALE * multiply(column_coef, all_images)
    text_grad, grads = backward(text_params, text_saved, grad_embedding, text_tokens.shape[1])
    shards = (
        lax.psum_scatter(grads[0], "dp", scatter_dimension=1, tiled=True),
        lax.psum_scatter(grads[1], "dp", scatter_dimension=1, tiled=True),
        lax.psum_scatter(grads[2], "dp", scatter_dimension=0, tiled=True),
        lax.psum_scatter(grads[3], "dp", scatter_dimension=0, tiled=True),
        lax.psum_scatter(grads[4], "dp", scatter_dimension=0, tiled=True),
        lax.psum_scatter(grads[5], "dp", scatter_dimension=0, tiled=True),
        lax.psum_scatter(grads[6], "dp", scatter_dimension=1, tiled=True),
        lax.psum_scatter(grads[7], "dp", scatter_dimension=0, tiled=True),
        lax.psum_scatter(grads[8], "dp", scatter_dimension=0, tiled=True),
        lax.psum_scatter(grads[9], "dp", scatter_dimension=0, tiled=True),
    )
    totals = (
        lax.psum(shards[0].astype(jnp.bfloat16), "tower").astype(jnp.float32),
        lax.psum(shards[1].astype(jnp.bfloat16), "tower").astype(jnp.float32),
        lax.psum(shards[2].astype(jnp.bfloat16), "tower").astype(jnp.float32),
        lax.psum(shards[3].astype(jnp.bfloat16), "tower").astype(jnp.float32),
        lax.psum(shards[4].astype(jnp.bfloat16), "tower").astype(jnp.float32),
        lax.psum(shards[5].astype(jnp.bfloat16), "tower").astype(jnp.float32),
        lax.psum(shards[6].astype(jnp.bfloat16), "tower").astype(jnp.float32),
        lax.psum(shards[7].astype(jnp.bfloat16), "tower").astype(jnp.float32),
        lax.psum(shards[8].astype(jnp.bfloat16), "tower").astype(jnp.float32),
        lax.psum(shards[9].astype(jnp.bfloat16), "tower").astype(jnp.float32),
    )
    return (
        loss_value,
        text_grad,
        totals[0],
        totals[1],
        totals[2],
        totals[3],
        totals[4],
        totals[5],
        totals[6],
        totals[7],
        totals[8],
        totals[9],
    )


def solution(mesh):
    n = mesh.shape["dp"]
    whole, both = P(), P(("tower", "dp"), None, None)
    fits = FF // n * 4 == D and n % 8 == 0
    body = functools.partial(on_device, n) if fits else plain_on_device
    out_specs = (P(), both, P(None, "dp"), P(None, "dp"), P("dp", None), P("dp"), P("dp", None), P("dp"), P(None, "dp"), P("dp"), P("dp", None), P("dp"))
    return jax.shard_map(body, mesh=mesh, in_specs=(both, both) + (whole,) * 22, out_specs=out_specs, check_vma=False)
```
